32 devices in a mesh: grp: 4 (over x, core), blk: 8 (over z, y).
Axes of the slice: x: 2, y: 2, z: 4, core: 2. Of those that a mesh axis runs over, the one named last changes fastest.
Arguments:
- stamps: float32 [32, 32, 64, 128], P(('grp', 'blk')), may hold values from -1 to 1
- stamp_target: int32 [32, 32, 128], P(('grp', 'blk')), may hold values from 0 to 4095
- pair_counts: int32 [32, 32], P(('grp', 'blk')), may hold values from 0 to 128, as said below
- conductance: float32 [8, 8192], P(None, ('grp', 'blk')), may hold values from 4 to 12
- block_cols: int32 [16, 8192], P(None, ('grp', 'blk')), may hold values from 0 to 8191, as said below
- newton_residual: float32 [8, 8192], P(None, ('grp', 'blk')), may hold values from -30 to 30
Outputs:
- update: float32 [8, 8192], P(None, ('grp', 'blk'))
- jacobian_blocks: float32 [16, 8, 8, 8192], P(None, None, None, ('grp', 'blk'))
- preconditioned_rhs: float32 [8, 8192], P(None, ('grp', 'blk'))
The draws below stay inside these ranges and needn't reach their ends.
Inputs may be any that keep to these rules, and one draw needn't show every extreme that they name: `stamp_target`: A stamp's target is its block slot times 256 plus its block row local to the owner. `pair_counts`: every device sends exactly 128 live blocks to itself and exactly 128 to the next device in the order of grp+blk (the last device to the first), and at most 32 to every other owner; one owner drawn from the seed receives exactly 32 from every device other than itself and the device before it. `block_cols`: slot 0 of block row n names n itself; slots 1 to 7 name rows of the same group of 2048 rows as n; over the 256 block rows of one device, the slots from 8 on name rows owned by each device exactly 64 times.
All inputs are finite; a program needn't handle non-finite values.
Results may differ from the reference program's by a relative error of at most 0.0003.
Values sent between devices are 32-bit elements; how exact they have to be, the bound alone decides.
No kernel may reach another device: no remote copies, remote signals or barrier semaphores. Data moves between devices by JAX's collectives and lax.ppermute only.
A program may use at most 128 MiB of HBM per device.

```python
import math
import jax
import jax.numpy as jnp
from jax import lax

NBR = 256
CAP = 128
K = 16
KRYLOV = 5
SWEEPS = 2
LOW = 32
NB = 8192
GROUP_ROWS = 2048
DEVICES = 32


def draw_pair_counts(key, part):
    key_hot, key_cold, key_warm, key_full = jax.random.split(jax.random.fold_in(key, 11), 4)
    hot = jax.random.randint(key_hot, (1, DEVICES), 0, 4) == 0
    cold_counts = jax.random.randint(key_cold, (DEVICES, DEVICES), LOW // 4, LOW // 2 + 1)
    warm_counts = jax.random.randint(key_warm, (DEVICES, DEVICES), LOW // 2, LOW + 1)
    counts = jnp.where(hot, warm_counts, cold_counts)
    full_owner = jax.random.randint(key_full, (), 0, DEVICES)
    col_ids = jnp.arange(DEVICES)[None, :]
    row_ids = jnp.arange(DEVICES)[:, None]
    counts = jnp.where(col_ids == full_owner, LOW, counts)
    paired = (row_ids == col_ids) | (col_ids == (row_ids + 1) % DEVICES)
    counts = jnp.where(paired, CAP, counts)
    return counts.astype(jnp.int32)


def shuffle_one(one_key):
    return jax.random.permutation(one_key, (K - K // 2) * NBR)


def draw_block_cols(key, part):
    key_near, key_owner, key_row = jax.random.split(jax.random.fold_in(key, 23), 3)
    row_ids = jnp.arange(NB, dtype=jnp.int32)
    group_start = row_ids // GROUP_ROWS * GROUP_ROWS
    near_cols = group_start[None, :] + jax.random.randint(key_near, (K // 2 - 1, NB), 0, GROUP_ROWS)
    far_slots = K - K // 2
    owner_keys = jax.random.split(key_owner, DEVICES)
    shuffled = jax.vmap(shuffle_one)(owner_keys)
    far_owner = shuffled % DEVICES
    far_local = jax.random.randint(key_row, (DEVICES, far_slots * NBR), 0, NBR)
    far_cols = (far_owner * NBR + far_local).reshape(DEVICES, far_slots, NBR)
    far_cols = far_cols.transpose(1, 0, 2).reshape(far_slots, NB)
    return jnp.concatenate([row_ids[None, :], near_cols, far_cols.astype(jnp.int32)], axis=0).astype(jnp.int32)


def touch_ends(values, own_key, least, largest):
    shape = values.shape
    place = [jax.random.randint(jax.random.fold_in(own_key, axis), (), 0, shape[axis]) for axis in range(len(shape))]
    values = values.at[tuple(place)].set(least)
    longest = shape.index(max(shape))
    place[longest] = (place[longest] + 1) % shape[longest]
    return values.at[tuple(place)].set(largest)


def block_scale(key, extent, pieces, smallest, largest):
    level = 1.0
    for axis_at, blocks in pieces:
        draws = jax.random.uniform(jax.random.fold_in(jax.random.fold_in(key, 6), axis_at), (blocks,), jnp.float32, smallest / len(pieces), largest / len(pieces))
        level = level * jnp.repeat(jnp.exp(draws), extent[axis_at] // blocks).reshape((-1,) + (1,) * (len(extent) - 1 - axis_at))
    return level


def bell_draw(stream_key, shape, deviation, reach, cuts=(), held_as=jnp.bfloat16):
    level = block_scale(stream_key, shape, cuts, -0.22, 0.18) if cuts else 1.0
    array = jax.random.normal(stream_key, shape, jnp.float32) * deviation * level
    return jnp.minimum(jnp.maximum(array, -reach), reach).astype(held_as)


def setup_inputs(seed: int = 0) -> dict:
    streams_of = jax.random.split(jax.random.key(seed), 7)
    stamps = jnp.clip(jax.random.uniform(streams_of[0], (DEVICES, DEVICES, 64, CAP), jnp.float32, -1.0, 1.0) * block_scale(streams_of[0], (DEVICES, DEVICES, 64, CAP), ((0, 32),), -0.4, 0.0), -1.0, 1.0)
    stamp_target = touch_ends(jax.random.randint(streams_of[1], (DEVICES, DEVICES, CAP), 0, K * NBR), jax.random.fold_in(streams_of[1], 1), 0, (K * NBR) - 1).astype(jnp.int32)
    pair_counts = draw_pair_counts(jax.random.fold_in(streams_of[6], 71), 0)
    conductance = jnp.clip(jnp.exp(math.log(12.0) - 1.0986123 * jax.random.uniform(streams_of[3], (8, NB), jnp.float32) ** block_scale(streams_of[3], (8, NB), ((1, 32),), -0.2, 0.2)), 4.0, 12.0)
    block_cols = draw_block_cols(jax.random.fold_in(streams_of[6], 71), 0)
    newton_residual = bell_draw(streams_of[5], (8, NB), 5.0, 30.0, ((1, 32),), jnp.float32)
    return {"stamps": stamps, "stamp_target": stamp_target, "pair_counts": pair_counts, "conductance": conductance, "block_cols": block_cols, "newton_residual": newton_residual}


EPS = 1e-06

def invert_blocks(diag):
    size = diag.shape[0]
    eye_mat = jnp.eye(size, dtype=jnp.float32)[:, :, None]
    inverse = eye_mat * jnp.ones_like(diag[:1])
    work = diag
    for pivot_row in range(size):
        scale = 1.0 / work[pivot_row, pivot_row]
        top_work = work[pivot_row] * scale
        top_inverse = inverse[pivot_row] * scale
        factor = work[:, pivot_row]
        work = work - factor[:, None, :] * top_work[None]
        inverse = inverse - factor[:, None, :] * top_inverse[None]
        work = work.at[pivot_row].set(top_work)
        inverse = inverse.at[pivot_row].set(top_inverse)
    return inverse

def solve_small(matrix, rhs_vector):
    count = matrix.shape[0]
    work, vector = (matrix, rhs_vector)
    for pivot_row in range(count):
        scale = 1.0 / work[pivot_row, pivot_row]
        top_work = work[pivot_row] * scale
        top_rhs = vector[pivot_row] * scale
        factor = work[:, pivot_row]
        work = work - factor[:, None] * top_work[None, :]
        vector = vector - factor * top_rhs
        work = work.at[pivot_row].set(top_work)
        vector = vector.at[pivot_row].set(top_rhs)
    return vector

def block_apply(inverse, vector):
    return jnp.einsum('abn,bn->an', inverse, vector, precision=lax.Precision.HIGHEST)

def couple(jacobian, picked):
    return jnp.einsum('kabn,bkn->an', jacobian, picked, precision=lax.Precision.HIGHEST)

def reference(stamps, stamp_target, pair_counts, conductance, block_cols, newton_residual):
    slot_ids = jnp.arange(CAP, dtype=jnp.int32)
    owners = jnp.arange(DEVICES, dtype=jnp.int32)

    def add_source(summed, source):
        values, targets, counts = source
        live = slot_ids[None, :] < counts[:, None]
        values = jnp.where(live[:, None, :], values, 0.0)
        where_to = targets // NBR * NB + owners[:, None] * NBR + targets % NBR
        flat = values.transpose(1, 0, 2).reshape(64, DEVICES * CAP)
        return (summed.at[:, where_to.reshape(-1)].add(flat), None)
    summed, _ = lax.scan(add_source, jnp.zeros((64, K * NB), jnp.float32), (stamps, stamp_target, pair_counts))
    jacobian = summed.reshape(8, 8, K, NB).transpose(2, 0, 1, 3)
    identity = jnp.eye(8, dtype=jnp.float32)
    jacobian = jacobian.at[0].add(identity[:, :, None] * conductance[:, None, :])
    inverse = invert_blocks(jacobian[0])
    row_ids = jnp.arange(NB, dtype=jnp.int32)
    near = (block_cols // GROUP_ROWS == (row_ids // GROUP_ROWS)[None, :]) & (jnp.arange(K, dtype=jnp.int32)[:, None] >= 1)

    def precondition(vector):
        result = block_apply(inverse, vector)
        for sweep_index in range(SWEEPS):
            picked = jnp.where(near[None], result[:, block_cols], 0.0)
            result = block_apply(inverse, vector - couple(jacobian, picked))
        return result

    def operate(vector):
        return couple(jacobian, vector[:, block_cols])
    rhs_field = -newton_residual
    beta = jnp.sqrt(jnp.sum(rhs_field * rhs_field) + EPS)
    basis = [rhs_field / beta]
    search = []
    hess = jnp.zeros((KRYLOV + 1, KRYLOV), jnp.float32)
    for krylov_step in range(KRYLOV):
        direction = precondition(basis[krylov_step])
        search.append(direction)
        image = operate(direction)
        projections = jnp.stack([jnp.sum(basis_vec * image) for basis_vec in basis])
        for index_i, basis_vec in enumerate(basis):
            image = image - projections[index_i] * basis_vec
        length = jnp.sqrt(jnp.sum(image * image) + EPS)
        hess = hess.at[:krylov_step + 1, krylov_step].set(projections)
        hess = hess.at[krylov_step + 1, krylov_step].set(length)
        if krylov_step + 1 < KRYLOV:
            basis.append(image / length)
    normal = jnp.dot(hess.T, hess, precision=lax.Precision.HIGHEST)
    coef = solve_small(normal, beta * hess[0])
    update = coef[0] * search[0]
    for index_j in range(1, KRYLOV):
        update = update + coef[index_j] * search[index_j]
    return (update, jacobian, beta * search[0])
```

```python
import functools

import jax
import jax.numpy as jnp
from jax import lax
from jax.experimental import pallas as pl
from jax.experimental.pallas import tpu as pltpu
from jax.sharding import PartitionSpec as P

K = 16
KRYLOV = 5
LOW = 32
EPS = 1e-06
LANES = 128
AXES = ("grp", "blk")

F32 = jnp.float32
BF16 = jnp.bfloat16
I32 = jnp.int32

LANE_GATHER = lax.GatherDimensionNumbers(
    offset_dims=(),
    collapsed_slice_dims=(1,),
    start_index_map=(1,),
    operand_batching_dims=(0,),
    start_indices_batching_dims=(0,),
)


def lane_gather(source, lanes):
    return lax.gather(
        source,
        lanes[..., None],
        LANE_GATHER,
        slice_sizes=(1, 1),
        mode=lax.GatherScatterMode.PROMISE_IN_BOUNDS,
    )


def call(kernel, out_shape, *args, scratch=(), vmem=32 * 2**20):
    return pl.pallas_call(
        kernel,
        out_shape=out_shape,
        in_specs=[pl.BlockSpec(memory_space=pltpu.VMEM)] * len(args),
        out_specs=jax.tree.map(lambda _: pl.BlockSpec(memory_space=pltpu.VMEM), out_shape),
        scratch_shapes=list(scratch),
        compiler_params=pltpu.CompilerParams(vmem_limit_bytes=vmem),
    )(*args)


def iota(shape, axis):
    return lax.broadcasted_iota(I32, shape, axis)


def halves_of(rows):
    return rows // LANES


def half(index):
    return slice(index * LANES, (index + 1) * LANES)


def stack_rows(rows):
    sub = iota((8, LANES), 0)
    out = jnp.zeros((8, LANES), F32)
    for a, value in enumerate(rows):
        out = jnp.where(sub == a, jnp.sum(value, axis=0, keepdims=True), out)
    return out


def apply_inverse(inv_ref, vector):
    out = []
    for h, value in enumerate(vector):
        out.append(stack_rows([inv_ref[a, :, half(h)] * value for a in range(8)]))
    return out


def couple(jac_ref, index_ref, sources, first, last, acc, base=0):
    count = len(acc)

    def step(k, acc):
        out = []
        for h in range(count):
            index = index_ref[k - base, :, half(h)]
            at, lanes = index >> 7, index & (LANES - 1)
            picked = jnp.zeros((8, LANES), F32)
            for s, source in enumerate(sources):
                picked = jnp.where(at == s, lane_gather(source(), lanes), picked)
            out.append([acc[h][a] + jac_ref[k, a, :, half(h)] * picked for a in range(8)])
        return out

    return lax.fori_loop(first, last, step, acc)


def zero_acc(count):
    return [[jnp.zeros((8, LANES), F32) for _ in range(8)] for _ in range(count)]


def group_sources(ref):
    members, _, rows = ref.shape
    return [
        (lambda d=d, h=h: ref[d, :, half(h)]) for d in range(members) for h in range(halves_of(rows))
    ]


def spread(ref, vector):
    for d in range(ref.shape[0]):
        for h, value in enumerate(vector):
            ref[d, :, half(h)] = value


def load(ref):
    return [ref[:, half(h)] for h in range(halves_of(ref.shape[1]))]


def dots_block(pairs):
    sub, lane = iota((8, LANES), 0), iota((8, LANES), 1)
    blocks = []
    for start in (0, 8):
        rows = jnp.zeros((8, LANES), F32)
        for i, (left, right) in enumerate(pairs[start : start + 8]):
            total = sum(x * y for x, y in zip(left, right))
            rows = jnp.where(sub == i, jnp.sum(total, axis=0, keepdims=True), rows)
        blocks.append(jnp.sum(rows, axis=1, keepdims=True))
    return jnp.where(lane < 96, blocks[0], blocks[1])


def read_dots(total, count):
    lane = iota((8, LANES), 1)
    out = []
    for at in (64, 96):
        column = jnp.sum(jnp.where(lane == at, total, 0.0), axis=1, keepdims=True)
        column = jnp.broadcast_to(column, (8, LANES))
        out += [jnp.broadcast_to(column[i : i + 1, :], (8, LANES)) for i in range(8)]
    return out[:count]


def pack_kernel(
    place_ref, stamps_ref, target_ref, counts_ref, cols_ref, send_ref, next_ref, own_ref, near_ref, pos_ref
):
    devices = stamps_ref.shape[0]
    local_rows = cols_ref.shape[1]
    far_slots = K - K // 2
    per_owner = far_slots * local_rows // devices
    me, nxt = place_ref[0], place_ref[1]
    group_start, group_rows = place_ref[2], place_ref[3]
    lane = iota((1, LANES), 1)

    live = iota((devices, LANES), 1) < counts_ref[...]
    target = jnp.where(live, target_ref[...], -1).astype(F32)
    for ref, at in ((next_ref, nxt), (own_ref, me)):
        ref[0:64, :] = stamps_ref[at]
        mine = iota((devices, LANES), 0) == at
        row = jnp.sum(jnp.where(mine, target, 0.0), axis=0, keepdims=True)
        ref[64:72, :] = jnp.broadcast_to(row, (8, LANES))
    ids = iota((devices, LANES), 0)
    low = jnp.where((ids == me) | (ids == nxt) | (iota((devices, LANES), 1) >= LOW), -1.0, target)

    owners = iota((devices, LANES), 0)
    before = (iota((LANES, LANES), 0) < iota((LANES, LANES), 1)).astype(BF16)
    running = jnp.zeros((devices, 1), F32)
    asked = jnp.zeros((devices, LANES), F32)
    tiled = iota((LANES, LANES), 0) & (per_owner - 1)
    for k in range(far_slots):
        for h in range(halves_of(local_rows)):
            cols = cols_ref[K // 2 + k : K // 2 + k + 1, half(h)]
            owner = cols // local_rows
            row = cols - owner * local_rows
            hot = (owners == owner).astype(F32)
            ahead = jnp.dot(hot.astype(BF16), before, preferred_element_type=F32) + running
            running = running + jnp.sum(hot, axis=1, keepdims=True)
            rank = jnp.sum(hot * ahead, axis=0, keepdims=True).astype(I32)
            asked += lax.dot_general(
                (hot * row.astype(F32)).astype(BF16),
                (tiled == rank).astype(F32).astype(BF16),
                (((1,), (1,)), ((), ())),
                preferred_element_type=F32,
            )
            pos_ref[k, :, half(h)] = jnp.broadcast_to(owner * per_owner + rank, (8, LANES))

    for d in range(devices):
        packed = jnp.zeros((16, LANES), F32)
        for g in range(4):
            piece = stamps_ref[d, 16 * g : 16 * g + 16, :]
            if g:
                piece = pltpu.roll(piece, LOW * g, 1)
            packed = jnp.where(lane // LOW == g, piece, packed)
        send_ref[d, 0:16, :] = packed
        sub = iota((8, LANES), 0)
        send_ref[d, 16:24, :] = jnp.where(sub == 0, low[d : d + 1, :], asked[d : d + 1, :])

    for k in range(K):
        for h in range(halves_of(local_rows)):
            cols = cols_ref[k : k + 1, half(h)] - group_start
            near = (cols >= 0) & (cols < group_rows)
            near_ref[k, :, half(h)] = jnp.broadcast_to(jnp.where(near, cols, -1), (8, LANES))


def assemble_kernel(
    recv_ref, prev_ref, own_ref, cond_ref, resid_ref, jac_ref, inv_ref, served_ref, z_ref, dots_ref, left_ref, right_ref
):
    devices = recv_ref.shape[0]
    local_rows = cond_ref.shape[1]
    lane = iota((1, LANES), 1)
    blocks = devices // 4 + 2

    def block(q):
        if q == 0:
            return own_ref[0:64, :], own_ref[64:65, :]
        if q == 1:
            return prev_ref[0:64, :], prev_ref[64:65, :]
        first = 4 * (q - 2)
        rows = []
        for g in range(4):
            out = jnp.zeros((16, LANES), F32)
            for j in range(4):
                piece = recv_ref[first + j, 0:16, :]
                if j != g:
                    piece = pltpu.roll(piece, (LOW * (j - g)) % LANES, 1)
                out = jnp.where(lane // LOW == j, piece, out)
            rows.append(out)
        target = jnp.full((1, LANES), -1.0, F32)
        for j in range(4):
            piece = recv_ref[first + j, 16:17, :]
            if j:
                piece = pltpu.roll(piece, LOW * j, 1)
            target = jnp.where(lane // LOW == j, piece, target)
        return jnp.concatenate(rows, axis=0), target

    most = 10
    for start in range(0, blocks, most):
        stop = min(start + most, blocks)
        width = 2 * (stop - start) * LANES
        values = []
        for q in range(start, stop):
            at = 2 * (q - start) * LANES
            stamp, target = block(q)
            target = target.astype(I32)
            slot, row = target >> (local_rows.bit_length() - 1), target & (local_rows - 1)
            hot = (iota((local_rows, LANES), 0) == row).astype(F32).astype(BF16)
            right_ref[:, at : at + LANES] = hot
            right_ref[:, at + LANES : at + 2 * LANES] = hot
            high = stamp.astype(BF16)
            low = (stamp - high.astype(F32)).astype(BF16)
            values.append((at, slot, high, low))

        for k in range(K):
            for at, slot, high, low in values:
                mask = (slot == k).astype(F32).astype(BF16)
                left_ref[64 * k : 64 * k + 64, at : at + LANES] = high * mask
                left_ref[64 * k : 64 * k + 64, at + LANES : at + 2 * LANES] = low * mask
        total = lax.dot_general(
            left_ref[:, 0:width],
            right_ref[:, 0:width],
            (((1,), (1,)), ((), ())),
            preferred_element_type=F32,
        ).reshape(K, 8, 8, local_rows)
        if start == 0:
            jac_ref[...] = total
        else:
            jac_ref[...] += total
    sub = iota((8, local_rows), 0)
    for a in range(8):
        jac_ref[0, a] = jac_ref[0, a] + jnp.where(sub == a, cond_ref[a : a + 1, :], 0.0)

    work = [jac_ref[0, a] for a in range(8)]
    inverse = [jnp.where(sub == a, 1.0, 0.0).astype(F32) for a in range(8)]
    for p in range(8):
        scale = 1.0 / work[p][p : p + 1, :]
        top_work, top_inverse = work[p] * scale, inverse[p] * scale
        for a in range(8):
            if a != p:
                factor = work[a][p : p + 1, :]
                work[a] = work[a] - factor * top_work
                inverse[a] = inverse[a] - factor * top_inverse
        work[p], inverse[p] = top_work, top_inverse
    for a in range(8):
        inv_ref[a] = inverse[a]

    for d in range(devices):
        served_ref[d] = jnp.broadcast_to(recv_ref[d, 17:18, :].astype(I32), (8, LANES))
    rhs = [-value for value in load(resid_ref)]
    spread(z_ref, apply_inverse(inv_ref, rhs))
    dots_ref[...] = dots_block([(rhs, rhs)])


def first_sweep_kernel(rhs, group_ref, vector_ref, jac_ref, inv_ref, near_ref, z_ref):
    vector = load(vector_ref)
    if rhs:
        vector = [-value for value in vector]
    acc = couple(jac_ref, near_ref, group_sources(group_ref), 1, K, zero_acc(len(vector)))
    spread(z_ref, apply_inverse(inv_ref, [v - stack_rows(c) for v, c in zip(vector, acc)]))


def second_sweep_kernel(
    rhs, group_ref, vector_ref, jac_ref, inv_ref, near_ref, served_ref, dots_ref, z_ref, far_ref, own_ref, coupled_ref
):
    vector = load(vector_ref)
    if rhs:
        vector = [-value for value in vector]
    acc = couple(jac_ref, near_ref, group_sources(group_ref), 1, K, zero_acc(len(vector)))
    coupled = [stack_rows(c) for c in acc]
    result = apply_inverse(inv_ref, [v - c for v, c in zip(vector, coupled)])
    spread(z_ref, result)
    for h, value in enumerate(result):
        own_ref[:, half(h)] = value
        coupled_ref[:, half(h)] = coupled[h]
    dots = dots_ref[...]
    lane = iota((8, LANES), 1)
    for d in range(far_ref.shape[0]):
        index = served_ref[d]
        lanes = index & (LANES - 1)
        picked = lane_gather(result[0], lanes)
        for h in range(1, len(result)):
            picked = jnp.where(index >> 7 == h, lane_gather(result[h], lanes), picked)
        far_ref[d] = jnp.where(lane < 64, picked, dots)


def combine(terms):
    return functools.reduce(lambda x, y: x + y, terms)


def orthogonalize(dots, step, gram):
    count = step + 1
    for i in range(count):
        gram[(i, step)] = gram[(step, i)] = dots[i]
    along = dots[count : 2 * count]
    hess = [gram[(i, step)] + along[i] for i in range(count)]
    coefs = [(1.0 - h if i == step else -h) for i, h in enumerate(hess)]
    square = dots[2 * count]
    for i in range(count):
        inner = combine([coefs[l] * gram[(i, l)] for l in range(count)])
        square = square + coefs[i] * (2.0 * along[i] + inner)
    length = jnp.sqrt(jnp.maximum(square, 0.0) + EPS)
    return hess, length, coefs


def read_scalars(refs):
    gram, hess, lengths = {}, {}, []
    beta = refs[0][0]
    for step, ref in enumerate(refs[1:]):
        count = step + 1
        for i in range(count):
            gram[(i, step)] = gram[(step, i)] = ref[i]
            hess[(i, step)] = ref[count + i]
        hess[(count, step)] = ref[2 * count]
    return beta, gram, hess


def operate_kernel(step, group_ref, far_ref, own_ref, coupled_ref, vector_ref, jac_ref, inv_ref, near_ref, pos_ref, *refs):
    states, scalar_refs = refs[:step], refs[step : 2 * step]
    state_ref, scalars_ref, vector_out_ref, z_ref, dots_ref = refs[2 * step :]
    devices = far_ref.shape[0]
    rows = own_ref.shape[1]
    count = halves_of(rows)
    per_owner = (K - K // 2) * rows // devices
    each = LANES // per_owner
    lane = iota((8, LANES), 1)

    arrived = []
    total = jnp.zeros((8, LANES), F32)
    for q in range(devices // each):
        out = far_ref[q * each]
        total = total + out
        for j in range(1, each):
            piece = far_ref[q * each + j]
            total = total + piece
            out = jnp.where(lane // per_owner == j, pltpu.roll(piece, j * per_owner, 1), out)
        arrived.append(out)

    acc = couple(jac_ref, near_ref, group_sources(group_ref), 1, K // 2, zero_acc(count))
    acc = couple(jac_ref, pos_ref, [(lambda v=v: v) for v in arrived], K // 2, K, acc, K // 2)
    image = [stack_rows(c) - n for c, n in zip(acc, load(coupled_ref))]
    search = load(own_ref)
    vector = load(vector_ref)

    if step == 0:
        vector = [-value for value in vector]
        length = jnp.sqrt(read_dots(total, 1)[0] + EPS)
        scalars_ref[0] = length
        coefs = []
    else:
        _, gram, _ = read_scalars(scalar_refs)
        dots = read_dots(total, 2 * step + 1)
        hess, length, coefs = orthogonalize(dots, step - 1, gram)
        for i in range(step):
            scalars_ref[i] = gram[(i, step - 1)]
            scalars_ref[step + i] = hess[i]
        scalars_ref[2 * step] = length
    scale = 1.0 / length

    def recombine(part, fresh):
        out = []
        for h, value in enumerate(fresh):
            for c, ref in zip(coefs, states):
                value = value + c * ref[part, :, half(h)]
            value = value * scale
            state_ref[part, :, half(h)] = value
            out.append(value)
        return out

    basis = [[ref[0, :, half(h)] for h in range(count)] for ref in states]
    basis.append(recombine(0, vector))
    recombine(1, search)
    image = recombine(2, image)
    for h, value in enumerate(image):
        vector_out_ref[:, half(h)] = value
    spread(z_ref, apply_inverse(inv_ref, image))
    pairs = [(b, basis[-1]) for b in basis] + [(b, image) for b in basis] + [(image, image)]
    block = dots_block(pairs)
    if step + 1 < KRYLOV:
        dots_ref[...] = block
    else:
        for d in range(devices):
            dots_ref[d] = block


def finish_kernel(dots_ref, *refs):
    states, scalar_refs = refs[:KRYLOV], refs[KRYLOV : 2 * KRYLOV]
    update_ref, first_ref = refs[2 * KRYLOV :]
    total = combine([dots_ref[d] for d in range(dots_ref.shape[0])])
    beta, gram, hess = read_scalars(scalar_refs)
    last, length, _ = orthogonalize(read_dots(total, 2 * KRYLOV + 1), KRYLOV - 1, gram)
    for i, value in enumerate(last):
        hess[(i, KRYLOV - 1)] = value
    hess[(KRYLOV, KRYLOV - 1)] = length

    work = [
        [combine([hess[(l, i)] * hess[(l, j)] for l in range(min(i, j) + 2)]) for j in range(KRYLOV)]
        for i in range(KRYLOV)
    ]
    vector = [beta * hess[(0, j)] for j in range(KRYLOV)]
    for p in range(KRYLOV):
        scale = 1.0 / work[p][p]
        top_work = [value * scale for value in work[p]]
        top = vector[p] * scale
        for i in range(KRYLOV):
            if i != p:
                factor = work[i][p]
                work[i] = [w - factor * t for w, t in zip(work[i], top_work)]
                vector[i] = vector[i] - factor * top
        work[p], vector[p] = top_work, top
    for h in range(halves_of(update_ref.shape[1])):
        update_ref[:, half(h)] = combine([c * ref[1, :, half(h)] for c, ref in zip(vector, states)])
        first_ref[:, half(h)] = beta * states[0][1, :, half(h)]


def shape(*dims, dtype=F32):
    return jax.ShapeDtypeStruct(dims, dtype)


def exchange(array, axes):
    return lax.all_to_all(array, axes, split_axis=0, concat_axis=0, tiled=True)


def local(stamps, stamp_target, pair_counts, conductance, block_cols, newton_residual):
    members = lax.axis_size("blk")
    devices = lax.axis_size("grp") * members
    rows = conductance.shape[1]
    me = lax.axis_index("grp") * members + lax.axis_index("blk")
    group_rows = rows * members
    place = jnp.stack([me, lax.rem(me + 1, devices), lax.axis_index("grp") * group_rows, group_rows]).astype(I32)

    send, to_next, own, near, pos = pl.pallas_call(
        pack_kernel,
        out_shape=(
            shape(devices, 24, LANES),
            shape(72, LANES),
            shape(72, LANES),
            shape(K, 8, rows, dtype=I32),
            shape(K - K // 2, 8, rows, dtype=I32),
        ),
        in_specs=[pl.BlockSpec(memory_space=pltpu.SMEM)] + [pl.BlockSpec(memory_space=pltpu.VMEM)] * 4,
        out_specs=tuple(pl.BlockSpec(memory_space=pltpu.VMEM) for _ in range(5)),
        compiler_params=pltpu.CompilerParams(vmem_limit_bytes=32 * 2**20),
    )(place, stamps[0], stamp_target[0], pair_counts.reshape(devices, 1), block_cols)
    got = exchange(send, AXES)
    prev = lax.ppermute(to_next, AXES, [(i, (i + 1) % devices) for i in range(devices)])

    width = 2 * LANES * min(devices // 4 + 2, 10)
    jacobian, inverse, served, z, dots = call(
        assemble_kernel,
        (
            shape(K, 8, 8, rows),
            shape(8, 8, rows),
            shape(devices, 8, LANES, dtype=I32),
            shape(members, 8, rows),
            shape(8, LANES),
        ),
        got,
        prev,
        own,
        conductance,
        newton_residual,
        scratch=(pltpu.VMEM((64 * K, width), BF16), pltpu.VMEM((rows, width), BF16)),
    )

    states, scalars = [], []
    vector = newton_residual
    for step in range(KRYLOV):
        rhs = step == 0
        z = call(
            functools.partial(first_sweep_kernel, rhs),
            shape(members, 8, rows),
            exchange(z, "blk"),
            vector,
            jacobian,
            inverse,
            near,
        )
        z, far, result, coupled = call(
            functools.partial(second_sweep_kernel, rhs),
            (shape(members, 8, rows), shape(devices, 8, LANES), shape(8, rows), shape(8, rows)),
            exchange(z, "blk"),
            vector,
            jacobian,
            inverse,
            near,
            served,
            dots,
        )
        last = step + 1 == KRYLOV
        state, scalar, vector, z, dots = call(
            functools.partial(operate_kernel, step),
            (
                shape(3, 8, rows),
                shape(2 * step + 1, 8, LANES),
                shape(8, rows),
                shape(members, 8, rows),
                shape(devices, 8, LANES) if last else shape(8, LANES),
            ),
            exchange(z, "blk"),
            exchange(far, AXES),
            result,
            coupled,
            vector,
            jacobian,
            inverse,
            near,
            pos,
            *states,
            *scalars,
        )
        states.append(state)
        scalars.append(scalar)

    update, first = call(
        finish_kernel, (shape(8, rows), shape(8, rows)), exchange(dots, AXES), *states, *scalars
    )
    return update, jacobian, first


def solution(mesh):
    placed = (
        P(AXES, None, None, None),
        P(AXES, None, None),
        P(AXES, None),
        P(None, AXES),
        P(None, AXES),
        P(None, AXES),
    )
    return jax.shard_map(
        local,
        mesh=mesh,
        in_specs=placed,
        out_specs=(P(None, AXES), P(None, None, None, AXES), P(None, AXES)),
        check_vma=False,
    )
```

```python
import functools

import jax
import jax.numpy as jnp
from jax import lax
from jax.experimental import pallas as pl
from jax.experimental.pallas import tpu as pltpu
from jax.sharding import PartitionSpec as P

K = 16
KRYLOV = 5
LOW = 32
EPS = 1e-06
LANES = 128
AXES = ("grp", "blk")

F32 = jnp.float32
BF16 = jnp.bfloat16
I32 = jnp.int32

LANE_GATHER = lax.GatherDimensionNumbers(
    offset_dims=(),
    collapsed_slice_dims=(1,),
    start_index_map=(1,),
    operand_batching_dims=(0,),
    start_indices_batching_dims=(0,),
)


def lane_gather(source, lanes):
    return lax.gather(
        source,
        lanes[..., None],
        LANE_GATHER,
        slice_sizes=(1, 1),
        mode=lax.GatherScatterMode.PROMISE_IN_BOUNDS,
    )


def call(kernel, out_shape, *args, scratch=(), vmem=32 * 2**20):
    return pl.pallas_call(
        kernel,
        out_shape=out_shape,
        in_specs=[pl.BlockSpec(memory_space=pltpu.VMEM)] * len(args),
        out_specs=jax.tree.map(lambda _: pl.BlockSpec(memory_space=pltpu.VMEM), out_shape),
        scratch_shapes=list(scratch),
        compiler_params=pltpu.CompilerParams(vmem_limit_bytes=vmem),
    )(*args)


def iota(shape, axis):
    return lax.broadcasted_iota(I32, shape, axis)


def halves_of(rows):
    return rows // LANES


def half(index):
    return slice(index * LANES, (index + 1) * LANES)


def stack_rows(rows):
    sub = iota((8, LANES), 0)
    out = jnp.zeros((8, LANES), F32)
    for a, value in enumerate(rows):
        out = jnp.where(sub == a, jnp.sum(value, axis=0, keepdims=True), out)
    return out


def apply_inverse(inv_ref, vector):
    out = []
    for h, value in enumerate(vector):
        out.append(stack_rows([inv_ref[a, :, half(h)] * value for a in range(8)]))
    return out


def couple(jac_ref, index_ref, sources, first, last, acc, base=0):
    count = len(acc)

    def step(k, acc):
        out = []
        for h in range(count):
            index = index_ref[k - base, :, half(h)]
            at, lanes = index >> 7, index & (LANES - 1)
            picked = jnp.zeros((8, LANES), F32)
            for s, source in enumerate(sources):
                picked = jnp.where(at == s, lane_gather(source(), lanes), picked)
            out.append([acc[h][a] + jac_ref[k, a, :, half(h)] * picked for a in range(8)])
        return out

    return lax.fori_loop(first, last, step, acc)


def zero_acc(count):
    return [[jnp.zeros((8, LANES), F32) for _ in range(8)] for _ in range(count)]


def group_sources(refs):
    return [
        (lambda ref=ref, h=h: ref[:, half(h)]) for ref in refs for h in range(halves_of(refs[0].shape[1]))
    ]


def store(ref, vector):
    for h, value in enumerate(vector):
        ref[:, half(h)] = value


def load(ref):
    return [ref[:, half(h)] for h in range(halves_of(ref.shape[1]))]


def dots_block(pairs):
    sub, lane = iota((8, LANES), 0), iota((8, LANES), 1)
    blocks = []
    for start in (0, 8):
        rows = jnp.zeros((8, LANES), F32)
        for i, (left, right) in enumerate(pairs[start : start + 8]):
            total = sum(x * y for x, y in zip(left, right))
            rows = jnp.where(sub == i, jnp.sum(total, axis=0, keepdims=True), rows)
        blocks.append(jnp.sum(rows, axis=1, keepdims=True))
    return jnp.where(lane < 96, blocks[0], blocks[1])


def read_dots(total, count):
    lane = iota((8, LANES), 1)
    out = []
    for at in (64, 96):
        column = jnp.sum(jnp.where(lane == at, total, 0.0), axis=1, keepdims=True)
        column = jnp.broadcast_to(column, (8, LANES))
        out += [jnp.broadcast_to(column[i : i + 1, :], (8, LANES)) for i in range(8)]
    return out[:count]


def pack_kernel(
    place_ref, stamps_ref, target_ref, counts_ref, cols_ref, send_ref, next_ref, own_ref, near_ref, pos_ref
):
    devices = stamps_ref.shape[0]
    local_rows = cols_ref.shape[1]
    far_slots = K - K // 2
    per_owner = far_slots * local_rows // devices
    me, nxt = place_ref[0], place_ref[1]
    group_start, group_rows = place_ref[2], place_ref[3]
    lane = iota((1, LANES), 1)

    live = iota((devices, LANES), 1) < counts_ref[...]
    target = jnp.where(live, target_ref[...], -1).astype(F32)
    for ref, at in ((next_ref, nxt), (own_ref, me)):
        ref[0:64, :] = stamps_ref[at]
        mine = iota((devices, LANES), 0) == at
        row = jnp.sum(jnp.where(mine, target, 0.0), axis=0, keepdims=True)
        ref[64:72, :] = jnp.broadcast_to(row, (8, LANES))
    ids = iota((devices, LANES), 0)
    low = jnp.where((ids == me) | (ids == nxt) | (iota((devices, LANES), 1) >= LOW), -1.0, target)

    owners = iota((devices, LANES), 0)
    before = (iota((LANES, LANES), 0) < iota((LANES, LANES), 1)).astype(BF16)
    running = jnp.zeros((devices, 1), F32)
    asked = jnp.zeros((devices, LANES), F32)
    tiled = iota((LANES, LANES), 0) & (per_owner - 1)
    for k in range(far_slots):
        for h in range(halves_of(local_rows)):
            cols = cols_ref[K // 2 + k : K // 2 + k + 1, half(h)]
            owner = cols // local_rows
            row = cols - owner * local_rows
            hot = (owners == owner).astype(F32)
            ahead = jnp.dot(hot.astype(BF16), before, preferred_element_type=F32) + running
            running = running + jnp.sum(hot, axis=1, keepdims=True)
            rank = jnp.sum(hot * ahead, axis=0, keepdims=True).astype(I32)
            asked += lax.dot_general(
                (hot * row.astype(F32)).astype(BF16),
                (tiled == rank).astype(F32).astype(BF16),
                (((1,), (1,)), ((), ())),
                preferred_element_type=F32,
            )
            pos_ref[k, :, half(h)] = jnp.broadcast_to(owner * per_owner + rank, (8, LANES))

    for d in range(devices):
        packed = jnp.zeros((16, LANES), F32)
        for g in range(4):
            piece = stamps_ref[d, 16 * g : 16 * g + 16, :]
            if g:
                piece = pltpu.roll(piece, LOW * g, 1)
            packed = jnp.where(lane // LOW == g, piece, packed)
        send_ref[d, 0:16, :] = packed
        sub = iota((8, LANES), 0)
        send_ref[d, 16:24, :] = jnp.where(sub == 0, low[d : d + 1, :], asked[d : d + 1, :])

    for k in range(K):
        for h in range(halves_of(local_rows)):
            cols = cols_ref[k : k + 1, half(h)]
            near = (cols >= group_start) & (cols < group_start + group_rows)
            owner = cols // local_rows
            behind = me - owner
            behind = jnp.where(behind < 0, behind + group_rows // local_rows, behind)
            index = behind * local_rows + (cols - owner * local_rows)
            near_ref[k, :, half(h)] = jnp.broadcast_to(jnp.where(near, index, -1), (8, LANES))


def assemble_kernel(
    recv_ref, prev_ref, own_ref, cond_ref, resid_ref, jac_ref, inv_ref, served_ref, z_ref, dots_ref, left_ref, right_ref
):
    devices = recv_ref.shape[0]
    local_rows = cond_ref.shape[1]
    lane = iota((1, LANES), 1)
    blocks = devices // 4 + 2

    def block(q):
        if q == 0:
            return own_ref[0:64, :], own_ref[64:65, :]
        if q == 1:
            return prev_ref[0:64, :], prev_ref[64:65, :]
        first = 4 * (q - 2)
        rows = []
        for g in range(4):
            out = jnp.zeros((16, LANES), F32)
            for j in range(4):
                piece = recv_ref[first + j, 0:16, :]
                if j != g:
                    piece = pltpu.roll(piece, (LOW * (j - g)) % LANES, 1)
                out = jnp.where(lane // LOW == j, piece, out)
            rows.append(out)
        target = jnp.full((1, LANES), -1.0, F32)
        for j in range(4):
            piece = recv_ref[first + j, 16:17, :]
            if j:
                piece = pltpu.roll(piece, LOW * j, 1)
            target = jnp.where(lane // LOW == j, piece, target)
        return jnp.concatenate(rows, axis=0), target

    most = 10
    for start in range(0, blocks, most):
        stop = min(start + most, blocks)
        width = 2 * (stop - start) * LANES
        values = []
        for q in range(start, stop):
            at = 2 * (q - start) * LANES
            stamp, target = block(q)
            target = target.astype(I32)
            slot, row = target >> (local_rows.bit_length() - 1), target & (local_rows - 1)
            hot = (iota((local_rows, LANES), 0) == row).astype(F32).astype(BF16)
            right_ref[:, at : at + LANES] = hot
            right_ref[:, at + LANES : at + 2 * LANES] = hot
            high = stamp.astype(BF16)
            low = (stamp - high.astype(F32)).astype(BF16)
            values.append((at, slot, high, low))

        for k in range(K):
            for at, slot, high, low in values:
                mask = (slot == k).astype(F32).astype(BF16)
                left_ref[64 * k : 64 * k + 64, at : at + LANES] = high * mask
                left_ref[64 * k : 64 * k + 64, at + LANES : at + 2 * LANES] = low * mask
        total = lax.dot_general(
            left_ref[:, 0:width],
            right_ref[:, 0:width],
            (((1,), (1,)), ((), ())),
            preferred_element_type=F32,
        ).reshape(K, 8, 8, local_rows)
        if start == 0:
            jac_ref[...] = total
        else:
            jac_ref[...] += total
    sub = iota((8, local_rows), 0)
    for a in range(8):
        jac_ref[0, a] = jac_ref[0, a] + jnp.where(sub == a, cond_ref[a : a + 1, :], 0.0)

    work = [jac_ref[0, a] for a in range(8)]
    inverse = [jnp.where(sub == a, 1.0, 0.0).astype(F32) for a in range(8)]
    for p in range(8):
        scale = 1.0 / work[p][p : p + 1, :]
        top_work, top_inverse = work[p] * scale, inverse[p] * scale
        for a in range(8):
            if a != p:
                factor = work[a][p : p + 1, :]
                work[a] = work[a] - factor * top_work
                inverse[a] = inverse[a] - factor * top_inverse
        work[p], inverse[p] = top_work, top_inverse
    for a in range(8):
        inv_ref[a] = inverse[a]

    for d in range(devices):
        served_ref[d] = jnp.broadcast_to(recv_ref[d, 17:18, :].astype(I32), (8, LANES))
    rhs = [-value for value in load(resid_ref)]
    store(z_ref, apply_inverse(inv_ref, rhs))
    dots_ref[...] = dots_block([(rhs, rhs)])


def first_sweep_kernel(rhs, members, *refs):
    group, (vector_ref, jac_ref, inv_ref, near_ref, z_ref) = refs[:members], refs[members:]
    vector = load(vector_ref)
    if rhs:
        vector = [-value for value in vector]
    acc = couple(jac_ref, near_ref, group_sources(group), 1, K, zero_acc(len(vector)))
    store(z_ref, apply_inverse(inv_ref, [v - stack_rows(c) for v, c in zip(vector, acc)]))


def second_sweep_kernel(rhs, members, *refs):
    group, refs = refs[:members], refs[members:]
    vector_ref, jac_ref, inv_ref, near_ref, served_ref, dots_ref, z_ref, far_ref, coupled_ref = refs
    vector = load(vector_ref)
    if rhs:
        vector = [-value for value in vector]
    acc = couple(jac_ref, near_ref, group_sources(group), 1, K, zero_acc(len(vector)))
    coupled = [stack_rows(c) for c in acc]
    result = apply_inverse(inv_ref, [v - c for v, c in zip(vector, coupled)])
    store(z_ref, result)
    store(coupled_ref, coupled)
    dots = dots_ref[...]
    lane = iota((8, LANES), 1)
    for d in range(far_ref.shape[0]):
        index = served_ref[d]
        lanes = index & (LANES - 1)
        picked = lane_gather(result[0], lanes)
        for h in range(1, len(result)):
            picked = jnp.where(index >> 7 == h, lane_gather(result[h], lanes), picked)
        far_ref[d] = jnp.where(lane < 64, picked, dots)


def combine(terms):
    return functools.reduce(lambda x, y: x + y, terms)


def orthogonalize(dots, step, gram):
    count = step + 1
    for i in range(count):
        gram[(i, step)] = gram[(step, i)] = dots[i]
    along = dots[count : 2 * count]
    hess = [gram[(i, step)] + along[i] for i in range(count)]
    coefs = [(1.0 - h if i == step else -h) for i, h in enumerate(hess)]
    square = dots[2 * count]
    for i in range(count):
        inner = combine([coefs[l] * gram[(i, l)] for l in range(count)])
        square = square + coefs[i] * (2.0 * along[i] + inner)
    length = jnp.sqrt(jnp.maximum(square, 0.0) + EPS)
    return hess, length, coefs


def read_scalars(refs):
    gram, hess, lengths = {}, {}, []
    beta = refs[0][0]
    for step, ref in enumerate(refs[1:]):
        count = step + 1
        for i in range(count):
            gram[(i, step)] = gram[(step, i)] = ref[i]
            hess[(i, step)] = ref[count + i]
        hess[(count, step)] = ref[2 * count]
    return beta, gram, hess


def operate_kernel(step, members, *refs):
    group, refs = refs[:members], refs[members:]
    far_ref, coupled_ref, vector_ref, jac_ref, inv_ref, near_ref, pos_ref = refs[:7]
    refs = refs[7:]
    states, scalar_refs = refs[:step], refs[step : 2 * step]
    state_ref, scalars_ref, vector_out_ref, z_ref, dots_ref = refs[2 * step :]
    devices = far_ref.shape[0]
    rows = coupled_ref.shape[1]
    count = halves_of(rows)
    per_owner = (K - K // 2) * rows // devices
    each = LANES // per_owner
    lane = iota((8, LANES), 1)

    arrived = []
    total = jnp.zeros((8, LANES), F32)
    for q in range(devices // each):
        out = far_ref[q * each]
        total = total + out
        for j in range(1, each):
            piece = far_ref[q * each + j]
            total = total + piece
            out = jnp.where(lane // per_owner == j, pltpu.roll(piece, j * per_owner, 1), out)
        arrived.append(out)

    acc = couple(jac_ref, near_ref, group_sources(group), 1, K // 2, zero_acc(count))
    acc = couple(jac_ref, pos_ref, [(lambda v=v: v) for v in arrived], K // 2, K, acc, K // 2)
    image = [stack_rows(c) - n for c, n in zip(acc, load(coupled_ref))]
    search = load(group[0])
    vector = load(vector_ref)

    if step == 0:
        vector = [-value for value in vector]
        length = jnp.sqrt(read_dots(total, 1)[0] + EPS)
        scalars_ref[0] = length
        coefs = []
    else:
        _, gram, _ = read_scalars(scalar_refs)
        dots = read_dots(total, 2 * step + 1)
        hess, length, coefs = orthogonalize(dots, step - 1, gram)
        for i in range(step):
            scalars_ref[i] = gram[(i, step - 1)]
            scalars_ref[step + i] = hess[i]
        scalars_ref[2 * step] = length
    scale = 1.0 / length

    def recombine(part, fresh):
        out = []
        for h, value in enumerate(fresh):
            for c, ref in zip(coefs, states):
                value = value + c * ref[part, :, half(h)]
            value = value * scale
            state_ref[part, :, half(h)] = value
            out.append(value)
        return out

    basis = [[ref[0, :, half(h)] for h in range(count)] for ref in states]
    basis.append(recombine(0, vector))
    recombine(1, search)
    image = recombine(2, image)
    store(vector_out_ref, image)
    store(z_ref, apply_inverse(inv_ref, image))
    pairs = [(b, basis[-1]) for b in basis] + [(b, image) for b in basis] + [(image, image)]
    block = dots_block(pairs)
    if step + 1 < KRYLOV:
        dots_ref[...] = block
    else:
        for d in range(devices):
            dots_ref[d] = block


def finish_kernel(dots_ref, *refs):
    states, scalar_refs = refs[:KRYLOV], refs[KRYLOV : 2 * KRYLOV]
    update_ref, first_ref = refs[2 * KRYLOV :]
    total = combine([dots_ref[d] for d in range(dots_ref.shape[0])])
    beta, gram, hess = read_scalars(scalar_refs)
    last, length, _ = orthogonalize(read_dots(total, 2 * KRYLOV + 1), KRYLOV - 1, gram)
    for i, value in enumerate(last):
        hess[(i, KRYLOV - 1)] = value
    hess[(KRYLOV, KRYLOV - 1)] = length

    work = [
        [combine([hess[(l, i)] * hess[(l, j)] for l in range(min(i, j) + 2)]) for j in range(KRYLOV)]
        for i in range(KRYLOV)
    ]
    vector = [beta * hess[(0, j)] for j in range(KRYLOV)]
    for p in range(KRYLOV):
        scale = 1.0 / work[p][p]
        top_work = [value * scale for value in work[p]]
        top = vector[p] * scale
        for i in range(KRYLOV):
            if i != p:
                factor = work[i][p]
                work[i] = [w - factor * t for w, t in zip(work[i], top_work)]
                vector[i] = vector[i] - factor * top
        work[p], vector[p] = top_work, top
    for h in range(halves_of(update_ref.shape[1])):
        update_ref[:, half(h)] = combine([c * ref[1, :, half(h)] for c, ref in zip(vector, states)])
        first_ref[:, half(h)] = beta * states[0][1, :, half(h)]


def shape(*dims, dtype=F32):
    return jax.ShapeDtypeStruct(dims, dtype)


def exchange(array, axes):
    return lax.all_to_all(array, axes, split_axis=0, concat_axis=0, tiled=True)


def gather_group(array):
    members = lax.axis_size("blk")
    return [array] + [
        lax.ppermute(array, "blk", [(i, (i + d) % members) for i in range(members)]) for d in range(1, members)
    ]


def local(stamps, stamp_target, pair_counts, conductance, block_cols, newton_residual):
    members = lax.axis_size("blk")
    devices = lax.axis_size("grp") * members
    rows = conductance.shape[1]
    me = lax.axis_index("grp") * members + lax.axis_index("blk")
    group_rows = rows * members
    place = jnp.stack([me, lax.rem(me + 1, devices), lax.axis_index("grp") * group_rows, group_rows]).astype(I32)

    send, to_next, own, near, pos = pl.pallas_call(
        pack_kernel,
        out_shape=(
            shape(devices, 24, LANES),
            shape(72, LANES),
            shape(72, LANES),
            shape(K, 8, rows, dtype=I32),
            shape(K - K // 2, 8, rows, dtype=I32),
        ),
        in_specs=[pl.BlockSpec(memory_space=pltpu.SMEM)] + [pl.BlockSpec(memory_space=pltpu.VMEM)] * 4,
        out_specs=tuple(pl.BlockSpec(memory_space=pltpu.VMEM) for _ in range(5)),
        compiler_params=pltpu.CompilerParams(vmem_limit_bytes=32 * 2**20),
    )(place, stamps[0], stamp_target[0], pair_counts.reshape(devices, 1), block_cols)
    got = exchange(send, AXES)
    prev = lax.ppermute(to_next, AXES, [(i, (i + 1) % devices) for i in range(devices)])

    width = 2 * LANES * min(devices // 4 + 2, 10)
    jacobian, inverse, served, z, dots = call(
        assemble_kernel,
        (
            shape(K, 8, 8, rows),
            shape(8, 8, rows),
            shape(devices, 8, LANES, dtype=I32),
            shape(8, rows),
            shape(8, LANES),
        ),
        got,
        prev,
        own,
        conductance,
        newton_residual,
        scratch=(pltpu.VMEM((64 * K, width), BF16), pltpu.VMEM((rows, width), BF16)),
    )

    states, scalars = [], []
    vector = newton_residual
    for step in range(KRYLOV):
        rhs = step == 0
        z = call(
            functools.partial(first_sweep_kernel, rhs, members),
            shape(8, rows),
            *gather_group(z),
            vector,
            jacobian,
            inverse,
            near,
        )
        z, far, coupled = call(
            functools.partial(second_sweep_kernel, rhs, members),
            (shape(8, rows), shape(devices, 8, LANES), shape(8, rows)),
            *gather_group(z),
            vector,
            jacobian,
            inverse,
            near,
            served,
            dots,
        )
        last = step + 1 == KRYLOV
        state, scalar, vector, z, dots = call(
            functools.partial(operate_kernel, step, members),
            (
                shape(3, 8, rows),
                shape(2 * step + 1, 8, LANES),
                shape(8, rows),
                shape(8, rows),
                shape(devices, 8, LANES) if last else shape(8, LANES),
            ),
            *gather_group(z),
            exchange(far, AXES),
            coupled,
            vector,
            jacobian,
            inverse,
            near,
            pos,
            *states,
            *scalars,
        )
        states.append(state)
        scalars.append(scalar)

    update, first = call(
        finish_kernel, (shape(8, rows), shape(8, rows)), exchange(dots, AXES), *states, *scalars
    )
    return update, jacobian, first


def solution(mesh):
    placed = (
        P(AXES, None, None, None),
        P(AXES, None, None),
        P(AXES, None),
        P(None, AXES),
        P(None, AXES),
        P(None, AXES),
    )
    return jax.shard_map(
        local,
        mesh=mesh,
        in_specs=placed,
        out_specs=(P(None, AXES), P(None, None, None, AXES), P(None, AXES)),
        check_vma=False,
    )
```

```python
import functools

import jax
import jax.numpy as jnp
from jax import lax
from jax.experimental import pallas as pl
from jax.experimental.pallas import tpu as pltpu
from jax.sharding import PartitionSpec as P

K = 16
KRYLOV = 5
LOW = 32
EPS = 1e-06
LANES = 128
AXES = ("grp", "blk")

F32 = jnp.float32
BF16 = jnp.bfloat16
I32 = jnp.int32

LANE_GATHER = lax.GatherDimensionNumbers(
    offset_dims=(),
    collapsed_slice_dims=(1,),
    start_index_map=(1,),
    operand_batching_dims=(0,),
    start_indices_batching_dims=(0,),
)


def lane_gather(source, lanes):
    return lax.gather(
        source,
        lanes[..., None],
        LANE_GATHER,
        slice_sizes=(1, 1),
        mode=lax.GatherScatterMode.PROMISE_IN_BOUNDS,
    )


def call(kernel, out_shape, *args, scratch=(), vmem=32 * 2**20):
    return pl.pallas_call(
        kernel,
        out_shape=out_shape,
        in_specs=[pl.BlockSpec(memory_space=pltpu.VMEM)] * len(args),
        out_specs=jax.tree.map(lambda _: pl.BlockSpec(memory_space=pltpu.VMEM), out_shape),
        scratch_shapes=list(scratch),
        compiler_params=pltpu.CompilerParams(vmem_limit_bytes=vmem),
    )(*args)


def iota(shape, axis):
    return lax.broadcasted_iota(I32, shape, axis)


def halves_of(rows):
    return rows // LANES


def half(index):
    return slice(index * LANES, (index + 1) * LANES)


def stack_rows(rows):
    sub = iota((8, LANES), 0)
    out = jnp.zeros((8, LANES), F32)
    for a, value in enumerate(rows):
        out = jnp.where(sub == a, jnp.sum(value, axis=0, keepdims=True), out)
    return out


def apply_inverse(inv_ref, vector):
    out = []
    for h, value in enumerate(vector):
        out.append(stack_rows([inv_ref[a, :, half(h)] * value for a in range(8)]))
    return out


def couple(jac_ref, index_ref, sources, first, last, acc, base=0):
    count = len(acc)

    def step(k, acc):
        out = []
        for h in range(count):
            index = index_ref[k - base, :, half(h)]
            at, lanes = index >> 7, index & (LANES - 1)
            picked = jnp.zeros((8, LANES), F32)
            for s, source in enumerate(sources):
                picked = jnp.where(at == s, lane_gather(source(), lanes), picked)
            out.append([acc[h][a] + jac_ref[k, a, :, half(h)] * picked for a in range(8)])
        return out

    return lax.fori_loop(first, last, step, acc)


def zero_acc(count):
    return [[jnp.zeros((8, LANES), F32) for _ in range(8)] for _ in range(count)]


def group_sources(refs):
    return [
        (lambda ref=ref, d=d, h=h: ref[d, :, half(h)])
        for ref in refs
        for d in range(ref.shape[0])
        for h in range(halves_of(ref.shape[2]))
    ]


def store(ref, vector):
    for h, value in enumerate(vector):
        ref[:, half(h)] = value


def load(ref):
    return [ref[:, half(h)] for h in range(halves_of(ref.shape[1]))]


def dots_block(pairs):
    sub, lane = iota((8, LANES), 0), iota((8, LANES), 1)
    blocks = []
    for start in (0, 8):
        rows = jnp.zeros((8, LANES), F32)
        for i, (left, right) in enumerate(pairs[start : start + 8]):
            total = sum(x * y for x, y in zip(left, right))
            rows = jnp.where(sub == i, jnp.sum(total, axis=0, keepdims=True), rows)
        blocks.append(jnp.sum(rows, axis=1, keepdims=True))
    return jnp.where(lane < 96, blocks[0], blocks[1])


def read_dots(total, count):
    lane = iota((8, LANES), 1)
    out = []
    for at in (64, 96):
        column = jnp.sum(jnp.where(lane == at, total, 0.0), axis=1, keepdims=True)
        column = jnp.broadcast_to(column, (8, LANES))
        out += [jnp.broadcast_to(column[i : i + 1, :], (8, LANES)) for i in range(8)]
    return out[:count]


def pack_kernel(
    place_ref, stamps_ref, target_ref, counts_ref, cols_ref, send_ref, next_ref, own_ref, near_ref, pos_ref
):
    devices = stamps_ref.shape[0]
    local_rows = cols_ref.shape[1]
    far_slots = K - K // 2
    per_owner = far_slots * local_rows // devices
    me, nxt = place_ref[0], place_ref[1]
    group_start, group_rows = place_ref[2], place_ref[3]
    lane = iota((1, LANES), 1)

    live = iota((devices, LANES), 1) < counts_ref[...]
    target = jnp.where(live, target_ref[...], -1).astype(F32)
    for ref, at in ((next_ref, nxt), (own_ref, me)):
        ref[0:64, :] = stamps_ref[at]
        mine = iota((devices, LANES), 0) == at
        row = jnp.sum(jnp.where(mine, target, 0.0), axis=0, keepdims=True)
        ref[64:72, :] = jnp.broadcast_to(row, (8, LANES))
    ids = iota((devices, LANES), 0)
    low = jnp.where((ids == me) | (ids == nxt) | (iota((devices, LANES), 1) >= LOW), -1.0, target)

    owners = iota((devices, LANES), 0)
    before = (iota((LANES, LANES), 0) < iota((LANES, LANES), 1)).astype(BF16)
    running = jnp.zeros((devices, 1), F32)
    asked = jnp.zeros((devices, LANES), F32)
    tiled = iota((LANES, LANES), 0) & (per_owner - 1)
    for k in range(far_slots):
        for h in range(halves_of(local_rows)):
            cols = cols_ref[K // 2 + k : K // 2 + k + 1, half(h)]
            owner = cols // local_rows
            row = cols - owner * local_rows
            hot = (owners == owner).astype(F32)
            ahead = jnp.dot(hot.astype(BF16), before, preferred_element_type=F32) + running
            running = running + jnp.sum(hot, axis=1, keepdims=True)
            rank = jnp.sum(hot * ahead, axis=0, keepdims=True).astype(I32)
            asked += lax.dot_general(
                (hot * row.astype(F32)).astype(BF16),
                (tiled == rank).astype(F32).astype(BF16),
                (((1,), (1,)), ((), ())),
                preferred_element_type=F32,
            )
            pos_ref[k, :, half(h)] = jnp.broadcast_to(owner * per_owner + rank, (8, LANES))

    for d in range(devices):
        packed = jnp.zeros((16, LANES), F32)
        for g in range(4):
            piece = stamps_ref[d, 16 * g : 16 * g + 16, :]
            if g:
                piece = pltpu.roll(piece, LOW * g, 1)
            packed = jnp.where(lane // LOW == g, piece, packed)
        send_ref[d, 0:16, :] = packed
        sub = iota((8, LANES), 0)
        send_ref[d, 16:24, :] = jnp.where(sub == 0, low[d : d + 1, :], asked[d : d + 1, :])

    for k in range(K):
        for h in range(halves_of(local_rows)):
            cols = cols_ref[k : k + 1, half(h)]
            near = (cols >= group_start) & (cols < group_start + group_rows)
            owner = cols // local_rows
            index = (owner ^ me) * local_rows + (cols - owner * local_rows)
            near_ref[k, :, half(h)] = jnp.broadcast_to(jnp.where(near, index, -1), (8, LANES))


def assemble_kernel(
    recv_ref, prev_ref, own_ref, cond_ref, resid_ref, jac_ref, inv_ref, served_ref, z_ref, dots_ref, left_ref, right_ref
):
    devices = recv_ref.shape[0]
    local_rows = cond_ref.shape[1]
    lane = iota((1, LANES), 1)
    blocks = devices // 4 + 2

    def block(q):
        if q == 0:
            return own_ref[0:64, :], own_ref[64:65, :]
        if q == 1:
            return prev_ref[0:64, :], prev_ref[64:65, :]
        first = 4 * (q - 2)
        rows = []
        for g in range(4):
            out = jnp.zeros((16, LANES), F32)
            for j in range(4):
                piece = recv_ref[first + j, 0:16, :]
                if j != g:
                    piece = pltpu.roll(piece, (LOW * (j - g)) % LANES, 1)
                out = jnp.where(lane // LOW == j, piece, out)
            rows.append(out)
        target = jnp.full((1, LANES), -1.0, F32)
        for j in range(4):
            piece = recv_ref[first + j, 16:17, :]
            if j:
                piece = pltpu.roll(piece, LOW * j, 1)
            target = jnp.where(lane // LOW == j, piece, target)
        return jnp.concatenate(rows, axis=0), target

    most = 10
    for start in range(0, blocks, most):
        stop = min(start + most, blocks)
        width = 2 * (stop - start) * LANES
        values = []
        for q in range(start, stop):
            at = 2 * (q - start) * LANES
            stamp, target = block(q)
            target = target.astype(I32)
            slot, row = target >> (local_rows.bit_length() - 1), target & (local_rows - 1)
            hot = (iota((local_rows, LANES), 0) == row).astype(F32).astype(BF16)
            right_ref[:, at : at + LANES] = hot
            right_ref[:, at + LANES : at + 2 * LANES] = hot
            high = stamp.astype(BF16)
            low = (stamp - high.astype(F32)).astype(BF16)
            values.append((at, slot, high, low))

        for k in range(K):
            for at, slot, high, low in values:
                mask = (slot == k).astype(F32).astype(BF16)
                left_ref[64 * k : 64 * k + 64, at : at + LANES] = high * mask
                left_ref[64 * k : 64 * k + 64, at + LANES : at + 2 * LANES] = low * mask
        total = lax.dot_general(
            left_ref[:, 0:width],
            right_ref[:, 0:width],
            (((1,), (1,)), ((), ())),
            preferred_element_type=F32,
        ).reshape(K, 8, 8, local_rows)
        if start == 0:
            jac_ref[...] = total
        else:
            jac_ref[...] += total
    sub = iota((8, local_rows), 0)
    for a in range(8):
        jac_ref[0, a] = jac_ref[0, a] + jnp.where(sub == a, cond_ref[a : a + 1, :], 0.0)

    work = [jac_ref[0, a] for a in range(8)]
    inverse = [jnp.where(sub == a, 1.0, 0.0).astype(F32) for a in range(8)]
    for p in range(8):
        scale = 1.0 / work[p][p : p + 1, :]
        top_work, top_inverse = work[p] * scale, inverse[p] * scale
        for a in range(8):
            if a != p:
                factor = work[a][p : p + 1, :]
                work[a] = work[a] - factor * top_work
                inverse[a] = inverse[a] - factor * top_inverse
        work[p], inverse[p] = top_work, top_inverse
    for a in range(8):
        inv_ref[a] = inverse[a]

    for d in range(devices):
        served_ref[d] = jnp.broadcast_to(recv_ref[d, 17:18, :].astype(I32), (8, LANES))
    rhs = [-value for value in load(resid_ref)]
    store(z_ref, apply_inverse(inv_ref, rhs))
    dots_ref[...] = dots_block([(rhs, rhs)])


def first_sweep_kernel(rhs, held_ref, other_ref, vector_ref, jac_ref, inv_ref, near_ref, z_ref):
    group = held_ref, other_ref
    vector = load(vector_ref)
    if rhs:
        vector = [-value for value in vector]
    acc = couple(jac_ref, near_ref, group_sources(group), 1, K, zero_acc(len(vector)))
    store(z_ref, apply_inverse(inv_ref, [v - stack_rows(c) for v, c in zip(vector, acc)]))


def second_sweep_kernel(
    rhs,
    held_ref,
    other_ref,
    vector_ref,
    jac_ref,
    inv_ref,
    near_ref,
    served_ref,
    dots_ref,
    z_ref,
    far_ref,
    coupled_ref,
):
    group = held_ref, other_ref
    vector = load(vector_ref)
    if rhs:
        vector = [-value for value in vector]
    acc = couple(jac_ref, near_ref, group_sources(group), 1, K, zero_acc(len(vector)))
    coupled = [stack_rows(c) for c in acc]
    result = apply_inverse(inv_ref, [v - c for v, c in zip(vector, coupled)])
    store(z_ref, result)
    store(coupled_ref, coupled)
    dots = dots_ref[...]
    lane = iota((8, LANES), 1)
    for d in range(far_ref.shape[0]):
        index = served_ref[d]
        lanes = index & (LANES - 1)
        picked = lane_gather(result[0], lanes)
        for h in range(1, len(result)):
            picked = jnp.where(index >> 7 == h, lane_gather(result[h], lanes), picked)
        far_ref[d] = jnp.where(lane < 64, picked, dots)


def combine(terms):
    return functools.reduce(lambda x, y: x + y, terms)


def orthogonalize(dots, step, gram):
    count = step + 1
    for i in range(count):
        gram[(i, step)] = gram[(step, i)] = dots[i]
    along = dots[count : 2 * count]
    hess = [gram[(i, step)] + along[i] for i in range(count)]
    coefs = [(1.0 - h if i == step else -h) for i, h in enumerate(hess)]
    square = dots[2 * count]
    for i in range(count):
        inner = combine([coefs[l] * gram[(i, l)] for l in range(count)])
        square = square + coefs[i] * (2.0 * along[i] + inner)
    length = jnp.sqrt(jnp.maximum(square, 0.0) + EPS)
    return hess, length, coefs


def read_scalars(refs):
    gram, hess, lengths = {}, {}, []
    beta = refs[0][0]
    for step, ref in enumerate(refs[1:]):
        count = step + 1
        for i in range(count):
            gram[(i, step)] = gram[(step, i)] = ref[i]
            hess[(i, step)] = ref[count + i]
        hess[(count, step)] = ref[2 * count]
    return beta, gram, hess


def operate_kernel(step, *refs):
    held_ref, other_ref, far_ref, coupled_ref, vector_ref, jac_ref, inv_ref, near_ref, pos_ref = refs[:9]
    group, refs = (held_ref, other_ref), refs[9:]
    states, scalar_refs = refs[:step], refs[step : 2 * step]
    state_ref, scalars_ref, vector_out_ref, z_ref, dots_ref = refs[2 * step :]
    devices = far_ref.shape[0]
    rows = coupled_ref.shape[1]
    count = halves_of(rows)
    per_owner = (K - K // 2) * rows // devices
    each = LANES // per_owner
    lane = iota((8, LANES), 1)

    arrived = []
    total = jnp.zeros((8, LANES), F32)
    for q in range(devices // each):
        out = far_ref[q * each]
        total = total + out
        for j in range(1, each):
            piece = far_ref[q * each + j]
            total = total + piece
            out = jnp.where(lane // per_owner == j, pltpu.roll(piece, j * per_owner, 1), out)
        arrived.append(out)

    acc = couple(jac_ref, near_ref, group_sources(group), 1, K // 2, zero_acc(count))
    acc = couple(jac_ref, pos_ref, [(lambda v=v: v) for v in arrived], K // 2, K, acc, K // 2)
    image = [stack_rows(c) - n for c, n in zip(acc, load(coupled_ref))]
    search = [held_ref[0, :, half(h)] for h in range(count)]
    vector = load(vector_ref)

    if step == 0:
        vector = [-value for value in vector]
        length = jnp.sqrt(read_dots(total, 1)[0] + EPS)
        scalars_ref[0] = length
        coefs = []
    else:
        _, gram, _ = read_scalars(scalar_refs)
        dots = read_dots(total, 2 * step + 1)
        hess, length, coefs = orthogonalize(dots, step - 1, gram)
        for i in range(step):
            scalars_ref[i] = gram[(i, step - 1)]
            scalars_ref[step + i] = hess[i]
        scalars_ref[2 * step] = length
    scale = 1.0 / length

    def recombine(part, fresh):
        out = []
        for h, value in enumerate(fresh):
            for c, ref in zip(coefs, states):
                value = value + c * ref[part, :, half(h)]
            value = value * scale
            state_ref[part, :, half(h)] = value
            out.append(value)
        return out

    basis = [[ref[0, :, half(h)] for h in range(count)] for ref in states]
    basis.append(recombine(0, vector))
    recombine(1, search)
    image = recombine(2, image)
    store(vector_out_ref, image)
    store(z_ref, apply_inverse(inv_ref, image))
    pairs = [(b, basis[-1]) for b in basis] + [(b, image) for b in basis] + [(image, image)]
    block = dots_block(pairs)
    if step + 1 < KRYLOV:
        dots_ref[...] = block
    else:
        for d in range(devices):
            dots_ref[d] = block


def finish_kernel(dots_ref, *refs):
    states, scalar_refs = refs[:KRYLOV], refs[KRYLOV : 2 * KRYLOV]
    update_ref, first_ref = refs[2 * KRYLOV :]
    total = combine([dots_ref[d] for d in range(dots_ref.shape[0])])
    beta, gram, hess = read_scalars(scalar_refs)
    last, length, _ = orthogonalize(read_dots(total, 2 * KRYLOV + 1), KRYLOV - 1, gram)
    for i, value in enumerate(last):
        hess[(i, KRYLOV - 1)] = value
    hess[(KRYLOV, KRYLOV - 1)] = length

    work = [
        [combine([hess[(l, i)] * hess[(l, j)] for l in range(min(i, j) + 2)]) for j in range(KRYLOV)]
        for i in range(KRYLOV)
    ]
    vector = [beta * hess[(0, j)] for j in range(KRYLOV)]
    for p in range(KRYLOV):
        scale = 1.0 / work[p][p]
        top_work = [value * scale for value in work[p]]
        top = vector[p] * scale
        for i in range(KRYLOV):
            if i != p:
                factor = work[i][p]
                work[i] = [w - factor * t for w, t in zip(work[i], top_work)]
                vector[i] = vector[i] - factor * top
        work[p], vector[p] = top_work, top
    for h in range(halves_of(update_ref.shape[1])):
        update_ref[:, half(h)] = combine([c * ref[1, :, half(h)] for c, ref in zip(vector, states)])
        first_ref[:, half(h)] = beta * states[0][1, :, half(h)]


def shape(*dims, dtype=F32):
    return jax.ShapeDtypeStruct(dims, dtype)


def exchange(array, axes):
    return lax.all_to_all(array, axes, split_axis=0, concat_axis=0, tiled=True)


def gather_group(array):
    members = lax.axis_size("blk")
    held = array[None]
    while True:
        bit = held.shape[0]
        other = lax.ppermute(held, "blk", [(i, i ^ bit) for i in range(members)])
        if 2 * bit == members:
            return held, other
        held = jnp.concatenate([held, other])


def local(stamps, stamp_target, pair_counts, conductance, block_cols, newton_residual):
    members = lax.axis_size("blk")
    devices = lax.axis_size("grp") * members
    rows = conductance.shape[1]
    me = lax.axis_index("grp") * members + lax.axis_index("blk")
    group_rows = rows * members
    place = jnp.stack([me, lax.rem(me + 1, devices), lax.axis_index("grp") * group_rows, group_rows]).astype(I32)

    send, to_next, own, near, pos = pl.pallas_call(
        pack_kernel,
        out_shape=(
            shape(devices, 24, LANES),
            shape(72, LANES),
            shape(72, LANES),
            shape(K, 8, rows, dtype=I32),
            shape(K - K // 2, 8, rows, dtype=I32),
        ),
        in_specs=[pl.BlockSpec(memory_space=pltpu.SMEM)] + [pl.BlockSpec(memory_space=pltpu.VMEM)] * 4,
        out_specs=tuple(pl.BlockSpec(memory_space=pltpu.VMEM) for _ in range(5)),
        compiler_params=pltpu.CompilerParams(vmem_limit_bytes=32 * 2**20),
    )(place, stamps[0], stamp_target[0], pair_counts.reshape(devices, 1), block_cols)
    got = exchange(send, AXES)
    prev = lax.ppermute(to_next, AXES, [(i, (i + 1) % devices) for i in range(devices)])

    width = 2 * LANES * min(devices // 4 + 2, 10)
    jacobian, inverse, served, z, dots = call(
        assemble_kernel,
        (
            shape(K, 8, 8, rows),
            shape(8, 8, rows),
            shape(devices, 8, LANES, dtype=I32),
            shape(8, rows),
            shape(8, LANES),
        ),
        got,
        prev,
        own,
        conductance,
        newton_residual,
        scratch=(pltpu.VMEM((64 * K, width), BF16), pltpu.VMEM((rows, width), BF16)),
    )

    states, scalars = [], []
    vector = newton_residual
    for step in range(KRYLOV):
        rhs = step == 0
        z = call(
            functools.partial(first_sweep_kernel, rhs),
            shape(8, rows),
            *gather_group(z),
            vector,
            jacobian,
            inverse,
            near,
        )
        z, far, coupled = call(
            functools.partial(second_sweep_kernel, rhs),
            (shape(8, rows), shape(devices, 8, LANES), shape(8, rows)),
            *gather_group(z),
            vector,
            jacobian,
            inverse,
            near,
            served,
            dots,
        )
        last = step + 1 == KRYLOV
        state, scalar, vector, z, dots = call(
            functools.partial(operate_kernel, step),
            (
                shape(3, 8, rows),
                shape(2 * step + 1, 8, LANES),
                shape(8, rows),
                shape(8, rows),
                shape(devices, 8, LANES) if last else shape(8, LANES),
            ),
            *gather_group(z),
            exchange(far, AXES),
            coupled,
            vector,
            jacobian,
            inverse,
            near,
            pos,
            *states,
            *scalars,
        )
        states.append(state)
        scalars.append(scalar)

    update, first = call(
        finish_kernel, (shape(8, rows), shape(8, rows)), exchange(dots, AXES), *states, *scalars
    )
    return update, jacobian, first


def solution(mesh):
    placed = (
        P(AXES, None, None, None),
        P(AXES, None, None),
        P(AXES, None),
        P(None, AXES),
        P(None, AXES),
        P(None, AXES),
    )
    return jax.shard_map(
        local,
        mesh=mesh,
        in_specs=placed,
        out_specs=(P(None, AXES), P(None, None, None, AXES), P(None, AXES)),
        check_vma=False,
    )
```

```python
import functools

import jax
import jax.numpy as jnp
from jax import lax
from jax.experimental import pallas as pl
from jax.experimental.pallas import tpu as pltpu
from jax.sharding import PartitionSpec as P

K = 16
KRYLOV = 5
LOW = 32
EPS = 1e-06
LANES = 128
AXES = ("grp", "blk")

F32 = jnp.float32
BF16 = jnp.bfloat16
I32 = jnp.int32

LANE_GATHER = lax.GatherDimensionNumbers(
    offset_dims=(),
    collapsed_slice_dims=(1,),
    start_index_map=(1,),
    operand_batching_dims=(0,),
    start_indices_batching_dims=(0,),
)


def lane_gather(source, lanes):
    return lax.gather(
        source,
        lanes[..., None],
        LANE_GATHER,
        slice_sizes=(1, 1),
        mode=lax.GatherScatterMode.PROMISE_IN_BOUNDS,
    )


def call(kernel, out_shape, *args, scratch=(), vmem=32 * 2**20):
    return pl.pallas_call(
        kernel,
        out_shape=out_shape,
        in_specs=[pl.BlockSpec(memory_space=pltpu.SMEM if arg.dtype == I32 and arg.ndim == 1 else pltpu.VMEM) for arg in args],
        out_specs=jax.tree.map(lambda _: pl.BlockSpec(memory_space=pltpu.VMEM), out_shape),
        scratch_shapes=list(scratch),
        compiler_params=pltpu.CompilerParams(vmem_limit_bytes=vmem),
    )(*args)


def iota(shape, axis):
    return lax.broadcasted_iota(I32, shape, axis)


def halves_of(rows):
    return rows // LANES


def half(index):
    return slice(index * LANES, (index + 1) * LANES)


def stack_rows(rows):
    sub = iota((8, LANES), 0)
    out = jnp.zeros((8, LANES), F32)
    for a, value in enumerate(rows):
        out = jnp.where(sub == a, jnp.sum(value, axis=0, keepdims=True), out)
    return out


def apply_inverse(inv_ref, vector):
    out = []
    for h, value in enumerate(vector):
        out.append(stack_rows([inv_ref[a, :, half(h)] * value for a in range(8)]))
    return out


def couple(jac_ref, index_ref, sources, first, last, acc, base=0, flip=None):
    count = len(acc)

    def step(k, acc):
        out = []
        for h in range(count):
            index = index_ref[k - base, :, half(h)]
            if flip is not None:
                index = index ^ flip
            at, lanes = index >> 7, index & (LANES - 1)
            picked = jnp.zeros((8, LANES), F32)
            for s, source in enumerate(sources):
                picked = jnp.where(at == s, lane_gather(source(), lanes), picked)
            out.append([acc[h][a] + jac_ref[k, a, :, half(h)] * picked for a in range(8)])
        return out

    for k in range(first, last):
        acc = step(k, acc)
    return acc


def zero_acc(count):
    return [[jnp.zeros((8, LANES), F32) for _ in range(8)] for _ in range(count)]


def group_sources(refs):
    return [
        (lambda ref=ref, d=d, h=h: ref[d, :, half(h)])
        for ref in refs
        for d in range(ref.shape[0])
        for h in range(halves_of(ref.shape[2]))
    ]


def store(ref, vector):
    for h, value in enumerate(vector):
        ref[:, half(h)] = value


def spread(ref, vector):
    for d in range(ref.shape[0]):
        for h, value in enumerate(vector):
            ref[d, :, half(h)] = value


def load(ref):
    return [ref[:, half(h)] for h in range(halves_of(ref.shape[1]))]


def dots_block(pairs):
    sub, lane = iota((8, LANES), 0), iota((8, LANES), 1)
    blocks = []
    for start in (0, 8):
        rows = jnp.zeros((8, LANES), F32)
        for i, (left, right) in enumerate(pairs[start : start + 8]):
            total = sum(x * y for x, y in zip(left, right))
            rows = jnp.where(sub == i, jnp.sum(total, axis=0, keepdims=True), rows)
        blocks.append(jnp.sum(rows, axis=1, keepdims=True))
    return jnp.where(lane < 96, blocks[0], blocks[1])


def read_dots(total, count):
    lane = iota((8, LANES), 1)
    out = []
    for at in (64, 96):
        column = jnp.sum(jnp.where(lane == at, total, 0.0), axis=1, keepdims=True)
        column = jnp.broadcast_to(column, (8, LANES))
        out += [jnp.broadcast_to(column[i : i + 1, :], (8, LANES)) for i in range(8)]
    return out[:count]


def pack_kernel(
    place_ref, stamps_ref, target_ref, counts_ref, cols_ref, send_ref, next_ref, own_ref, near_ref, pos_ref
):
    devices = stamps_ref.shape[0]
    local_rows = cols_ref.shape[1]
    far_slots = K - K // 2
    per_owner = far_slots * local_rows // devices
    me, nxt = place_ref[0], place_ref[1]
    group_start, group_rows = place_ref[2], place_ref[3]
    lane = iota((1, LANES), 1)

    live = iota((devices, LANES), 1) < counts_ref[...]
    target = jnp.where(live, target_ref[...], -1).astype(F32)
    for ref, at in ((next_ref, nxt), (own_ref, me)):
        ref[0:64, :] = stamps_ref[at]
        mine = iota((devices, LANES), 0) == at
        row = jnp.sum(jnp.where(mine, target, 0.0), axis=0, keepdims=True)
        ref[64:72, :] = jnp.broadcast_to(row, (8, LANES))
    ids = iota((devices, LANES), 0)
    low = jnp.where((ids == me) | (ids == nxt) | (iota((devices, LANES), 1) >= LOW), -1.0, target)

    owners = iota((devices, LANES), 0)
    before = (iota((LANES, LANES), 0) < iota((LANES, LANES), 1)).astype(BF16)
    running = jnp.zeros((devices, 1), F32)
    asked = jnp.zeros((devices, LANES), F32)
    tiled = iota((LANES, LANES), 0) & (per_owner - 1)
    for k in range(far_slots):
        for h in range(halves_of(local_rows)):
            cols = cols_ref[K // 2 + k : K // 2 + k + 1, half(h)]
            owner = cols // local_rows
            row = cols - owner * local_rows
            hot = (owners == owner).astype(F32)
            ahead = jnp.dot(hot.astype(BF16), before, preferred_element_type=F32) + running
            running = running + jnp.sum(hot, axis=1, keepdims=True)
            rank = jnp.sum(hot * ahead, axis=0, keepdims=True).astype(I32)
            asked += lax.dot_general(
                (hot * row.astype(F32)).astype(BF16),
                (tiled == rank).astype(F32).astype(BF16),
                (((1,), (1,)), ((), ())),
                preferred_element_type=F32,
            )
            pos_ref[k, :, half(h)] = jnp.broadcast_to(owner * per_owner + rank, (8, LANES))

    for d in range(devices):
        packed = jnp.zeros((16, LANES), F32)
        for g in range(4):
            piece = stamps_ref[d, 16 * g : 16 * g + 16, :]
            if g:
                piece = pltpu.roll(piece, LOW * g, 1)
            packed = jnp.where(lane // LOW == g, piece, packed)
        send_ref[d, 0:16, :] = packed
        sub = iota((8, LANES), 0)
        send_ref[d, 16:24, :] = jnp.where(sub == 0, low[d : d + 1, :], asked[d : d + 1, :])

    for k in range(K):
        for h in range(halves_of(local_rows)):
            cols = cols_ref[k : k + 1, half(h)]
            near = (cols >= group_start) & (cols < group_start + group_rows)
            near_ref[k, :, half(h)] = jnp.broadcast_to(jnp.where(near, cols - group_start, -1), (8, LANES))


def assemble_kernel(
    recv_ref, prev_ref, own_ref, cond_ref, resid_ref, whole_ref, jac_ref, inv_ref, served_ref, z_ref, dots_ref, left_ref, right_ref
):
    devices = recv_ref.shape[0]
    local_rows = cond_ref.shape[1]
    lane = iota((1, LANES), 1)
    blocks = devices // 4 + 2

    def block(q):
        if q == 0:
            return own_ref[0:64, :], own_ref[64:65, :]
        if q == 1:
            return prev_ref[0:64, :], prev_ref[64:65, :]
        first = 4 * (q - 2)
        rows = []
        for g in range(4):
            out = jnp.zeros((16, LANES), F32)
            for j in range(4):
                piece = recv_ref[first + j, 0:16, :]
                if j != g:
                    piece = pltpu.roll(piece, (LOW * (j - g)) % LANES, 1)
                out = jnp.where(lane // LOW == j, piece, out)
            rows.append(out)
        target = jnp.full((1, LANES), -1.0, F32)
        for j in range(4):
            piece = recv_ref[first + j, 16:17, :]
            if j:
                piece = pltpu.roll(piece, LOW * j, 1)
            target = jnp.where(lane // LOW == j, piece, target)
        return jnp.concatenate(rows, axis=0), target

    most = 10
    for start in range(0, blocks, most):
        stop = min(start + most, blocks)
        width = 2 * (stop - start) * LANES
        values = []
        for q in range(start, stop):
            at = 2 * (q - start) * LANES
            stamp, target = block(q)
            target = target.astype(I32)
            slot, row = target >> (local_rows.bit_length() - 1), target & (local_rows - 1)
            hot = (iota((local_rows, LANES), 0) == row).astype(F32).astype(BF16)
            right_ref[:, at : at + LANES] = hot
            right_ref[:, at + LANES : at + 2 * LANES] = hot
            high = stamp.astype(BF16)
            low = (stamp - high.astype(F32)).astype(BF16)
            values.append((at, slot, high, low))

        for k in range(K):
            for at, slot, high, low in values:
                mask = (slot == k).astype(F32).astype(BF16)
                left_ref[64 * k : 64 * k + 64, at : at + LANES] = high * mask
                left_ref[64 * k : 64 * k + 64, at + LANES : at + 2 * LANES] = low * mask
        total = lax.dot_general(
            left_ref[:, 0:width],
            right_ref[:, 0:width],
            (((1,), (1,)), ((), ())),
            preferred_element_type=F32,
        ).reshape(K, 8, 8, local_rows)
        if start == 0:
            jac_ref[...] = total
        else:
            jac_ref[...] += total
    sub = iota((8, local_rows), 0)
    for a in range(8):
        jac_ref[0, a] = jac_ref[0, a] + jnp.where(sub == a, cond_ref[a : a + 1, :], 0.0)

    whole_ref[...] = jac_ref[...]

    work = [jac_ref[0, a] for a in range(8)]
    inverse = [jnp.where(sub == a, 1.0, 0.0).astype(F32) for a in range(8)]
    for p in range(8):
        scale = 1.0 / work[p][p : p + 1, :]
        top_work, top_inverse = work[p] * scale, inverse[p] * scale
        for a in range(8):
            if a != p:
                factor = work[a][p : p + 1, :]
                work[a] = work[a] - factor * top_work
                inverse[a] = inverse[a] - factor * top_inverse
        work[p], inverse[p] = top_work, top_inverse
    for a in range(8):
        inv_ref[a] = inverse[a]

    for d in range(devices):
        served_ref[d] = jnp.broadcast_to(recv_ref[d, 17:18, :].astype(I32), (8, LANES))
    rhs = [-value for value in load(resid_ref)]
    spread(z_ref, apply_inverse(inv_ref, rhs))
    dots_ref[...] = dots_block([(rhs, rhs)])


def first_sweep_kernel(rhs, group_ref, vector_ref, jac_ref, inv_ref, near_ref, z_ref):
    vector = load(vector_ref)
    if rhs:
        vector = [-value for value in vector]
    acc = couple(jac_ref, near_ref, group_sources([group_ref]), 1, K, zero_acc(len(vector)))
    spread(z_ref, apply_inverse(inv_ref, [v - stack_rows(c) for v, c in zip(vector, acc)]))


def second_sweep_kernel(
    rhs,
    group_ref,
    vector_ref,
    jac_ref,
    inv_ref,
    near_ref,
    served_ref,
    dots_ref,
    z_ref,
    far_ref,
    coupled_ref,
):
    vector = load(vector_ref)
    if rhs:
        vector = [-value for value in vector]
    acc = couple(jac_ref, near_ref, group_sources([group_ref]), 1, K, zero_acc(len(vector)))
    coupled = [stack_rows(c) for c in acc]
    result = apply_inverse(inv_ref, [v - c for v, c in zip(vector, coupled)])
    z_ref[0, :, :] = jnp.concatenate(result, axis=1)
    store(coupled_ref, coupled)
    dots = dots_ref[...]
    lane = iota((8, LANES), 1)
    for d in range(far_ref.shape[0]):
        index = served_ref[d]
        lanes = index & (LANES - 1)
        picked = lane_gather(result[0], lanes)
        for h in range(1, len(result)):
            picked = jnp.where(index >> 7 == h, lane_gather(result[h], lanes), picked)
        far_ref[d] = jnp.where(lane < 64, picked, dots)


def combine(terms):
    return functools.reduce(lambda x, y: x + y, terms)


def orthogonalize(dots, step, gram):
    count = step + 1
    for i in range(count):
        gram[(i, step)] = gram[(step, i)] = dots[i]
    along = dots[count : 2 * count]
    hess = [gram[(i, step)] + along[i] for i in range(count)]
    coefs = [(1.0 - h if i == step else -h) for i, h in enumerate(hess)]
    square = dots[2 * count]
    for i in range(count):
        inner = combine([coefs[l] * gram[(i, l)] for l in range(count)])
        square = square + coefs[i] * (2.0 * along[i] + inner)
    length = jnp.sqrt(jnp.maximum(square, 0.0) + EPS)
    return hess, length, coefs


def read_scalars(refs):
    gram, hess, lengths = {}, {}, []
    beta = refs[0][0]
    for step, ref in enumerate(refs[1:]):
        count = step + 1
        for i in range(count):
            gram[(i, step)] = gram[(step, i)] = ref[i]
            hess[(i, step)] = ref[count + i]
        hess[(count, step)] = ref[2 * count]
    return beta, gram, hess


def operate_kernel(step, parts, place_ref, *refs):
    group, refs = refs[:parts], refs[parts:]
    far_ref, coupled_ref, vector_ref, jac_ref, inv_ref, near_ref, pos_ref = refs[:7]
    refs = refs[7:]
    states, scalar_refs = refs[:step], refs[step : 2 * step]
    state_ref, scalars_ref, vector_out_ref, z_ref, dots_ref = refs[2 * step :]
    devices = far_ref.shape[0]
    rows = coupled_ref.shape[1]
    count = halves_of(rows)
    per_owner = (K - K // 2) * rows // devices
    each = LANES // per_owner
    lane = iota((8, LANES), 1)

    arrived = []
    total = jnp.zeros((8, LANES), F32)
    for q in range(devices // each):
        out = far_ref[q * each]
        total = total + out
        for j in range(1, each):
            piece = far_ref[q * each + j]
            total = total + piece
            out = jnp.where(lane // per_owner == j, pltpu.roll(piece, j * per_owner, 1), out)
        arrived.append(out)

    acc = couple(jac_ref, near_ref, group_sources(group), 1, K // 2, zero_acc(count), flip=place_ref[4])
    acc = couple(jac_ref, pos_ref, [(lambda v=v: v) for v in arrived], K // 2, K, acc, K // 2)
    image = [stack_rows(c) - n for c, n in zip(acc, load(coupled_ref))]
    search = [group[0][0, :, half(h)] for h in range(count)]
    vector = load(vector_ref)

    if step == 0:
        vector = [-value for value in vector]
        length = jnp.sqrt(read_dots(total, 1)[0] + EPS)
        scalars_ref[0] = length
        coefs = []
    else:
        _, gram, _ = read_scalars(scalar_refs)
        dots = read_dots(total, 2 * step + 1)
        hess, length, coefs = orthogonalize(dots, step - 1, gram)
        for i in range(step):
            scalars_ref[i] = gram[(i, step - 1)]
            scalars_ref[step + i] = hess[i]
        scalars_ref[2 * step] = length
    scale = 1.0 / length

    def recombine(part, fresh):
        out = []
        for h, value in enumerate(fresh):
            for c, ref in zip(coefs, states):
                value = value + c * ref[part, :, half(h)]
            value = value * scale
            state_ref[part, :, half(h)] = value
            out.append(value)
        return out

    basis = [[ref[0, :, half(h)] for h in range(count)] for ref in states]
    basis.append(recombine(0, vector))
    recombine(1, search)
    image = recombine(2, image)
    store(vector_out_ref, image)
    spread(z_ref, apply_inverse(inv_ref, image))
    pairs = [(b, basis[-1]) for b in basis] + [(b, image) for b in basis] + [(image, image)]
    block = dots_block(pairs)
    if step + 1 < KRYLOV:
        dots_ref[...] = block
    else:
        for d in range(devices):
            dots_ref[d] = block


def finish_kernel(dots_ref, *refs):
    states, scalar_refs = refs[:KRYLOV], refs[KRYLOV : 2 * KRYLOV]
    update_ref, first_ref = refs[2 * KRYLOV :]
    total = combine([dots_ref[d] for d in range(dots_ref.shape[0])])
    beta, gram, hess = read_scalars(scalar_refs)
    last, length, _ = orthogonalize(read_dots(total, 2 * KRYLOV + 1), KRYLOV - 1, gram)
    for i, value in enumerate(last):
        hess[(i, KRYLOV - 1)] = value
    hess[(KRYLOV, KRYLOV - 1)] = length

    work = [
        [combine([hess[(l, i)] * hess[(l, j)] for l in range(min(i, j) + 2)]) for j in range(KRYLOV)]
        for i in range(KRYLOV)
    ]
    vector = [beta * hess[(0, j)] for j in range(KRYLOV)]
    for p in range(KRYLOV):
        scale = 1.0 / work[p][p]
        top_work = [value * scale for value in work[p]]
        top = vector[p] * scale
        for i in range(KRYLOV):
            if i != p:
                factor = work[i][p]
                work[i] = [w - factor * t for w, t in zip(work[i], top_work)]
                vector[i] = vector[i] - factor * top
        work[p], vector[p] = top_work, top
    for h in range(halves_of(update_ref.shape[1])):
        update_ref[:, half(h)] = combine([c * ref[1, :, half(h)] for c, ref in zip(vector, states)])
        first_ref[:, half(h)] = beta * states[0][1, :, half(h)]


def shape(*dims, dtype=F32):
    return jax.ShapeDtypeStruct(dims, dtype)


def exchange(array, axes):
    return lax.all_to_all(array, axes, split_axis=0, concat_axis=0, tiled=True)


def gather_group(array):
    members = lax.axis_size("blk")

    def partner(held, bits):
        return lax.ppermute(held, "blk", [(i, i ^ bits) for i in range(members)])

    pair = jnp.concatenate([array, partner(array, 1)])
    return [pair] + [partner(pair, bits) for bits in range(2, members, 2)]


def local(stamps, stamp_target, pair_counts, conductance, block_cols, newton_residual):
    members = lax.axis_size("blk")
    devices = lax.axis_size("grp") * members
    rows = conductance.shape[1]
    me = lax.axis_index("grp") * members + lax.axis_index("blk")
    group_rows = rows * members
    place = jnp.stack([me, lax.rem(me + 1, devices), lax.axis_index("grp") * group_rows, group_rows, lax.axis_index("blk") * rows]).astype(I32)

    send, to_next, own, near, pos = pl.pallas_call(
        pack_kernel,
        out_shape=(
            shape(devices, 24, LANES),
            shape(72, LANES),
            shape(72, LANES),
            shape(K, 8, rows, dtype=I32),
            shape(K - K // 2, 8, rows, dtype=I32),
        ),
        in_specs=[pl.BlockSpec(memory_space=pltpu.SMEM)] + [pl.BlockSpec(memory_space=pltpu.VMEM)] * 4,
        out_specs=tuple(pl.BlockSpec(memory_space=pltpu.VMEM) for _ in range(5)),
        compiler_params=pltpu.CompilerParams(vmem_limit_bytes=32 * 2**20),
    )(place, stamps[0], stamp_target[0], pair_counts.reshape(devices, 1), block_cols)
    got = exchange(send, AXES)
    prev = lax.ppermute(to_next, AXES, [(i, (i + 1) % devices) for i in range(devices)])

    width = 2 * LANES * min(devices // 4 + 2, 10)
    jacobian, blocks, inverse, served, z, dots = call(
        assemble_kernel,
        (
            shape(K, 8, 8, rows),
            shape(K, 8, 8, rows),
            shape(8, 8, rows),
            shape(devices, 8, LANES, dtype=I32),
            shape(members, 8, rows),
            shape(8, LANES),
        ),
        got,
        prev,
        own,
        conductance,
        newton_residual,
        scratch=(pltpu.VMEM((64 * K, width), BF16), pltpu.VMEM((rows, width), BF16)),
    )

    states, scalars = [], []
    vector = newton_residual
    for step in range(KRYLOV):
        rhs = step == 0
        z = call(
            functools.partial(first_sweep_kernel, rhs),
            shape(members, 8, rows),
            exchange(z, "blk"),
            vector,
            blocks,
            inverse,
            near,
        )
        z, far, coupled = call(
            functools.partial(second_sweep_kernel, rhs),
            (shape(1, 8, rows), shape(devices, 8, LANES), shape(8, rows)),
            exchange(z, "blk"),
            vector,
            blocks,
            inverse,
            near,
            served,
            dots,
        )
        last = step + 1 == KRYLOV
        parts = gather_group(z)
        state, scalar, vector, z, dots = call(
            functools.partial(operate_kernel, step, len(parts)),
            (
                shape(3, 8, rows),
                shape(2 * step + 1, 8, LANES),
                shape(8, rows),
                shape(members, 8, rows),
                shape(devices, 8, LANES) if last else shape(8, LANES),
            ),
            place,
            *parts,
            exchange(far, AXES),
            coupled,
            vector,
            blocks,
            inverse,
            near,
            pos,
            *states,
            *scalars,
        )
        states.append(state)
        scalars.append(scalar)

    update, first = call(
        finish_kernel, (shape(8, rows), shape(8, rows)), exchange(dots, AXES), *states, *scalars
    )
    return update, jacobian, first


def solution(mesh):
    placed = (
        P(AXES, None, None, None),
        P(AXES, None, None),
        P(AXES, None),
        P(None, AXES),
        P(None, AXES),
        P(None, AXES),
    )
    return jax.shard_map(
        local,
        mesh=mesh,
        in_specs=placed,
        out_specs=(P(None, AXES), P(None, None, None, AXES), P(None, AXES)),
        check_vma=False,
    )
```

```python
import functools

import jax
import jax.numpy as jnp
from jax import lax
from jax.experimental import pallas as pl
from jax.experimental.pallas import tpu as pltpu
from jax.sharding import PartitionSpec as P

K = 16
KRYLOV = 5
LOW = 32
EPS = 1e-06
LANES = 128
AXES = ("grp", "blk")

F32 = jnp.float32
BF16 = jnp.bfloat16
I32 = jnp.int32

LANE_GATHER = lax.GatherDimensionNumbers(
    offset_dims=(),
    collapsed_slice_dims=(1,),
    start_index_map=(1,),
    operand_batching_dims=(0,),
    start_indices_batching_dims=(0,),
)


def lane_gather(source, lanes):
    return lax.gather(
        source,
        lanes[..., None],
        LANE_GATHER,
        slice_sizes=(1, 1),
        mode=lax.GatherScatterMode.PROMISE_IN_BOUNDS,
    )


def call(kernel, out_shape, *args, scratch=(), vmem=32 * 2**20):
    return pl.pallas_call(
        kernel,
        out_shape=out_shape,
        in_specs=[pl.BlockSpec(memory_space=pltpu.SMEM if arg.dtype == I32 and arg.ndim == 1 else pltpu.VMEM) for arg in args],
        out_specs=jax.tree.map(lambda _: pl.BlockSpec(memory_space=pltpu.VMEM), out_shape),
        scratch_shapes=list(scratch),
        compiler_params=pltpu.CompilerParams(vmem_limit_bytes=vmem),
    )(*args)


def iota(shape, axis):
    return lax.broadcasted_iota(I32, shape, axis)


def halves_of(rows):
    return rows // LANES


def half(index):
    return slice(index * LANES, (index + 1) * LANES)


def stack_rows(rows):
    sub = iota((8, LANES), 0)
    out = jnp.zeros((8, LANES), F32)
    for a, value in enumerate(rows):
        out = jnp.where(sub == a, jnp.sum(value, axis=0, keepdims=True), out)
    return out


def apply_inverse(inv_ref, vector):
    out = []
    for h, value in enumerate(vector):
        out.append(stack_rows([inv_ref[a, :, half(h)] * value for a in range(8)]))
    return out


def couple(jac_ref, picks, first, last, acc):
    count = len(acc)
    for k in range(first, last):
        for h in range(count):
            picked = jnp.zeros((8, LANES), F32)
            for index_ref, base, sources in picks:
                index = index_ref[k - base, :, half(h)]
                at, lanes = index >> 7, index & (LANES - 1)
                for s, source in enumerate(sources):
                    picked = jnp.where(at == s, lane_gather(source(), lanes), picked)
            for a in range(8):
                acc[h][a] = acc[h][a] + jac_ref[k, a, :, half(h)] * picked
    return acc


def zero_acc(count):
    return [[jnp.zeros((8, LANES), F32) for _ in range(8)] for _ in range(count)]


def block_sources(ref, first, members, count):
    return [(lambda d=d, h=h: ref[first + d, :, half(h)]) for d in range(members) for h in range(count)]


def store(ref, vector):
    for h, value in enumerate(vector):
        ref[:, half(h)] = value


def spread(ref, vector):
    for d in range(ref.shape[0]):
        for h, value in enumerate(vector):
            ref[d, :, half(h)] = value


def load(ref):
    return [ref[:, half(h)] for h in range(halves_of(ref.shape[1]))]


def dots_block(pairs):
    sub, lane = iota((8, LANES), 0), iota((8, LANES), 1)
    blocks = []
    for start in (0, 8):
        rows = jnp.zeros((8, LANES), F32)
        for i, (left, right) in enumerate(pairs[start : start + 8]):
            total = sum(x * y for x, y in zip(left, right))
            rows = jnp.where(sub == i, jnp.sum(total, axis=0, keepdims=True), rows)
        blocks.append(jnp.sum(rows, axis=1, keepdims=True))
    return jnp.where(lane < 96, blocks[0], blocks[1])


def read_dots(total, count):
    lane = iota((8, LANES), 1)
    out = []
    for at in (64, 96):
        column = jnp.sum(jnp.where(lane == at, total, 0.0), axis=1, keepdims=True)
        column = jnp.broadcast_to(column, (8, LANES))
        out += [jnp.broadcast_to(column[i : i + 1, :], (8, LANES)) for i in range(8)]
    return out[:count]


def pack_kernel(
    place_ref,
    stamps_any,
    target_ref,
    counts_ref,
    cols_ref,
    send_ref,
    next_ref,
    own_ref,
    near_ref,
    pos_ref,
    stamps_ref,
    arrival,
):
    copy = pltpu.make_async_copy(stamps_any, stamps_ref, arrival)
    copy.start()
    devices = stamps_ref.shape[0]
    local_rows = cols_ref.shape[1]
    far_slots = K - K // 2
    per_owner = far_slots * local_rows // devices
    me, nxt = place_ref[0], place_ref[1]
    group_start, group_rows = place_ref[2], place_ref[3]
    lane = iota((1, LANES), 1)

    ids, slots = iota((devices, LANES), 0), iota((devices, LANES), 1)
    counts = jnp.broadcast_to(counts_ref[...], (devices, devices))
    diagonal = iota((devices, devices), 0) == iota((devices, devices), 1)
    counts = jnp.sum(jnp.where(diagonal, counts, 0).astype(F32), axis=1, keepdims=True)
    target = jnp.where(slots.astype(F32) < counts, target_ref[...].astype(F32), -1.0)
    low = jnp.where((ids == me) | (ids == nxt) | (slots >= LOW), -1.0, target)

    owners = iota((devices, LANES), 0)
    before = (iota((LANES, LANES), 0) < iota((LANES, LANES), 1)).astype(BF16)
    running = jnp.zeros((devices, 1), F32)
    asked = jnp.zeros((devices, LANES), F32)
    tiled = iota((LANES, LANES), 0) & (per_owner - 1)
    for k in range(far_slots):
        for h in range(halves_of(local_rows)):
            cols = cols_ref[K // 2 + k : K // 2 + k + 1, half(h)]
            owner = cols // local_rows
            row = cols - owner * local_rows
            hot = (owners == owner).astype(F32)
            ahead = jnp.dot(hot.astype(BF16), before, preferred_element_type=F32) + running
            running = running + jnp.sum(hot, axis=1, keepdims=True)
            rank = jnp.sum(hot * ahead, axis=0, keepdims=True).astype(I32)
            asked += lax.dot_general(
                (hot * row.astype(F32)).astype(BF16),
                (tiled == rank).astype(F32).astype(BF16),
                (((1,), (1,)), ((), ())),
                preferred_element_type=F32,
            )
            near = (cols >= group_start) & (cols < group_start + group_rows)
            pos = jnp.where(near, -1, owner * per_owner + rank)
            pos_ref[k, :, half(h)] = jnp.broadcast_to(pos, (8, LANES))

    copy.wait()
    for ref, at in ((next_ref, nxt), (own_ref, me)):
        ref[0:64, :] = stamps_ref[at]
        row = jnp.sum(jnp.where(ids == at, target, 0.0), axis=0, keepdims=True)
        ref[64:72, :] = jnp.broadcast_to(row, (8, LANES))
    for d in range(devices):
        packed = jnp.zeros((16, LANES), F32)
        for g in range(4):
            piece = stamps_ref[d, 16 * g : 16 * g + 16, :]
            if g:
                piece = pltpu.roll(piece, LOW * g, 1)
            packed = jnp.where(lane // LOW == g, piece, packed)
        send_ref[d, 0:16, :] = packed
        sub = iota((8, LANES), 0)
        send_ref[d, 16:24, :] = jnp.where(sub == 0, low[d : d + 1, :], asked[d : d + 1, :])

    for k in range(K):
        for h in range(halves_of(local_rows)):
            cols = cols_ref[k : k + 1, half(h)]
            near = (cols >= group_start) & (cols < group_start + group_rows)
            near_ref[k, :, half(h)] = jnp.broadcast_to(jnp.where(near, cols - group_start, -1), (8, LANES))


def assemble_kernel(
    recv_ref, prev_ref, own_ref, cond_ref, resid_ref, whole_ref, jac_ref, inv_ref, served_ref, z_ref, left_ref, right_ref
):
    devices = recv_ref.shape[0]
    local_rows = cond_ref.shape[1]
    lane = iota((1, LANES), 1)
    blocks = devices // 4 + 2

    def block(q):
        if q == 0:
            return own_ref[0:64, :], own_ref[64:65, :]
        if q == 1:
            return prev_ref[0:64, :], prev_ref[64:65, :]
        first = 4 * (q - 2)
        rows = []
        for g in range(4):
            out = jnp.zeros((16, LANES), F32)
            for j in range(4):
                piece = recv_ref[first + j, 0:16, :]
                if j != g:
                    piece = pltpu.roll(piece, (LOW * (j - g)) % LANES, 1)
                out = jnp.where(lane // LOW == j, piece, out)
            rows.append(out)
        target = jnp.full((1, LANES), -1.0, F32)
        for j in range(4):
            piece = recv_ref[first + j, 16:17, :]
            if j:
                piece = pltpu.roll(piece, LOW * j, 1)
            target = jnp.where(lane // LOW == j, piece, target)
        return jnp.concatenate(rows, axis=0), target

    most = 10
    for start in range(0, blocks, most):
        stop = min(start + most, blocks)
        width = 2 * (stop - start) * LANES
        values = []
        for q in range(start, stop):
            at = 2 * (q - start) * LANES
            stamp, target = block(q)
            target = target.astype(I32)
            slot, row = target >> (local_rows.bit_length() - 1), target & (local_rows - 1)
            hot = (iota((local_rows, LANES), 0) == row).astype(F32).astype(BF16)
            right_ref[:, at : at + LANES] = hot
            right_ref[:, at + LANES : at + 2 * LANES] = hot
            high = stamp.astype(BF16)
            low = (stamp - high.astype(F32)).astype(BF16)
            values.append((at, slot, high, low))

        for k in range(K):
            for at, slot, high, low in values:
                mask = (slot == k).astype(F32).astype(BF16)
                left_ref[64 * k : 64 * k + 64, at : at + LANES] = high * mask
                left_ref[64 * k : 64 * k + 64, at + LANES : at + 2 * LANES] = low * mask
        total = lax.dot_general(
            left_ref[:, 0:width],
            right_ref[:, 0:width],
            (((1,), (1,)), ((), ())),
            preferred_element_type=F32,
        ).reshape(K, 8, 8, local_rows)
        if start == 0:
            jac_ref[...] = total
        else:
            jac_ref[...] += total
    sub = iota((8, local_rows), 0)
    for a in range(8):
        jac_ref[0, a] = jac_ref[0, a] + jnp.where(sub == a, cond_ref[a : a + 1, :], 0.0)

    whole_ref[...] = jac_ref[...]

    work = [jac_ref[0, a] for a in range(8)]
    inverse = [jnp.where(sub == a, 1.0, 0.0).astype(F32) for a in range(8)]
    for p in range(8):
        scale = 1.0 / work[p][p : p + 1, :]
        top_work, top_inverse = work[p] * scale, inverse[p] * scale
        for a in range(8):
            if a != p:
                factor = work[a][p : p + 1, :]
                work[a] = work[a] - factor * top_work
                inverse[a] = inverse[a] - factor * top_inverse
        work[p], inverse[p] = top_work, top_inverse
    for a in range(8):
        inv_ref[a] = inverse[a]

    for d in range(devices):
        served_ref[d] = jnp.broadcast_to(recv_ref[d, 17:18, :].astype(I32), (8, LANES))
    rhs = [-value for value in load(resid_ref)]
    spread(z_ref, apply_inverse(inv_ref, rhs) + [dots_block([(rhs, rhs)])])


def first_sweep_kernel(rhs, place_ref, group_ref, vector_ref, jac_ref, inv_ref, near_ref, z_ref, dots_ref):
    vector = load(vector_ref)
    if rhs:
        vector = [-value for value in vector]
    members, count = group_ref.shape[0], len(vector)
    sources = block_sources(group_ref, 0, members, count)
    acc = couple(jac_ref, [(near_ref, 0, sources)], 1, K, zero_acc(count))
    spread(z_ref, apply_inverse(inv_ref, [v - stack_rows(c) for v, c in zip(vector, acc)]))
    dots_ref[0] = combine([group_ref[d, :, half(count)] for d in range(members)])
    dots_ref[1] = group_ref[place_ref[0] - place_ref[4], :, half(count)]


def second_sweep_kernel(
    rhs,
    place_ref,
    group_ref,
    vector_ref,
    jac_ref,
    inv_ref,
    near_ref,
    served_ref,
    dots_ref,
    send_ref,
    coupled_ref,
):
    vector = load(vector_ref)
    if rhs:
        vector = [-value for value in vector]
    members, count = group_ref.shape[0], len(vector)
    sources = block_sources(group_ref, 0, members, count)
    acc = couple(jac_ref, [(near_ref, 0, sources)], 1, K, zero_acc(count))
    coupled = [stack_rows(c) for c in acc]
    result = apply_inverse(inv_ref, [v - c for v, c in zip(vector, coupled)])
    store(coupled_ref, coupled)
    dots = dots_ref[1]
    lane = iota((8, LANES), 1)
    for d in range(send_ref.shape[0]):
        index = served_ref[d]
        lanes = index & (LANES - 1)
        picked = lane_gather(result[0], lanes)
        for h in range(1, count):
            picked = jnp.where(index >> 7 == h, lane_gather(result[h], lanes), picked)
        send_ref[d, :, half(0)] = jnp.where(lane < 64, picked, dots)
        for h in range(1, count):
            send_ref[d, :, half(h)] = result[h]
    for d in range(members):
        send_ref[place_ref[4] + d, :, half(0)] = result[0]


def combine(terms):
    return functools.reduce(lambda x, y: x + y, terms)


def orthogonalize(dots, step, gram):
    count = step + 1
    for i in range(count):
        gram[(i, step)] = gram[(step, i)] = dots[i]
    along = dots[count : 2 * count]
    hess = [gram[(i, step)] + along[i] for i in range(count)]
    coefs = [(1.0 - h if i == step else -h) for i, h in enumerate(hess)]
    square = dots[2 * count]
    for i in range(count):
        inner = combine([coefs[l] * gram[(i, l)] for l in range(count)])
        square = square + coefs[i] * (2.0 * along[i] + inner)
    length = jnp.sqrt(jnp.maximum(square, 0.0) + EPS)
    return hess, length, coefs


def read_scalars(refs):
    gram, hess, lengths = {}, {}, []
    beta = refs[0][0]
    for step, ref in enumerate(refs[1:]):
        count = step + 1
        for i in range(count):
            gram[(i, step)] = gram[(step, i)] = ref[i]
            hess[(i, step)] = ref[count + i]
        hess[(count, step)] = ref[2 * count]
    return beta, gram, hess


def operate_kernel(step, members, place_ref, recv_ref, group_dots_ref, coupled_ref, vector_ref, *refs):
    jac_ref, inv_ref, near_ref, pos_ref = refs[:4]
    refs = refs[4:]
    states, scalar_refs = refs[:step], refs[step : 2 * step]
    state_ref, scalars_ref, vector_out_ref, z_ref = refs[2 * step :]
    devices = recv_ref.shape[0]
    rows = coupled_ref.shape[1]
    count = halves_of(rows)
    per_owner = (K - K // 2) * rows // devices
    each = LANES // per_owner
    lane = iota((8, LANES), 1)
    me, first = place_ref[0], place_ref[4]

    arrived = []
    total = group_dots_ref[0]
    for q in range(devices // each):
        out = recv_ref[q * each, :, half(0)]
        for j in range(each):
            d = q * each + j
            piece = recv_ref[d, :, half(0)]
            outside = (d < first) | (d >= first + members)
            total = total + jnp.where(outside, piece, 0.0)
            if j:
                out = jnp.where(lane // per_owner == j, pltpu.roll(piece, j * per_owner, 1), out)
        arrived.append(out)

    near = (near_ref, 0, block_sources(recv_ref, first, members, count))
    acc = couple(jac_ref, [near], 1, K // 2, zero_acc(count))
    acc = couple(jac_ref, [near, (pos_ref, K // 2, [(lambda v=v: v) for v in arrived])], K // 2, K, acc)
    image = [stack_rows(c) - n for c, n in zip(acc, load(coupled_ref))]
    search = [recv_ref[me, :, half(h)] for h in range(count)]
    vector = load(vector_ref)

    if step == 0:
        vector = [-value for value in vector]
        length = jnp.sqrt(read_dots(total, 1)[0] + EPS)
        scalars_ref[0] = length
        coefs = []
    else:
        _, gram, _ = read_scalars(scalar_refs)
        dots = read_dots(total, 2 * step + 1)
        hess, length, coefs = orthogonalize(dots, step - 1, gram)
        for i in range(step):
            scalars_ref[i] = gram[(i, step - 1)]
            scalars_ref[step + i] = hess[i]
        scalars_ref[2 * step] = length
    scale = 1.0 / length

    def recombine(part, fresh):
        out = []
        for h, value in enumerate(fresh):
            for c, ref in zip(coefs, states):
                value = value + c * ref[part, :, half(h)]
            value = value * scale
            state_ref[part, :, half(h)] = value
            out.append(value)
        return out

    basis = [[ref[0, :, half(h)] for h in range(count)] for ref in states]
    basis.append(recombine(0, vector))
    recombine(1, search)
    image = recombine(2, image)
    store(vector_out_ref, image)
    pairs = [(b, basis[-1]) for b in basis] + [(b, image) for b in basis] + [(image, image)]
    block = dots_block(pairs)
    spread(z_ref, apply_inverse(inv_ref, image) + [block] if step + 1 < KRYLOV else [block])


def finish_kernel(dots_ref, *refs):
    states, scalar_refs = refs[:KRYLOV], refs[KRYLOV : 2 * KRYLOV]
    update_ref, first_ref = refs[2 * KRYLOV :]
    total = combine([dots_ref[d] for d in range(dots_ref.shape[0])])
    beta, gram, hess = read_scalars(scalar_refs)
    last, length, _ = orthogonalize(read_dots(total, 2 * KRYLOV + 1), KRYLOV - 1, gram)
    for i, value in enumerate(last):
        hess[(i, KRYLOV - 1)] = value
    hess[(KRYLOV, KRYLOV - 1)] = length

    work = [
        [combine([hess[(l, i)] * hess[(l, j)] for l in range(min(i, j) + 2)]) for j in range(KRYLOV)]
        for i in range(KRYLOV)
    ]
    vector = [beta * hess[(0, j)] for j in range(KRYLOV)]
    for p in range(KRYLOV):
        scale = 1.0 / work[p][p]
        top_work = [value * scale for value in work[p]]
        top = vector[p] * scale
        for i in range(KRYLOV):
            if i != p:
                factor = work[i][p]
                work[i] = [w - factor * t for w, t in zip(work[i], top_work)]
                vector[i] = vector[i] - factor * top
        work[p], vector[p] = top_work, top
    for h in range(halves_of(update_ref.shape[1])):
        update_ref[:, half(h)] = combine([c * ref[1, :, half(h)] for c, ref in zip(vector, states)])
        first_ref[:, half(h)] = beta * states[0][1, :, half(h)]


def shape(*dims, dtype=F32):
    return jax.ShapeDtypeStruct(dims, dtype)


def exchange(array, axes):
    return lax.all_to_all(array, axes, split_axis=0, concat_axis=0, tiled=True)


def local(stamps, stamp_target, pair_counts, conductance, block_cols, newton_residual):
    members = lax.axis_size("blk")
    devices = lax.axis_size("grp") * members
    rows = conductance.shape[1]
    me = lax.axis_index("grp") * members + lax.axis_index("blk")
    group = lax.axis_index("grp") * members
    place = jnp.stack([me, lax.rem(me + 1, devices), group * rows, members * rows, group]).astype(I32)

    send, to_next, own, near, pos = pl.pallas_call(
        pack_kernel,
        out_shape=(
            shape(devices, 24, LANES),
            shape(72, LANES),
            shape(72, LANES),
            shape(K, 8, rows, dtype=I32),
            shape(K - K // 2, 8, rows, dtype=I32),
        ),
        in_specs=[pl.BlockSpec(memory_space=space) for space in (pltpu.SMEM, pl.ANY) + 3 * (pltpu.VMEM,)],
        out_specs=tuple(pl.BlockSpec(memory_space=pltpu.VMEM) for _ in range(5)),
        scratch_shapes=[pltpu.VMEM(stamps.shape[1:], F32), pltpu.SemaphoreType.DMA],
        compiler_params=pltpu.CompilerParams(vmem_limit_bytes=32 * 2**20),
    )(place, stamps[0], stamp_target[0], pair_counts, block_cols)
    got = exchange(send, AXES)
    prev = lax.ppermute(to_next, AXES, [(i, (i + 1) % devices) for i in range(devices)])

    width = 2 * LANES * min(devices // 4 + 2, 10)
    jacobian, blocks, inverse, served, z = call(
        assemble_kernel,
        (
            shape(K, 8, 8, rows),
            shape(K, 8, 8, rows),
            shape(8, 8, rows),
            shape(devices, 8, LANES, dtype=I32),
            shape(members, 8, rows + LANES),
        ),
        got,
        prev,
        own,
        conductance,
        newton_residual,
        scratch=(pltpu.VMEM((64 * K, width), BF16), pltpu.VMEM((rows, width), BF16)),
    )

    states, scalars = [], []
    vector = newton_residual
    for step in range(KRYLOV):
        rhs = step == 0
        z, group_dots = call(
            functools.partial(first_sweep_kernel, rhs),
            (shape(members, 8, rows), shape(2, 8, LANES)),
            place,
            exchange(z, "blk"),
            vector,
            blocks,
            inverse,
            near,
        )
        send, coupled = call(
            functools.partial(second_sweep_kernel, rhs),
            (shape(devices, 8, rows), shape(8, rows)),
            place,
            exchange(z, "blk"),
            vector,
            blocks,
            inverse,
            near,
            served,
            group_dots,
        )
        last = step + 1 == KRYLOV
        state, scalar, vector, z = call(
            functools.partial(operate_kernel, step, members),
            (
                shape(3, 8, rows),
                shape(2 * step + 1, 8, LANES),
                shape(8, rows),
                shape(devices, 8, LANES) if last else shape(members, 8, rows + LANES),
            ),
            place,
            exchange(send, AXES),
            group_dots,
            coupled,
            vector,
            blocks,
            inverse,
            near,
            pos,
            *states,
            *scalars,
        )
        states.append(state)
        scalars.append(scalar)

    update, first = call(finish_kernel, (shape(8, rows), shape(8, rows)), exchange(z, AXES), *states, *scalars)
    return update, jacobian, first


def solution(mesh):
    placed = (
        P(AXES, None, None, None),
        P(AXES, None, None),
        P(AXES, None),
        P(None, AXES),
        P(None, AXES),
        P(None, AXES),
    )
    return jax.shard_map(
        local,
        mesh=mesh,
        in_specs=placed,
        out_specs=(P(None, AXES), P(None, None, None, AXES), P(None, AXES)),
        check_vma=False,
    )
```

```python
import functools

import jax
import jax.numpy as jnp
from jax import lax
from jax.experimental import pallas as pl
from jax.experimental.pallas import tpu as pltpu
from jax.sharding import PartitionSpec as P

K = 16
KRYLOV = 5
LOW = 32
EPS = 1e-06
LANES = 128
AXES = ("grp", "blk")

F32 = jnp.float32
BF16 = jnp.bfloat16
I32 = jnp.int32

LANE_GATHER = lax.GatherDimensionNumbers(
    offset_dims=(),
    collapsed_slice_dims=(1,),
    start_index_map=(1,),
    operand_batching_dims=(0,),
    start_indices_batching_dims=(0,),
)


def lane_gather(source, lanes):
    return lax.gather(
        source,
        lanes[..., None],
        LANE_GATHER,
        slice_sizes=(1, 1),
        mode=lax.GatherScatterMode.PROMISE_IN_BOUNDS,
    )


def my_place(members):
    first = lax.axis_index("grp") * members
    return first + lax.axis_index("blk"), first


def call(kernel, out_shape, *args, scratch=(), vmem=32 * 2**20):
    return pl.pallas_call(
        kernel,
        out_shape=out_shape,
        in_specs=[pl.BlockSpec(memory_space=pltpu.VMEM)] * len(args),
        out_specs=jax.tree.map(lambda _: pl.BlockSpec(memory_space=pltpu.VMEM), out_shape),
        scratch_shapes=list(scratch),
        compiler_params=pltpu.CompilerParams(vmem_limit_bytes=vmem),
    )(*args)


def iota(shape, axis):
    return lax.broadcasted_iota(I32, shape, axis)


def halves_of(rows):
    return rows // LANES


def half(index):
    return slice(index * LANES, (index + 1) * LANES)


def stack_rows(rows):
    sub = iota((8, LANES), 0)
    out = jnp.zeros((8, LANES), F32)
    for a, value in enumerate(rows):
        out = jnp.where(sub == a, jnp.sum(value, axis=0, keepdims=True), out)
    return out


def apply_inverse(inv_ref, vector):
    out = []
    for h, value in enumerate(vector):
        out.append(stack_rows([inv_ref[a, :, half(h)] * value for a in range(8)]))
    return out


def couple(jac_ref, picks, first, last, acc):
    count = len(acc)
    for k in range(first, last):
        for h in range(count):
            picked = jnp.zeros((8, LANES), F32)
            for index_ref, base, sources in picks:
                index = index_ref[k - base, :, half(h)]
                at, lanes = index >> 7, index & (LANES - 1)
                for s, source in enumerate(sources):
                    picked = jnp.where(at == s, lane_gather(source(), lanes), picked)
            for a in range(8):
                acc[h][a] = acc[h][a] + jac_ref[k, a, :, half(h)] * picked
    return acc


def zero_acc(count):
    return [[jnp.zeros((8, LANES), F32) for _ in range(8)] for _ in range(count)]


def block_sources(ref, first, members, count):
    return [(lambda d=d, h=h: ref[first + d, :, half(h)]) for d in range(members) for h in range(count)]


def store(ref, vector):
    for h, value in enumerate(vector):
        ref[:, half(h)] = value


def spread(ref, vector):
    for d in range(ref.shape[0]):
        for h, value in enumerate(vector):
            ref[d, :, half(h)] = value


def load(ref):
    return [ref[:, half(h)] for h in range(halves_of(ref.shape[1]))]


def dots_block(pairs):
    sub, lane = iota((8, LANES), 0), iota((8, LANES), 1)
    blocks = []
    for start in (0, 8):
        rows = jnp.zeros((8, LANES), F32)
        for i, (left, right) in enumerate(pairs[start : start + 8]):
            total = sum(x * y for x, y in zip(left, right))
            rows = jnp.where(sub == i, jnp.sum(total, axis=0, keepdims=True), rows)
        blocks.append(jnp.sum(rows, axis=1, keepdims=True))
    return jnp.where(lane < 96, blocks[0], blocks[1])


def read_dots(total, count):
    lane = iota((8, LANES), 1)
    out = []
    for at in (64, 96):
        column = jnp.sum(jnp.where(lane == at, total, 0.0), axis=1, keepdims=True)
        column = jnp.broadcast_to(column, (8, LANES))
        out += [jnp.broadcast_to(column[i : i + 1, :], (8, LANES)) for i in range(8)]
    return out[:count]


def pack_kernel(
    members,
    stamps_any,
    target_ref,
    counts_ref,
    cols_ref,
    send_ref,
    next_ref,
    own_ref,
    near_ref,
    pos_ref,
    stamps_ref,
    arrival,
):
    copy = pltpu.make_async_copy(stamps_any, stamps_ref, arrival)
    copy.start()
    devices = stamps_ref.shape[0]
    local_rows = cols_ref.shape[1]
    far_slots = K - K // 2
    per_owner = far_slots * local_rows // devices
    me, first = my_place(members)
    nxt = jnp.where(me + 1 == devices, 0, me + 1)
    group_start, group_rows = first * local_rows, members * local_rows
    lane = iota((1, LANES), 1)

    ids, slots = iota((devices, LANES), 0), iota((devices, LANES), 1)
    counts = jnp.broadcast_to(counts_ref[...], (devices, devices))
    diagonal = iota((devices, devices), 0) == iota((devices, devices), 1)
    counts = jnp.sum(jnp.where(diagonal, counts, 0).astype(F32), axis=1, keepdims=True)
    target = jnp.where(slots.astype(F32) < counts, target_ref[...].astype(F32), -1.0)
    low = jnp.where((ids == me) | (ids == nxt) | (slots >= LOW), -1.0, target)

    owners = iota((devices, LANES), 0)
    before = (iota((LANES, LANES), 0) < iota((LANES, LANES), 1)).astype(BF16)
    running = jnp.zeros((devices, 1), F32)
    asked = jnp.zeros((devices, LANES), F32)
    tiled = iota((LANES, LANES), 0) - 64
    for k in range(far_slots):
        for h in range(halves_of(local_rows)):
            cols = cols_ref[K // 2 + k : K // 2 + k + 1, half(h)]
            owner = cols // local_rows
            row = cols - owner * local_rows
            hot = (owners == owner).astype(F32)
            ahead = jnp.dot(hot.astype(BF16), before, preferred_element_type=F32) + running
            running = running + jnp.sum(hot, axis=1, keepdims=True)
            rank = jnp.sum(hot * ahead, axis=0, keepdims=True).astype(I32)
            asked += lax.dot_general(
                (hot * row.astype(F32)).astype(BF16),
                (tiled == rank).astype(F32).astype(BF16),
                (((1,), (1,)), ((), ())),
                preferred_element_type=F32,
            )
            near = (cols >= group_start) & (cols < group_start + group_rows)
            pos = jnp.where(near, -1, owner * per_owner + rank)
            pos_ref[k, :, half(h)] = jnp.broadcast_to(pos, (8, LANES))

    copy.wait()
    for ref, at in ((next_ref, nxt), (own_ref, me)):
        ref[0:64, :] = stamps_ref[at]
        row = jnp.sum(jnp.where(ids == at, target, 0.0), axis=0, keepdims=True)
        ref[64:72, :] = jnp.broadcast_to(row, (8, LANES))
    for d in range(devices):
        packed = jnp.zeros((16, LANES), F32)
        for g in range(4):
            piece = stamps_ref[d, 16 * g : 16 * g + 16, :]
            if g:
                piece = pltpu.roll(piece, LOW * g, 1)
            packed = jnp.where(lane // LOW == g, piece, packed)
        for i in range(8):
            send_ref[d, i] = packed[2 * i : 2 * i + 2, :]
        ints = jnp.where(lane < 64, low[d : d + 1, :], asked[d : d + 1, :])
        send_ref[d, 8] = jnp.broadcast_to(ints, (2, LANES))

    for k in range(K):
        for h in range(halves_of(local_rows)):
            cols = cols_ref[k : k + 1, half(h)]
            near = (cols >= group_start) & (cols < group_start + group_rows)
            near_ref[k, :, half(h)] = jnp.broadcast_to(jnp.where(near, cols - group_start, -1), (8, LANES))


def assemble_kernel(
    recv_ref, prev_ref, own_ref, cond_ref, resid_ref, whole_ref, jac_ref, inv_ref, served_ref, z_ref, left_ref, right_ref
):
    devices = recv_ref.shape[0]
    local_rows = cond_ref.shape[1]
    lane = iota((1, LANES), 1)
    blocks = devices // 4 + 2

    def stamp_rows(d):
        return jnp.concatenate([recv_ref[d, i] for i in range(8)], axis=0)

    def block(q):
        if q == 0:
            return own_ref[0:64, :], own_ref[64:65, :]
        if q == 1:
            return prev_ref[0:64, :], prev_ref[64:65, :]
        first = 4 * (q - 2)
        rows = []
        pieces = [stamp_rows(first + j) for j in range(4)]
        for g in range(4):
            out = jnp.zeros((16, LANES), F32)
            for j in range(4):
                piece = pieces[j]
                if j != g:
                    piece = pltpu.roll(piece, (LOW * (j - g)) % LANES, 1)
                out = jnp.where(lane // LOW == j, piece, out)
            rows.append(out)
        target = jnp.full((1, LANES), -1.0, F32)
        for j in range(4):
            piece = recv_ref[first + j, 8, 0:1, :]
            if j:
                piece = pltpu.roll(piece, LOW * j, 1)
            target = jnp.where(lane // LOW == j, piece, target)
        return jnp.concatenate(rows, axis=0), target

    most = 10
    for start in range(0, blocks, most):
        stop = min(start + most, blocks)
        width = 2 * (stop - start) * LANES
        values = []
        for q in range(start, stop):
            at = 2 * (q - start) * LANES
            stamp, target = block(q)
            target = target.astype(I32)
            slot, row = target >> (local_rows.bit_length() - 1), target & (local_rows - 1)
            hot = (iota((local_rows, LANES), 0) == row).astype(F32).astype(BF16)
            right_ref[:, at : at + LANES] = hot
            right_ref[:, at + LANES : at + 2 * LANES] = hot
            high = stamp.astype(BF16)
            low = (stamp - high.astype(F32)).astype(BF16)
            values.append((at, slot, high, low))

        for k in range(K):
            for at, slot, high, low in values:
                mask = (slot == k).astype(F32).astype(BF16)
                left_ref[64 * k : 64 * k + 64, at : at + LANES] = high * mask
                left_ref[64 * k : 64 * k + 64, at + LANES : at + 2 * LANES] = low * mask
        total = lax.dot_general(
            left_ref[:, 0:width],
            right_ref[:, 0:width],
            (((1,), (1,)), ((), ())),
            preferred_element_type=F32,
        ).reshape(K, 8, 8, local_rows)
        if start == 0:
            jac_ref[...] = total
        else:
            jac_ref[...] += total
    sub = iota((8, local_rows), 0)
    for a in range(8):
        jac_ref[0, a] = jac_ref[0, a] + jnp.where(sub == a, cond_ref[a : a + 1, :], 0.0)

    whole_ref[...] = jac_ref[...]

    work = [jac_ref[0, a] for a in range(8)]
    inverse = [jnp.where(sub == a, 1.0, 0.0).astype(F32) for a in range(8)]
    for p in range(8):
        scale = 1.0 / work[p][p : p + 1, :]
        top_work, top_inverse = work[p] * scale, inverse[p] * scale
        for a in range(8):
            if a != p:
                factor = work[a][p : p + 1, :]
                work[a] = work[a] - factor * top_work
                inverse[a] = inverse[a] - factor * top_inverse
        work[p], inverse[p] = top_work, top_inverse
    for a in range(8):
        inv_ref[a] = inverse[a]

    for d in range(devices):
        asked = pltpu.roll(recv_ref[d, 8, 0:1, :], 64, 1).astype(I32)
        served_ref[d] = jnp.broadcast_to(asked, (8, LANES))
    rhs = [-value for value in load(resid_ref)]
    spread(z_ref, apply_inverse(inv_ref, rhs) + [dots_block([(rhs, rhs)])])


def first_sweep_kernel(rhs, group_ref, vector_ref, jac_ref, inv_ref, near_ref, z_ref, dots_ref):
    vector = load(vector_ref)
    if rhs:
        vector = [-value for value in vector]
    members, count = group_ref.shape[0], len(vector)
    sources = block_sources(group_ref, 0, members, count)
    acc = couple(jac_ref, [(near_ref, 0, sources)], 1, K, zero_acc(count))
    spread(z_ref, apply_inverse(inv_ref, [v - stack_rows(c) for v, c in zip(vector, acc)]))
    dots_ref[0] = combine([group_ref[d, :, half(count)] for d in range(members)])
    dots_ref[1] = group_ref[lax.axis_index("blk"), :, half(count)]


def second_sweep_kernel(
    rhs,
    group_ref,
    vector_ref,
    jac_ref,
    inv_ref,
    near_ref,
    served_ref,
    dots_ref,
    send_ref,
    coupled_ref,
):
    vector = load(vector_ref)
    if rhs:
        vector = [-value for value in vector]
    members, count = group_ref.shape[0], len(vector)
    sources = block_sources(group_ref, 0, members, count)
    acc = couple(jac_ref, [(near_ref, 0, sources)], 1, K, zero_acc(count))
    coupled = [stack_rows(c) for c in acc]
    result = apply_inverse(inv_ref, [v - c for v, c in zip(vector, coupled)])
    store(coupled_ref, coupled)
    dots = dots_ref[1]
    lane = iota((8, LANES), 1)
    for d in range(send_ref.shape[0]):
        index = served_ref[d]
        lanes = index & (LANES - 1)
        picked = lane_gather(result[0], lanes)
        for h in range(1, count):
            picked = jnp.where(index >> 7 == h, lane_gather(result[h], lanes), picked)
        send_ref[d, :, half(0)] = jnp.where(lane < 64, picked, dots)
        for h in range(1, count):
            send_ref[d, :, half(h)] = result[h]
    _, first = my_place(members)
    for d in range(members):
        send_ref[first + d, :, half(0)] = result[0]


def combine(terms):
    return functools.reduce(lambda x, y: x + y, terms)


def orthogonalize(dots, step, gram):
    count = step + 1
    for i in range(count):
        gram[(i, step)] = gram[(step, i)] = dots[i]
    along = dots[count : 2 * count]
    hess = [gram[(i, step)] + along[i] for i in range(count)]
    coefs = [(1.0 - h if i == step else -h) for i, h in enumerate(hess)]
    square = dots[2 * count]
    for i in range(count):
        inner = combine([coefs[l] * gram[(i, l)] for l in range(count)])
        square = square + coefs[i] * (2.0 * along[i] + inner)
    length = jnp.sqrt(jnp.maximum(square, 0.0) + EPS)
    return hess, length, coefs


def read_scalars(refs):
    gram, hess, lengths = {}, {}, []
    beta = refs[0][0]
    for step, ref in enumerate(refs[1:]):
        count = step + 1
        for i in range(count):
            gram[(i, step)] = gram[(step, i)] = ref[i]
            hess[(i, step)] = ref[count + i]
        hess[(count, step)] = ref[2 * count]
    return beta, gram, hess


def operate_kernel(step, members, recv_ref, group_dots_ref, coupled_ref, vector_ref, *refs):
    jac_ref, inv_ref, near_ref, pos_ref = refs[:4]
    refs = refs[4:]
    states, scalar_refs = refs[:step], refs[step : 2 * step]
    state_ref, scalars_ref, vector_out_ref, z_ref = refs[2 * step :]
    devices = recv_ref.shape[0]
    rows = coupled_ref.shape[1]
    count = halves_of(rows)
    per_owner = (K - K // 2) * rows // devices
    each = LANES // per_owner
    lane = iota((8, LANES), 1)
    me, first = my_place(members)

    arrived = []
    total = group_dots_ref[0]
    for q in range(devices // each):
        out = recv_ref[q * each, :, half(0)]
        for j in range(each):
            d = q * each + j
            piece = recv_ref[d, :, half(0)]
            outside = (d < first) | (d >= first + members)
            total = total + jnp.where(outside, piece, 0.0)
            if j:
                out = jnp.where(lane // per_owner == j, pltpu.roll(piece, j * per_owner, 1), out)
        arrived.append(out)

    near = (near_ref, 0, block_sources(recv_ref, first, members, count))
    acc = couple(jac_ref, [near], 1, K // 2, zero_acc(count))
    acc = couple(jac_ref, [near, (pos_ref, K // 2, [(lambda v=v: v) for v in arrived])], K // 2, K, acc)
    image = [stack_rows(c) - n for c, n in zip(acc, load(coupled_ref))]
    search = [recv_ref[me, :, half(h)] for h in range(count)]
    vector = load(vector_ref)

    if step == 0:
        vector = [-value for value in vector]
        length = jnp.sqrt(read_dots(total, 1)[0] + EPS)
        scalars_ref[0] = length
        coefs = []
    else:
        _, gram, _ = read_scalars(scalar_refs)
        dots = read_dots(total, 2 * step + 1)
        hess, length, coefs = orthogonalize(dots, step - 1, gram)
        for i in range(step):
            scalars_ref[i] = gram[(i, step - 1)]
            scalars_ref[step + i] = hess[i]
        scalars_ref[2 * step] = length
    scale = 1.0 / length

    def recombine(part, fresh):
        out = []
        for h, value in enumerate(fresh):
            for c, ref in zip(coefs, states):
                value = value + c * ref[part, :, half(h)]
            value = value * scale
            state_ref[part, :, half(h)] = value
            out.append(value)
        return out

    basis = [[ref[0, :, half(h)] for h in range(count)] for ref in states]
    basis.append(recombine(0, vector))
    recombine(1, search)
    image = recombine(2, image)
    store(vector_out_ref, image)
    pairs = [(b, basis[-1]) for b in basis] + [(b, image) for b in basis] + [(image, image)]
    block = dots_block(pairs)
    spread(z_ref, apply_inverse(inv_ref, image) + [block] if step + 1 < KRYLOV else [block])


def finish_kernel(dots_ref, *refs):
    states, scalar_refs = refs[:KRYLOV], refs[KRYLOV : 2 * KRYLOV]
    update_ref, first_ref = refs[2 * KRYLOV :]
    total = combine([dots_ref[d] for d in range(dots_ref.shape[0])])
    beta, gram, hess = read_scalars(scalar_refs)
    last, length, _ = orthogonalize(read_dots(total, 2 * KRYLOV + 1), KRYLOV - 1, gram)
    for i, value in enumerate(last):
        hess[(i, KRYLOV - 1)] = value
    hess[(KRYLOV, KRYLOV - 1)] = length

    work = [
        [combine([hess[(l, i)] * hess[(l, j)] for l in range(min(i, j) + 2)]) for j in range(KRYLOV)]
        for i in range(KRYLOV)
    ]
    vector = [beta * hess[(0, j)] for j in range(KRYLOV)]
    for p in range(KRYLOV):
        scale = 1.0 / work[p][p]
        top_work = [value * scale for value in work[p]]
        top = vector[p] * scale
        for i in range(KRYLOV):
            if i != p:
                factor = work[i][p]
                work[i] = [w - factor * t for w, t in zip(work[i], top_work)]
                vector[i] = vector[i] - factor * top
        work[p], vector[p] = top_work, top
    for h in range(halves_of(update_ref.shape[1])):
        update_ref[:, half(h)] = combine([c * ref[1, :, half(h)] for c, ref in zip(vector, states)])
        first_ref[:, half(h)] = beta * states[0][1, :, half(h)]


def shape(*dims, dtype=F32):
    return jax.ShapeDtypeStruct(dims, dtype)


def exchange(array, axes):
    return lax.all_to_all(array, axes, split_axis=0, concat_axis=0, tiled=True)


def local(stamps, stamp_target, pair_counts, conductance, block_cols, newton_residual):
    members = lax.axis_size("blk")
    devices = lax.axis_size("grp") * members
    rows = conductance.shape[1]

    send, to_next, own, near, pos = pl.pallas_call(
        functools.partial(pack_kernel, members),
        out_shape=(
            shape(devices, 9, 2, LANES),
            shape(72, LANES),
            shape(72, LANES),
            shape(K, 8, rows, dtype=I32),
            shape(K - K // 2, 8, rows, dtype=I32),
        ),
        in_specs=[pl.BlockSpec(memory_space=space) for space in (pl.ANY,) + 3 * (pltpu.VMEM,)],
        out_specs=tuple(pl.BlockSpec(memory_space=pltpu.VMEM) for _ in range(5)),
        scratch_shapes=[pltpu.VMEM(stamps.shape[1:], F32), pltpu.SemaphoreType.DMA],
        compiler_params=pltpu.CompilerParams(vmem_limit_bytes=60 * 2**20),
    )(stamps[0], stamp_target[0], pair_counts, block_cols)
    got = exchange(send, AXES)
    prev = lax.ppermute(to_next, AXES, [(i, (i + 1) % devices) for i in range(devices)])

    width = 2 * LANES * min(devices // 4 + 2, 10)
    jacobian, blocks, inverse, served, z = call(
        assemble_kernel,
        (
            shape(K, 8, 8, rows),
            shape(K, 8, 8, rows),
            shape(8, 8, rows),
            shape(devices, 8, LANES, dtype=I32),
            shape(members, 8, rows + LANES),
        ),
        got,
        prev,
        own,
        conductance,
        newton_residual,
        scratch=(pltpu.VMEM((64 * K, width), BF16), pltpu.VMEM((rows, width), BF16)),
    )

    states, scalars = [], []
    vector = newton_residual
    for step in range(KRYLOV):
        rhs = step == 0
        z, group_dots = call(
            functools.partial(first_sweep_kernel, rhs),
            (shape(members, 8, rows), shape(2, 8, LANES)),
            exchange(z, "blk"),
            vector,
            blocks,
            inverse,
            near,
        )
        send, coupled = call(
            functools.partial(second_sweep_kernel, rhs),
            (shape(devices, 8, rows), shape(8, rows)),
            exchange(z, "blk"),
            vector,
            blocks,
            inverse,
            near,
            served,
            group_dots,
        )
        last = step + 1 == KRYLOV
        state, scalar, vector, z = call(
            functools.partial(operate_kernel, step, members),
            (
                shape(3, 8, rows),
                shape(2 * step + 1, 8, LANES),
                shape(8, rows),
                shape(devices, 8, LANES) if last else shape(members, 8, rows + LANES),
            ),
            exchange(send, AXES),
            group_dots,
            coupled,
            vector,
            blocks,
            inverse,
            near,
            pos,
            *states,
            *scalars,
        )
        states.append(state)
        scalars.append(scalar)

    update, first = call(finish_kernel, (shape(8, rows), shape(8, rows)), exchange(z, AXES), *states, *scalars)
    return update, jacobian, first


def solution(mesh):
    placed = (
        P(AXES, None, None, None),
        P(AXES, None, None),
        P(AXES, None),
        P(None, AXES),
        P(None, AXES),
        P(None, AXES),
    )
    return jax.shard_map(
        local,
        mesh=mesh,
        in_specs=placed,
        out_specs=(P(None, AXES), P(None, None, None, AXES), P(None, AXES)),
        check_vma=False,
    )
```

```python
import functools

import jax
import jax.numpy as jnp
from jax import lax
from jax.experimental import pallas as pl
from jax.experimental.pallas import tpu as pltpu
from jax.sharding import PartitionSpec as P

K = 16
KRYLOV = 5
LOW = 32
EPS = 1e-06
LANES = 128
AXES = ("grp", "blk")

F32 = jnp.float32
BF16 = jnp.bfloat16
I32 = jnp.int32

LANE_GATHER = lax.GatherDimensionNumbers(
    offset_dims=(),
    collapsed_slice_dims=(1,),
    start_index_map=(1,),
    operand_batching_dims=(0,),
    start_indices_batching_dims=(0,),
)


def lane_gather(source, lanes):
    return lax.gather(
        source,
        lanes[..., None],
        LANE_GATHER,
        slice_sizes=(1, 1),
        mode=lax.GatherScatterMode.PROMISE_IN_BOUNDS,
    )


def my_place(members):
    first = lax.axis_index("grp") * members
    return first + lax.axis_index("blk"), first


def call(kernel, out_shape, *args, scratch=(), vmem=32 * 2**20):
    return pl.pallas_call(
        kernel,
        out_shape=out_shape,
        in_specs=[pl.BlockSpec(memory_space=pltpu.VMEM)] * len(args),
        out_specs=jax.tree.map(lambda _: pl.BlockSpec(memory_space=pltpu.VMEM), out_shape),
        scratch_shapes=list(scratch),
        compiler_params=pltpu.CompilerParams(vmem_limit_bytes=vmem),
    )(*args)


def iota(shape, axis):
    return lax.broadcasted_iota(I32, shape, axis)


def halves_of(rows):
    return rows // LANES


def half(index):
    return slice(index * LANES, (index + 1) * LANES)


def stack_rows(rows):
    sub = iota((8, LANES), 0)
    out = jnp.zeros((8, LANES), F32)
    for a, value in enumerate(rows):
        out = jnp.where(sub == a, jnp.sum(value, axis=0, keepdims=True), out)
    return out


def apply_inverse(inv_ref, vector):
    out = []
    for h, value in enumerate(vector):
        out.append(stack_rows([inv_ref[a, :, half(h)] * value for a in range(8)]))
    return out


def couple(jac_ref, picks, first, last, acc):
    count = len(acc)
    for k in range(first, last):
        for h in range(count):
            picked = jnp.zeros((8, LANES), F32)
            for index_ref, base, sources in picks:
                index = index_ref[k - base, :, half(h)]
                at, lanes = index >> 7, index & (LANES - 1)
                for s, source in enumerate(sources):
                    picked = jnp.where(at == s, lane_gather(source(), lanes), picked)
            for a in range(8):
                acc[h][a] = acc[h][a] + jac_ref[k, a, :, half(h)] * picked
    return acc


def zero_acc(count):
    return [[jnp.zeros((8, LANES), F32) for _ in range(8)] for _ in range(count)]


def block_sources(ref, first, members, count):
    return [(lambda d=d, h=h: ref[first + d, :, half(h)]) for d in range(members) for h in range(count)]


def store(ref, vector):
    for h, value in enumerate(vector):
        ref[:, half(h)] = value


def spread(ref, vector):
    for d in range(ref.shape[0]):
        for h, value in enumerate(vector):
            ref[d, :, half(h)] = value


def load(ref):
    return [ref[:, half(h)] for h in range(halves_of(ref.shape[1]))]


def dots_block(pairs):
    sub, lane = iota((8, LANES), 0), iota((8, LANES), 1)
    blocks = []
    for start in (0, 8):
        rows = jnp.zeros((8, LANES), F32)
        for i, (left, right) in enumerate(pairs[start : start + 8]):
            total = sum(x * y for x, y in zip(left, right))
            rows = jnp.where(sub == i, jnp.sum(total, axis=0, keepdims=True), rows)
        blocks.append(jnp.sum(rows, axis=1, keepdims=True))
    return jnp.where(lane < 96, blocks[0], blocks[1])


def read_dots(total, count):
    lane = iota((8, LANES), 1)
    out = []
    for at in (64, 96):
        column = jnp.sum(jnp.where(lane == at, total, 0.0), axis=1, keepdims=True)
        column = jnp.broadcast_to(column, (8, LANES))
        out += [jnp.broadcast_to(column[i : i + 1, :], (8, LANES)) for i in range(8)]
    return out[:count]


def live_targets(target_ref, counts_ref):
    devices = target_ref.shape[0]
    counts = jnp.broadcast_to(counts_ref[...], (devices, devices))
    diagonal = iota((devices, devices), 0) == iota((devices, devices), 1)
    counts = jnp.sum(jnp.where(diagonal, counts, 0).astype(F32), axis=1, keepdims=True)
    return jnp.where(iota((devices, LANES), 1).astype(F32) < counts, target_ref[...].astype(F32), -1.0)


def next_kernel(members, stamps_any, target_ref, counts_ref, next_ref, arrival):
    devices = stamps_any.shape[0]
    me, _ = my_place(members)
    nxt = jnp.where(me + 1 == devices, 0, me + 1)
    copy = pltpu.make_async_copy(stamps_any.at[nxt], next_ref.at[0:64], arrival)
    copy.start()
    target = live_targets(target_ref, counts_ref)
    row = jnp.sum(jnp.where(iota((devices, LANES), 0) == nxt, target, 0.0), axis=0, keepdims=True)
    next_ref[64:72, :] = jnp.broadcast_to(row, (8, LANES))
    copy.wait()


def pack_kernel(
    members,
    stamps_any,
    target_ref,
    counts_ref,
    cols_ref,
    send_ref,
    own_ref,
    near_ref,
    pos_ref,
    stamps_ref,
    arrival,
):
    copy = pltpu.make_async_copy(stamps_any, stamps_ref, arrival)
    copy.start()
    devices = stamps_ref.shape[0]
    local_rows = cols_ref.shape[1]
    far_slots = K - K // 2
    per_owner = far_slots * local_rows // devices
    me, first = my_place(members)
    nxt = jnp.where(me + 1 == devices, 0, me + 1)
    group_start, group_rows = first * local_rows, members * local_rows
    lane = iota((1, LANES), 1)

    ids, slots = iota((devices, LANES), 0), iota((devices, LANES), 1)
    target = live_targets(target_ref, counts_ref)
    low = jnp.where((ids == me) | (ids == nxt) | (slots >= LOW), -1.0, target)

    owners = iota((devices, LANES), 0)
    before = (iota((LANES, LANES), 0) < iota((LANES, LANES), 1)).astype(BF16)
    running = jnp.zeros((devices, 1), F32)
    asked = jnp.zeros((devices, LANES), F32)
    tiled = iota((LANES, LANES), 0) - 64
    for k in range(far_slots):
        for h in range(halves_of(local_rows)):
            cols = cols_ref[K // 2 + k : K // 2 + k + 1, half(h)]
            owner = cols // local_rows
            row = cols - owner * local_rows
            hot = (owners == owner).astype(F32)
            ahead = jnp.dot(hot.astype(BF16), before, preferred_element_type=F32) + running
            running = running + jnp.sum(hot, axis=1, keepdims=True)
            rank = jnp.sum(hot * ahead, axis=0, keepdims=True).astype(I32)
            asked += lax.dot_general(
                (hot * row.astype(F32)).astype(BF16),
                (tiled == rank).astype(F32).astype(BF16),
                (((1,), (1,)), ((), ())),
                preferred_element_type=F32,
            )
            near = (cols >= group_start) & (cols < group_start + group_rows)
            pos = jnp.where(near, -1, owner * per_owner + rank)
            pos_ref[k, :, half(h)] = jnp.broadcast_to(pos, (8, LANES))

    copy.wait()
    own_ref[0:64, :] = stamps_ref[me]
    row = jnp.sum(jnp.where(ids == me, target, 0.0), axis=0, keepdims=True)
    own_ref[64:72, :] = jnp.broadcast_to(row, (8, LANES))
    for d in range(devices):
        packed = jnp.zeros((16, LANES), F32)
        for g in range(4):
            piece = stamps_ref[d, 16 * g : 16 * g + 16, :]
            if g:
                piece = pltpu.roll(piece, LOW * g, 1)
            packed = jnp.where(lane // LOW == g, piece, packed)
        for i in range(8):
            send_ref[d, i] = packed[2 * i : 2 * i + 2, :]
        ints = jnp.where(lane < 64, low[d : d + 1, :], asked[d : d + 1, :])
        send_ref[d, 8] = jnp.broadcast_to(ints, (2, LANES))

    for k in range(K):
        for h in range(halves_of(local_rows)):
            cols = cols_ref[k : k + 1, half(h)]
            near = (cols >= group_start) & (cols < group_start + group_rows)
            near_ref[k, :, half(h)] = jnp.broadcast_to(jnp.where(near, cols - group_start, -1), (8, LANES))


def assemble_kernel(
    recv_ref, prev_ref, own_ref, cond_ref, resid_ref, whole_ref, jac_ref, inv_ref, served_ref, z_ref, left_ref, right_ref
):
    devices = recv_ref.shape[0]
    local_rows = cond_ref.shape[1]
    lane = iota((1, LANES), 1)
    blocks = devices // 4 + 2

    def stamp_rows(d):
        return jnp.concatenate([recv_ref[d, i] for i in range(8)], axis=0)

    def block(q):
        if q == 0:
            return own_ref[0:64, :], own_ref[64:65, :]
        if q == 1:
            return prev_ref[0:64, :], prev_ref[64:65, :]
        first = 4 * (q - 2)
        rows = []
        pieces = [stamp_rows(first + j) for j in range(4)]
        for g in range(4):
            out = jnp.zeros((16, LANES), F32)
            for j in range(4):
                piece = pieces[j]
                if j != g:
                    piece = pltpu.roll(piece, (LOW * (j - g)) % LANES, 1)
                out = jnp.where(lane // LOW == j, piece, out)
            rows.append(out)
        target = jnp.full((1, LANES), -1.0, F32)
        for j in range(4):
            piece = recv_ref[first + j, 8, 0:1, :]
            if j:
                piece = pltpu.roll(piece, LOW * j, 1)
            target = jnp.where(lane // LOW == j, piece, target)
        return jnp.concatenate(rows, axis=0), target

    most = 10
    for start in range(0, blocks, most):
        stop = min(start + most, blocks)
        width = 2 * (stop - start) * LANES
        values = []
        for q in range(start, stop):
            at = 2 * (q - start) * LANES
            stamp, target = block(q)
            target = target.astype(I32)
            slot, row = target >> (local_rows.bit_length() - 1), target & (local_rows - 1)
            hot = (iota((local_rows, LANES), 0) == row).astype(F32).astype(BF16)
            right_ref[:, at : at + LANES] = hot
            right_ref[:, at + LANES : at + 2 * LANES] = hot
            high = stamp.astype(BF16)
            low = (stamp - high.astype(F32)).astype(BF16)
            values.append((at, slot, high, low))

        for k in range(K):
            for at, slot, high, low in values:
                mask = (slot == k).astype(F32).astype(BF16)
                left_ref[64 * k : 64 * k + 64, at : at + LANES] = high * mask
                left_ref[64 * k : 64 * k + 64, at + LANES : at + 2 * LANES] = low * mask
        total = lax.dot_general(
            left_ref[:, 0:width],
            right_ref[:, 0:width],
            (((1,), (1,)), ((), ())),
            preferred_element_type=F32,
        ).reshape(K, 8, 8, local_rows)
        if start == 0:
            jac_ref[...] = total
        else:
            jac_ref[...] += total
    sub = iota((8, local_rows), 0)
    for a in range(8):
        jac_ref[0, a] = jac_ref[0, a] + jnp.where(sub == a, cond_ref[a : a + 1, :], 0.0)

    whole_ref[...] = jac_ref[...]

    work = [jac_ref[0, a] for a in range(8)]
    inverse = [jnp.where(sub == a, 1.0, 0.0).astype(F32) for a in range(8)]
    for p in range(8):
        scale = 1.0 / work[p][p : p + 1, :]
        top_work, top_inverse = work[p] * scale, inverse[p] * scale
        for a in range(8):
            if a != p:
                factor = work[a][p : p + 1, :]
                work[a] = work[a] - factor * top_work
                inverse[a] = inverse[a] - factor * top_inverse
        work[p], inverse[p] = top_work, top_inverse
    for a in range(8):
        inv_ref[a] = inverse[a]

    for d in range(devices):
        asked = pltpu.roll(recv_ref[d, 8, 0:1, :], 64, 1).astype(I32)
        served_ref[d] = jnp.broadcast_to(asked, (8, LANES))
    rhs = [-value for value in load(resid_ref)]
    spread(z_ref, apply_inverse(inv_ref, rhs) + [dots_block([(rhs, rhs)])])


def first_sweep_kernel(rhs, group_ref, vector_ref, jac_ref, inv_ref, near_ref, z_ref, dots_ref):
    vector = load(vector_ref)
    if rhs:
        vector = [-value for value in vector]
    members, count = group_ref.shape[0], len(vector)
    sources = block_sources(group_ref, 0, members, count)
    acc = couple(jac_ref, [(near_ref, 0, sources)], 1, K, zero_acc(count))
    spread(z_ref, apply_inverse(inv_ref, [v - stack_rows(c) for v, c in zip(vector, acc)]))
    dots_ref[0] = combine([group_ref[d, :, half(count)] for d in range(members)])
    dots_ref[1] = group_ref[lax.axis_index("blk"), :, half(count)]


def second_sweep_kernel(
    rhs,
    group_ref,
    vector_ref,
    jac_ref,
    inv_ref,
    near_ref,
    served_ref,
    dots_ref,
    send_ref,
    coupled_ref,
):
    vector = load(vector_ref)
    if rhs:
        vector = [-value for value in vector]
    members, count = group_ref.shape[0], len(vector)
    sources = block_sources(group_ref, 0, members, count)
    acc = couple(jac_ref, [(near_ref, 0, sources)], 1, K, zero_acc(count))
    coupled = [stack_rows(c) for c in acc]
    result = apply_inverse(inv_ref, [v - c for v, c in zip(vector, coupled)])
    store(coupled_ref, coupled)
    dots = dots_ref[1]
    lane = iota((8, LANES), 1)
    for d in range(send_ref.shape[0]):
        index = served_ref[d]
        lanes = index & (LANES - 1)
        picked = lane_gather(result[0], lanes)
        for h in range(1, count):
            picked = jnp.where(index >> 7 == h, lane_gather(result[h], lanes), picked)
        send_ref[d, :, half(0)] = jnp.where(lane < 64, picked, dots)
        for h in range(1, count):
            send_ref[d, :, half(h)] = result[h]
    _, first = my_place(members)
    for d in range(members):
        send_ref[first + d, :, half(0)] = result[0]


def combine(terms):
    return functools.reduce(lambda x, y: x + y, terms)


def orthogonalize(dots, step, gram):
    count = step + 1
    for i in range(count):
        gram[(i, step)] = gram[(step, i)] = dots[i]
    along = dots[count : 2 * count]
    hess = [gram[(i, step)] + along[i] for i in range(count)]
    coefs = [(1.0 - h if i == step else -h) for i, h in enumerate(hess)]
    square = dots[2 * count]
    for i in range(count):
        inner = combine([coefs[l] * gram[(i, l)] for l in range(count)])
        square = square + coefs[i] * (2.0 * along[i] + inner)
    length = jnp.sqrt(jnp.maximum(square, 0.0) + EPS)
    return hess, length, coefs


def read_scalars(refs):
    gram, hess, lengths = {}, {}, []
    beta = refs[0][0]
    for step, ref in enumerate(refs[1:]):
        count = step + 1
        for i in range(count):
            gram[(i, step)] = gram[(step, i)] = ref[i]
            hess[(i, step)] = ref[count + i]
        hess[(count, step)] = ref[2 * count]
    return beta, gram, hess


def operate_kernel(step, members, recv_ref, group_dots_ref, coupled_ref, vector_ref, *refs):
    jac_ref, inv_ref, near_ref, pos_ref = refs[:4]
    refs = refs[4:]
    states, scalar_refs = refs[:step], refs[step : 2 * step]
    state_ref, scalars_ref, vector_out_ref, z_ref = refs[2 * step :]
    devices = recv_ref.shape[0]
    rows = coupled_ref.shape[1]
    count = halves_of(rows)
    per_owner = (K - K // 2) * rows // devices
    each = LANES // per_owner
    lane = iota((8, LANES), 1)
    me, first = my_place(members)

    arrived = []
    total = group_dots_ref[0]
    for q in range(devices // each):
        out = recv_ref[q * each, :, half(0)]
        for j in range(each):
            d = q * each + j
            piece = recv_ref[d, :, half(0)]
            outside = (d < first) | (d >= first + members)
            total = total + jnp.where(outside, piece, 0.0)
            if j:
                out = jnp.where(lane // per_owner == j, pltpu.roll(piece, j * per_owner, 1), out)
        arrived.append(out)

    near = (near_ref, 0, block_sources(recv_ref, first, members, count))
    acc = couple(jac_ref, [near], 1, K // 2, zero_acc(count))
    acc = couple(jac_ref, [near, (pos_ref, K // 2, [(lambda v=v: v) for v in arrived])], K // 2, K, acc)
    image = [stack_rows(c) - n for c, n in zip(acc, load(coupled_ref))]
    search = [recv_ref[me, :, half(h)] for h in range(count)]
    vector = load(vector_ref)

    if step == 0:
        vector = [-value for value in vector]
        length = jnp.sqrt(read_dots(total, 1)[0] + EPS)
        scalars_ref[0] = length
        coefs = []
    else:
        _, gram, _ = read_scalars(scalar_refs)
        dots = read_dots(total, 2 * step + 1)
        hess, length, coefs = orthogonalize(dots, step - 1, gram)
        for i in range(step):
            scalars_ref[i] = gram[(i, step - 1)]
            scalars_ref[step + i] = hess[i]
        scalars_ref[2 * step] = length
    scale = 1.0 / length

    def recombine(part, fresh):
        out = []
        for h, value in enumerate(fresh):
            for c, ref in zip(coefs, states):
                value = value + c * ref[part, :, half(h)]
            value = value * scale
            state_ref[part, :, half(h)] = value
            out.append(value)
        return out

    basis = [[ref[0, :, half(h)] for h in range(count)] for ref in states]
    basis.append(recombine(0, vector))
    recombine(1, search)
    image = recombine(2, image)
    store(vector_out_ref, image)
    pairs = [(b, basis[-1]) for b in basis] + [(b, image) for b in basis] + [(image, image)]
    block = dots_block(pairs)
    spread(z_ref, apply_inverse(inv_ref, image) + [block] if step + 1 < KRYLOV else [block])


def finish_kernel(dots_ref, *refs):
    states, scalar_refs = refs[:KRYLOV], refs[KRYLOV : 2 * KRYLOV]
    update_ref, first_ref = refs[2 * KRYLOV :]
    total = combine([dots_ref[d] for d in range(dots_ref.shape[0])])
    beta, gram, hess = read_scalars(scalar_refs)
    last, length, _ = orthogonalize(read_dots(total, 2 * KRYLOV + 1), KRYLOV - 1, gram)
    for i, value in enumerate(last):
        hess[(i, KRYLOV - 1)] = value
    hess[(KRYLOV, KRYLOV - 1)] = length

    work = [
        [combine([hess[(l, i)] * hess[(l, j)] for l in range(min(i, j) + 2)]) for j in range(KRYLOV)]
        for i in range(KRYLOV)
    ]
    vector = [beta * hess[(0, j)] for j in range(KRYLOV)]
    for p in range(KRYLOV):
        scale = 1.0 / work[p][p]
        top_work = [value * scale for value in work[p]]
        top = vector[p] * scale
        for i in range(KRYLOV):
            if i != p:
                factor = work[i][p]
                work[i] = [w - factor * t for w, t in zip(work[i], top_work)]
                vector[i] = vector[i] - factor * top
        work[p], vector[p] = top_work, top
    for h in range(halves_of(update_ref.shape[1])):
        update_ref[:, half(h)] = combine([c * ref[1, :, half(h)] for c, ref in zip(vector, states)])
        first_ref[:, half(h)] = beta * states[0][1, :, half(h)]


def shape(*dims, dtype=F32):
    return jax.ShapeDtypeStruct(dims, dtype)


def exchange(array, axes):
    return lax.all_to_all(array, axes, split_axis=0, concat_axis=0, tiled=True)


def local(stamps, stamp_target, pair_counts, conductance, block_cols, newton_residual):
    members = lax.axis_size("blk")
    devices = lax.axis_size("grp") * members
    rows = conductance.shape[1]

    to_next = pl.pallas_call(
        functools.partial(next_kernel, members),
        out_shape=shape(72, LANES),
        in_specs=[pl.BlockSpec(memory_space=space) for space in (pl.ANY,) + 2 * (pltpu.VMEM,)],
        out_specs=pl.BlockSpec(memory_space=pltpu.VMEM),
        scratch_shapes=[pltpu.SemaphoreType.DMA],
        compiler_params=pltpu.CompilerParams(vmem_limit_bytes=60 * 2**20),
    )(stamps[0], stamp_target[0], pair_counts)
    prev = lax.ppermute(to_next, AXES, [(i, (i + 1) % devices) for i in range(devices)])
    send, own, near, pos = pl.pallas_call(
        functools.partial(pack_kernel, members),
        out_shape=(
            shape(devices, 9, 2, LANES),
            shape(72, LANES),
            shape(K, 8, rows, dtype=I32),
            shape(K - K // 2, 8, rows, dtype=I32),
        ),
        in_specs=[pl.BlockSpec(memory_space=space) for space in (pl.ANY,) + 3 * (pltpu.VMEM,)],
        out_specs=tuple(pl.BlockSpec(memory_space=pltpu.VMEM) for _ in range(4)),
        scratch_shapes=[pltpu.VMEM(stamps.shape[1:], F32), pltpu.SemaphoreType.DMA],
        compiler_params=pltpu.CompilerParams(vmem_limit_bytes=60 * 2**20),
    )(stamps[0], stamp_target[0], pair_counts, block_cols)
    send, prev = lax.optimization_barrier((send, prev))
    got = exchange(send, AXES)

    width = 2 * LANES * min(devices // 4 + 2, 10)
    jacobian, blocks, inverse, served, z = call(
        assemble_kernel,
        (
            shape(K, 8, 8, rows),
            shape(K, 8, 8, rows),
            shape(8, 8, rows),
            shape(devices, 8, LANES, dtype=I32),
            shape(members, 8, rows + LANES),
        ),
        got,
        prev,
        own,
        conductance,
        newton_residual,
        scratch=(pltpu.VMEM((64 * K, width), BF16), pltpu.VMEM((rows, width), BF16)),
    )

    states, scalars = [], []
    vector = newton_residual
    for step in range(KRYLOV):
        rhs = step == 0
        z, group_dots = call(
            functools.partial(first_sweep_kernel, rhs),
            (shape(members, 8, rows), shape(2, 8, LANES)),
            exchange(z, "blk"),
            vector,
            blocks,
            inverse,
            near,
        )
        send, coupled = call(
            functools.partial(second_sweep_kernel, rhs),
            (shape(devices, 8, rows), shape(8, rows)),
            exchange(z, "blk"),
            vector,
            blocks,
            inverse,
            near,
            served,
            group_dots,
        )
        last = step + 1 == KRYLOV
        state, scalar, vector, z = call(
            functools.partial(operate_kernel, step, members),
            (
                shape(3, 8, rows),
                shape(2 * step + 1, 8, LANES),
                shape(8, rows),
                shape(devices, 8, LANES) if last else shape(members, 8, rows + LANES),
            ),
            exchange(send, AXES),
            group_dots,
            coupled,
            vector,
            blocks,
            inverse,
            near,
            pos,
            *states,
            *scalars,
        )
        states.append(state)
        scalars.append(scalar)

    update, first = call(finish_kernel, (shape(8, rows), shape(8, rows)), exchange(z, AXES), *states, *scalars)
    return update, jacobian, first


def solution(mesh):
    placed = (
        P(AXES, None, None, None),
        P(AXES, None, None),
        P(AXES, None),
        P(None, AXES),
        P(None, AXES),
        P(None, AXES),
    )
    return jax.shard_map(
        local,
        mesh=mesh,
        in_specs=placed,
        out_specs=(P(None, AXES), P(None, None, None, AXES), P(None, AXES)),
        check_vma=False,
    )
```

```python
import functools

import jax
import jax.numpy as jnp
from jax import lax
from jax.experimental import pallas as pl
from jax.experimental.pallas import tpu as pltpu
from jax.sharding import PartitionSpec as P

K = 16
KRYLOV = 5
LOW = 32
EPS = 1e-06
LANES = 128
AXES = ("grp", "blk")

F32 = jnp.float32
BF16 = jnp.bfloat16
I32 = jnp.int32

LANE_GATHER = lax.GatherDimensionNumbers(
    offset_dims=(),
    collapsed_slice_dims=(1,),
    start_index_map=(1,),
    operand_batching_dims=(0,),
    start_indices_batching_dims=(0,),
)


def lane_gather(source, lanes):
    return lax.gather(
        source,
        lanes[..., None],
        LANE_GATHER,
        slice_sizes=(1, 1),
        mode=lax.GatherScatterMode.PROMISE_IN_BOUNDS,
    )


def my_place(members):
    first = lax.axis_index("grp") * members
    return first + lax.axis_index("blk"), first


def call(kernel, out_shape, *args, scratch=(), vmem=32 * 2**20):
    return pl.pallas_call(
        kernel,
        out_shape=out_shape,
        in_specs=[pl.BlockSpec(memory_space=pltpu.VMEM)] * len(args),
        out_specs=jax.tree.map(lambda _: pl.BlockSpec(memory_space=pltpu.VMEM), out_shape),
        scratch_shapes=list(scratch),
        compiler_params=pltpu.CompilerParams(vmem_limit_bytes=vmem),
    )(*args)


def iota(shape, axis):
    return lax.broadcasted_iota(I32, shape, axis)


def halves_of(rows):
    return rows // LANES


def half(index):
    return slice(index * LANES, (index + 1) * LANES)


def stack_rows(rows):
    sub = iota((8, LANES), 0)
    out = jnp.zeros((8, LANES), F32)
    for a, value in enumerate(rows):
        out = jnp.where(sub == a, jnp.sum(value, axis=0, keepdims=True), out)
    return out


def apply_inverse(inv_ref, vector):
    out = []
    for h, value in enumerate(vector):
        out.append(stack_rows([inv_ref[a, :, half(h)] * value for a in range(8)]))
    return out


def couple(jac_ref, picks, first, last, acc):
    count = len(acc)
    for k in range(first, last):
        for h in range(count):
            picked = jnp.zeros((8, LANES), F32)
            for index_ref, base, sources in picks:
                index = index_ref[k - base, :, half(h)]
                at, lanes = index >> 7, index & (LANES - 1)
                for s, source in enumerate(sources):
                    picked = jnp.where(at == s, lane_gather(source(), lanes), picked)
            for a in range(8):
                acc[h][a] = acc[h][a] + jac_ref[k, a, :, half(h)] * picked
    return acc


def zero_acc(count):
    return [[jnp.zeros((8, LANES), F32) for _ in range(8)] for _ in range(count)]


def block_sources(ref, first, members, count):
    return [(lambda d=d, h=h: ref[first + d, :, half(h)]) for d in range(members) for h in range(count)]


def store(ref, vector):
    for h, value in enumerate(vector):
        ref[:, half(h)] = value


def spread(ref, vector):
    for d in range(ref.shape[0]):
        for h, value in enumerate(vector):
            ref[d, :, half(h)] = value


def load(ref):
    return [ref[:, half(h)] for h in range(halves_of(ref.shape[1]))]


def dots_block(pairs):
    sub, lane = iota((8, LANES), 0), iota((8, LANES), 1)
    blocks = []
    for start in (0, 8):
        rows = jnp.zeros((8, LANES), F32)
        for i, (left, right) in enumerate(pairs[start : start + 8]):
            total = sum(x * y for x, y in zip(left, right))
            rows = jnp.where(sub == i, jnp.sum(total, axis=0, keepdims=True), rows)
        blocks.append(jnp.sum(rows, axis=1, keepdims=True))
    return jnp.where(lane < 96, blocks[0], blocks[1])


def read_dots(total, count):
    lane = iota((8, LANES), 1)
    out = []
    for at in (64, 96):
        column = jnp.sum(jnp.where(lane == at, total, 0.0), axis=1, keepdims=True)
        column = jnp.broadcast_to(column, (8, LANES))
        out += [jnp.broadcast_to(column[i : i + 1, :], (8, LANES)) for i in range(8)]
    return out[:count]


def pack_kernel(
    members,
    stamps_any,
    target_ref,
    counts_ref,
    cols_ref,
    send_ref,
    next_ref,
    own_ref,
    near_ref,
    pos_ref,
    stamps_ref,
    arrival,
):
    copy = pltpu.make_async_copy(stamps_any, stamps_ref, arrival)
    copy.start()
    devices = stamps_ref.shape[0]
    local_rows = cols_ref.shape[1]
    far_slots = K - K // 2
    per_owner = far_slots * local_rows // devices
    me, first = my_place(members)
    nxt = jnp.where(me + 1 == devices, 0, me + 1)
    group_start, group_rows = first * local_rows, members * local_rows
    lane = iota((1, LANES), 1)

    ids, slots = iota((devices, LANES), 0), iota((devices, LANES), 1)
    counts = jnp.broadcast_to(counts_ref[...], (devices, devices))
    diagonal = iota((devices, devices), 0) == iota((devices, devices), 1)
    counts = jnp.sum(jnp.where(diagonal, counts, 0).astype(F32), axis=1, keepdims=True)
    target = jnp.where(slots.astype(F32) < counts, target_ref[...].astype(F32), -1.0)
    low = jnp.where((ids == me) | (ids == nxt) | (slots >= LOW), -1.0, target)

    owners = iota((devices, LANES), 0)
    before = (iota((LANES, LANES), 0) < iota((LANES, LANES), 1)).astype(BF16)
    running = jnp.zeros((devices, 1), F32)
    asked = jnp.zeros((devices, LANES), F32)
    tiled = iota((LANES, LANES), 0) - 64
    for k in range(far_slots):
        for h in range(halves_of(local_rows)):
            cols = cols_ref[K // 2 + k : K // 2 + k + 1, half(h)]
            owner = cols // local_rows
            row = cols - owner * local_rows
            hot = (owners == owner).astype(F32)
            ahead = jnp.dot(hot.astype(BF16), before, preferred_element_type=F32) + running
            running = running + jnp.sum(hot, axis=1, keepdims=True)
            rank = jnp.sum(hot * ahead, axis=0, keepdims=True).astype(I32)
            asked += lax.dot_general(
                (hot * row.astype(F32)).astype(BF16),
                (tiled == rank).astype(F32).astype(BF16),
                (((1,), (1,)), ((), ())),
                preferred_element_type=F32,
            )
            near = (cols >= group_start) & (cols < group_start + group_rows)
            pos = jnp.where(near, -1, owner * per_owner + rank)
            pos_ref[k, :, half(h)] = jnp.broadcast_to(pos, (8, LANES))

    copy.wait()
    for ref, at in ((next_ref, nxt), (own_ref, me)):
        ref[0:64, :] = stamps_ref[at]
        row = jnp.sum(jnp.where(ids == at, target, 0.0), axis=0, keepdims=True)
        ref[64:72, :] = jnp.broadcast_to(row, (8, LANES))
    for d in range(devices):
        packed = jnp.zeros((16, LANES), F32)
        for g in range(4):
            piece = stamps_ref[d, 16 * g : 16 * g + 16, :]
            if g:
                piece = pltpu.roll(piece, LOW * g, 1)
            packed = jnp.where(lane // LOW == g, piece, packed)
        for i in range(8):
            send_ref[d, i] = packed[2 * i : 2 * i + 2, :]
        ints = jnp.where(lane < 64, low[d : d + 1, :], asked[d : d + 1, :])
        send_ref[d, 8] = jnp.broadcast_to(ints, (2, LANES))

    for k in range(K):
        for h in range(halves_of(local_rows)):
            cols = cols_ref[k : k + 1, half(h)]
            near = (cols >= group_start) & (cols < group_start + group_rows)
            near_ref[k, :, half(h)] = jnp.broadcast_to(jnp.where(near, cols - group_start, -1), (8, LANES))


def assemble_kernel(
    recv_ref, prev_ref, own_ref, cond_ref, resid_ref, whole_ref, jac_ref, inv_ref, served_ref, z_ref, dots_ref, left_ref, right_ref
):
    devices = recv_ref.shape[0]
    local_rows = cond_ref.shape[1]
    lane = iota((1, LANES), 1)
    blocks = devices // 4 + 2

    def stamp_rows(d):
        return jnp.concatenate([recv_ref[d, i] for i in range(8)], axis=0)

    def block(q):
        if q == 0:
            return own_ref[0:64, :], own_ref[64:65, :]
        if q == 1:
            return prev_ref[0:64, :], prev_ref[64:65, :]
        first = 4 * (q - 2)
        rows = []
        pieces = [stamp_rows(first + j) for j in range(4)]
        for g in range(4):
            out = jnp.zeros((16, LANES), F32)
            for j in range(4):
                piece = pieces[j]
                if j != g:
                    piece = pltpu.roll(piece, (LOW * (j - g)) % LANES, 1)
                out = jnp.where(lane // LOW == j, piece, out)
            rows.append(out)
        target = jnp.full((1, LANES), -1.0, F32)
        for j in range(4):
            piece = recv_ref[first + j, 8, 0:1, :]
            if j:
                piece = pltpu.roll(piece, LOW * j, 1)
            target = jnp.where(lane // LOW == j, piece, target)
        return jnp.concatenate(rows, axis=0), target

    most = 10
    for start in range(0, blocks, most):
        stop = min(start + most, blocks)
        width = 2 * (stop - start) * LANES
        values = []
        for q in range(start, stop):
            at = 2 * (q - start) * LANES
            stamp, target = block(q)
            target = target.astype(I32)
            slot, row = target >> (local_rows.bit_length() - 1), target & (local_rows - 1)
            hot = (iota((local_rows, LANES), 0) == row).astype(F32).astype(BF16)
            right_ref[:, at : at + LANES] = hot
            right_ref[:, at + LANES : at + 2 * LANES] = hot
            high = stamp.astype(BF16)
            low = (stamp - high.astype(F32)).astype(BF16)
            values.append((at, slot, high, low))

        for k in range(K):
            for at, slot, high, low in values:
                mask = (slot == k).astype(F32).astype(BF16)
                left_ref[64 * k : 64 * k + 64, at : at + LANES] = high * mask
                left_ref[64 * k : 64 * k + 64, at + LANES : at + 2 * LANES] = low * mask
        total = lax.dot_general(
            left_ref[:, 0:width],
            right_ref[:, 0:width],
            (((1,), (1,)), ((), ())),
            preferred_element_type=F32,
        ).reshape(K, 8, 8, local_rows)
        if start == 0:
            jac_ref[...] = total
        else:
            jac_ref[...] += total
    sub = iota((8, local_rows), 0)
    for a in range(8):
        jac_ref[0, a] = jac_ref[0, a] + jnp.where(sub == a, cond_ref[a : a + 1, :], 0.0)

    whole_ref[...] = jac_ref[...]

    work = [jac_ref[0, a] for a in range(8)]
    inverse = [jnp.where(sub == a, 1.0, 0.0).astype(F32) for a in range(8)]
    for p in range(8):
        scale = 1.0 / work[p][p : p + 1, :]
        top_work, top_inverse = work[p] * scale, inverse[p] * scale
        for a in range(8):
            if a != p:
                factor = work[a][p : p + 1, :]
                work[a] = work[a] - factor * top_work
                inverse[a] = inverse[a] - factor * top_inverse
        work[p], inverse[p] = top_work, top_inverse
    for a in range(8):
        inv_ref[a] = inverse[a]

    for d in range(devices):
        asked = pltpu.roll(recv_ref[d, 8, 0:1, :], 64, 1).astype(I32)
        served_ref[d] = jnp.broadcast_to(asked, (8, LANES))
    rhs = [-value for value in load(resid_ref)]
    spread(z_ref, apply_inverse(inv_ref, rhs))
    dots_ref[...] = dots_block([(rhs, rhs)])


def first_sweep_kernel(rhs, group_ref, vector_ref, jac_ref, inv_ref, near_ref, dots_ref, z_ref):
    vector = load(vector_ref)
    if rhs:
        vector = [-value for value in vector]
    members, count = group_ref.shape[0], len(vector)
    sources = block_sources(group_ref, 0, members, count)
    acc = couple(jac_ref, [(near_ref, 0, sources)], 1, K, zero_acc(count))
    result = apply_inverse(inv_ref, [v - stack_rows(c) for v, c in zip(vector, acc)])
    spread(z_ref, result + [dots_ref[...]])


def second_sweep_kernel(
    rhs,
    group_ref,
    vector_ref,
    jac_ref,
    inv_ref,
    near_ref,
    served_ref,
    dots_ref,
    send_ref,
    coupled_ref,
    own_ref,
    group_dots_ref,
):
    vector = load(vector_ref)
    if rhs:
        vector = [-value for value in vector]
    members, count = group_ref.shape[0], len(vector)
    sources = block_sources(group_ref, 0, members, count)
    acc = couple(jac_ref, [(near_ref, 0, sources)], 1, K, zero_acc(count))
    coupled = [stack_rows(c) for c in acc]
    result = apply_inverse(inv_ref, [v - c for v, c in zip(vector, coupled)])
    store(coupled_ref, coupled)
    store(own_ref, result)
    group_dots_ref[...] = combine([group_ref[d, :, half(count)] for d in range(members)])
    dots = dots_ref[...]
    lane = iota((8, LANES), 1)
    for d in range(send_ref.shape[0]):
        index = served_ref[d]
        lanes = index & (LANES - 1)
        picked = lane_gather(result[0], lanes)
        for h in range(1, count):
            picked = jnp.where(index >> 7 == h, lane_gather(result[h], lanes), picked)
        send_ref[d, :, half(0)] = jnp.where(lane < 64, picked, dots)
        for h in range(1, count):
            send_ref[d, :, half(h)] = result[h]
    _, first = my_place(members)
    for d in range(members):
        send_ref[first + d, :, half(0)] = result[0]


def combine(terms):
    return functools.reduce(lambda x, y: x + y, terms)


def orthogonalize(dots, step, gram):
    count = step + 1
    for i in range(count):
        gram[(i, step)] = gram[(step, i)] = dots[i]
    along = dots[count : 2 * count]
    hess = [gram[(i, step)] + along[i] for i in range(count)]
    coefs = [(1.0 - h if i == step else -h) for i, h in enumerate(hess)]
    square = dots[2 * count]
    for i in range(count):
        inner = combine([coefs[l] * gram[(i, l)] for l in range(count)])
        square = square + coefs[i] * (2.0 * along[i] + inner)
    length = jnp.sqrt(jnp.maximum(square, 0.0) + EPS)
    return hess, length, coefs


def read_scalars(refs):
    gram, hess, lengths = {}, {}, []
    beta = refs[0][0]
    for step, ref in enumerate(refs[1:]):
        count = step + 1
        for i in range(count):
            gram[(i, step)] = gram[(step, i)] = ref[i]
            hess[(i, step)] = ref[count + i]
        hess[(count, step)] = ref[2 * count]
    return beta, gram, hess


def operate_kernel(step, members, recv_ref, group_dots_ref, coupled_ref, *refs):
    jac_ref, inv_ref, near_ref, pos_ref = refs[:4]
    refs = refs[4:]
    images, scalar_refs = refs[:step], refs[step : 2 * step]
    image_ref, scalars_ref = refs[2 * step : 2 * step + 2]
    devices = recv_ref.shape[0]
    rows = coupled_ref.shape[1]
    count = halves_of(rows)
    per_owner = (K - K // 2) * rows // devices
    each = LANES // per_owner
    lane = iota((8, LANES), 1)
    _, first = my_place(members)

    arrived = []
    total = group_dots_ref[...]
    for q in range(devices // each):
        out = recv_ref[q * each, :, half(0)]
        for j in range(each):
            d = q * each + j
            piece = recv_ref[d, :, half(0)]
            outside = (d < first) | (d >= first + members)
            total = total + jnp.where(outside, piece, 0.0)
            if j:
                out = jnp.where(lane // per_owner == j, pltpu.roll(piece, j * per_owner, 1), out)
        arrived.append(out)

    near = (near_ref, 0, block_sources(recv_ref, first, members, count))
    acc = couple(jac_ref, [near], 1, K // 2, zero_acc(count))
    acc = couple(jac_ref, [near, (pos_ref, K // 2, [(lambda v=v: v) for v in arrived])], K // 2, K, acc)
    image = [stack_rows(c) - n for c, n in zip(acc, load(coupled_ref))]
    if step == 0:
        length = jnp.sqrt(read_dots(total, 1)[0] + EPS)
        scalars_ref[0] = length
        coefs = []
    else:
        _, gram, _ = read_scalars(scalar_refs)
        dots = read_dots(total, 2 * step + 1)
        hess, length, coefs = orthogonalize(dots, step - 1, gram)
        for i in range(step):
            scalars_ref[i] = gram[(i, step - 1)]
            scalars_ref[step + i] = hess[i]
            scalars_ref[2 * step + 1 + i] = coefs[i]
        scalars_ref[2 * step] = length
    image = recombine(coefs, length, image, [load(ref) for ref in images])
    store(image_ref, image)
    if step + 1 < KRYLOV:
        spread(refs[-1], apply_inverse(inv_ref, image))


def recombine(coefs, length, fresh, held):
    scale = 1.0 / length
    out = []
    for h, value in enumerate(fresh):
        for c, vector in zip(coefs, held):
            value = value + c * vector[h]
        out.append(value * scale)
    return out


def extend_kernel(step, scalars_ref, vector_ref, search_ref, image_ref, *refs):
    bases, searches = refs[:step], refs[step : 2 * step]
    basis_ref, search_out_ref, dots_ref = refs[2 * step :]
    coefs = [scalars_ref[2 * step + 1 + i] for i in range(step)]
    length = scalars_ref[2 * step]
    vector = load(vector_ref)
    if step == 0:
        vector = [-value for value in vector]
    basis = [load(ref) for ref in bases]
    basis.append(recombine(coefs, length, vector, basis))
    store(basis_ref, basis[-1])
    store(search_out_ref, recombine(coefs, length, load(search_ref), [load(ref) for ref in searches]))
    image = load(image_ref)
    block = dots_block([(b, basis[-1]) for b in basis] + [(b, image) for b in basis] + [(image, image)])
    if step + 1 < KRYLOV:
        dots_ref[...] = block
    else:
        for d in range(dots_ref.shape[0]):
            dots_ref[d] = block


def finish_kernel(dots_ref, *refs):
    searches, scalar_refs = refs[:KRYLOV], refs[KRYLOV : 2 * KRYLOV]
    update_ref, first_ref = refs[2 * KRYLOV :]
    total = combine([dots_ref[d] for d in range(dots_ref.shape[0])])
    beta, gram, hess = read_scalars(scalar_refs)
    last, length, _ = orthogonalize(read_dots(total, 2 * KRYLOV + 1), KRYLOV - 1, gram)
    for i, value in enumerate(last):
        hess[(i, KRYLOV - 1)] = value
    hess[(KRYLOV, KRYLOV - 1)] = length

    work = [
        [combine([hess[(l, i)] * hess[(l, j)] for l in range(min(i, j) + 2)]) for j in range(KRYLOV)]
        for i in range(KRYLOV)
    ]
    vector = [beta * hess[(0, j)] for j in range(KRYLOV)]
    for p in range(KRYLOV):
        scale = 1.0 / work[p][p]
        top_work = [value * scale for value in work[p]]
        top = vector[p] * scale
        for i in range(KRYLOV):
            if i != p:
                factor = work[i][p]
                work[i] = [w - factor * t for w, t in zip(work[i], top_work)]
                vector[i] = vector[i] - factor * top
        work[p], vector[p] = top_work, top
    for h in range(halves_of(update_ref.shape[1])):
        update_ref[:, half(h)] = combine([c * ref[:, half(h)] for c, ref in zip(vector, searches)])
        first_ref[:, half(h)] = beta * searches[0][:, half(h)]


def shape(*dims, dtype=F32):
    return jax.ShapeDtypeStruct(dims, dtype)


def exchange(array, axes):
    return lax.all_to_all(array, axes, split_axis=0, concat_axis=0, tiled=True)


def local(stamps, stamp_target, pair_counts, conductance, block_cols, newton_residual):
    members = lax.axis_size("blk")
    devices = lax.axis_size("grp") * members
    rows = conductance.shape[1]

    send, to_next, own, near, pos = pl.pallas_call(
        functools.partial(pack_kernel, members),
        out_shape=(
            shape(devices, 9, 2, LANES),
            shape(72, LANES),
            shape(72, LANES),
            shape(K, 8, rows, dtype=I32),
            shape(K - K // 2, 8, rows, dtype=I32),
        ),
        in_specs=[pl.BlockSpec(memory_space=space) for space in (pl.ANY,) + 3 * (pltpu.VMEM,)],
        out_specs=tuple(pl.BlockSpec(memory_space=pltpu.VMEM) for _ in range(5)),
        scratch_shapes=[pltpu.VMEM(stamps.shape[1:], F32), pltpu.SemaphoreType.DMA],
        compiler_params=pltpu.CompilerParams(vmem_limit_bytes=60 * 2**20),
    )(stamps[0], stamp_target[0], pair_counts, block_cols)
    got = exchange(send, AXES)
    prev = lax.ppermute(to_next, AXES, [(i, (i + 1) % devices) for i in range(devices)])

    width = 2 * LANES * min(devices // 4 + 2, 10)
    jacobian, blocks, inverse, served, z, dots = call(
        assemble_kernel,
        (
            shape(K, 8, 8, rows),
            shape(K, 8, 8, rows),
            shape(8, 8, rows),
            shape(devices, 8, LANES, dtype=I32),
            shape(members, 8, rows),
            shape(8, LANES),
        ),
        got,
        prev,
        own,
        conductance,
        newton_residual,
        scratch=(pltpu.VMEM((64 * K, width), BF16), pltpu.VMEM((rows, width), BF16)),
    )

    bases, searches, images, scalars = [], [], [], []
    vector = newton_residual
    for step in range(KRYLOV):
        rhs, last = step == 0, step + 1 == KRYLOV
        z = call(
            functools.partial(first_sweep_kernel, rhs),
            shape(members, 8, rows + LANES),
            exchange(z, "blk"),
            vector,
            blocks,
            inverse,
            near,
            dots,
        )
        send, coupled, search, group_dots = call(
            functools.partial(second_sweep_kernel, rhs),
            (shape(devices, 8, rows), shape(8, rows), shape(8, rows), shape(8, LANES)),
            exchange(z, "blk"),
            vector,
            blocks,
            inverse,
            near,
            served,
            dots,
        )
        image, scalar, *rest = call(
            functools.partial(operate_kernel, step, members),
            [shape(8, rows), shape(3 * step + 1, 8, LANES)] + ([] if last else [shape(members, 8, rows)]),
            exchange(send, AXES),
            group_dots,
            coupled,
            blocks,
            inverse,
            near,
            pos,
            *images,
            *scalars,
        )
        z = None if last else rest[0]
        basis, search, dots = call(
            functools.partial(extend_kernel, step),
            (shape(8, rows), shape(8, rows), shape(devices, 8, LANES) if last else shape(8, LANES)),
            scalar,
            vector,
            search,
            image,
            *bases,
            *searches,
        )
        vector = image
        bases.append(basis)
        searches.append(search)
        images.append(image)
        scalars.append(scalar)

    update, first = call(
        finish_kernel, (shape(8, rows), shape(8, rows)), exchange(dots, AXES), *searches, *scalars
    )
    return update, jacobian, first


def solution(mesh):
    placed = (
        P(AXES, None, None, None),
        P(AXES, None, None),
        P(AXES, None),
        P(None, AXES),
        P(None, AXES),
        P(None, AXES),
    )
    return jax.shard_map(
        local,
        mesh=mesh,
        in_specs=placed,
        out_specs=(P(None, AXES), P(None, None, None, AXES), P(None, AXES)),
        check_vma=False,
    )
```

```python
import functools

import jax
import jax.numpy as jnp
from jax import lax
from jax.experimental import pallas as pl
from jax.experimental.pallas import tpu as pltpu
from jax.sharding import PartitionSpec as P

K = 16
KRYLOV = 5
LOW = 32
EPS = 1e-06
LANES = 128
AXES = ("grp", "blk")

F32 = jnp.float32
BF16 = jnp.bfloat16
I32 = jnp.int32

LANE_GATHER = lax.GatherDimensionNumbers(
    offset_dims=(),
    collapsed_slice_dims=(1,),
    start_index_map=(1,),
    operand_batching_dims=(0,),
    start_indices_batching_dims=(0,),
)


def lane_gather(source, lanes):
    return lax.gather(
        source,
        lanes[..., None],
        LANE_GATHER,
        slice_sizes=(1, 1),
        mode=lax.GatherScatterMode.PROMISE_IN_BOUNDS,
    )


def my_place(members):
    first = lax.axis_index("grp") * members
    return first + lax.axis_index("blk"), first


def call(kernel, out_shape, *args, scratch=(), vmem=32 * 2**20):
    return pl.pallas_call(
        kernel,
        out_shape=out_shape,
        in_specs=[pl.BlockSpec(memory_space=pltpu.VMEM)] * len(args),
        out_specs=jax.tree.map(lambda _: pl.BlockSpec(memory_space=pltpu.VMEM), out_shape),
        scratch_shapes=list(scratch),
        compiler_params=pltpu.CompilerParams(vmem_limit_bytes=vmem),
    )(*args)


def iota(shape, axis):
    return lax.broadcasted_iota(I32, shape, axis)


def halves_of(rows):
    return rows // LANES


def half(index):
    return slice(index * LANES, (index + 1) * LANES)


def stack_rows(rows):
    sub = iota((8, LANES), 0)
    out = jnp.zeros((8, LANES), F32)
    for a, value in enumerate(rows):
        out = jnp.where(sub == a, jnp.sum(value, axis=0, keepdims=True), out)
    return out


def apply_inverse(inv_ref, vector):
    out = []
    for h, value in enumerate(vector):
        out.append(stack_rows([inv_ref[a, :, half(h)] * value for a in range(8)]))
    return out


def pick(index, sources):
    at, lanes = index >> 7, index & (LANES - 1)
    picked = jnp.zeros((8, LANES), F32)
    for s, source in enumerate(sources):
        picked = jnp.where(at == s, lane_gather(source(), lanes), picked)
    return picked


def couple(jac_ref, index_ref, base, sources, first, last, acc):
    count = len(acc)
    for k in range(first, last):
        for h in range(count):
            picked = pick(index_ref[k - base, :, half(h)], sources)
            for a in range(8):
                acc[h][a] = acc[h][a] + jac_ref[k, a, :, half(h)] * picked
    return acc


def zero_acc(count):
    return [[jnp.zeros((8, LANES), F32) for _ in range(8)] for _ in range(count)]


def block_sources(ref, first, members, count):
    return [(lambda d=d, h=h: ref[first + d, :, half(h)]) for d in range(members) for h in range(count)]


def store(ref, vector):
    for h, value in enumerate(vector):
        ref[:, half(h)] = value


def spread(ref, vector):
    for d in range(ref.shape[0]):
        for h, value in enumerate(vector):
            ref[d, :, half(h)] = value


def load(ref):
    return [ref[:, half(h)] for h in range(halves_of(ref.shape[1]))]


def dots_block(pairs):
    sub, lane = iota((8, LANES), 0), iota((8, LANES), 1)
    blocks = []
    for start in (0, 8):
        rows = jnp.zeros((8, LANES), F32)
        for i, (left, right) in enumerate(pairs[start : start + 8]):
            total = sum(x * y for x, y in zip(left, right))
            rows = jnp.where(sub == i, jnp.sum(total, axis=0, keepdims=True), rows)
        blocks.append(jnp.sum(rows, axis=1, keepdims=True))
    return jnp.where(lane < 96, blocks[0], blocks[1])


def dots_row(block):
    sub, lane = iota((8, LANES), 0), iota((8, LANES), 1)
    late = pltpu.roll(block, 64, 1)
    row = jnp.where(lane == sub, late, 0.0) + jnp.where(lane == sub + 8, pltpu.roll(block, 32, 1), 0.0)
    return jnp.sum(row, axis=0, keepdims=True)


def read_row(row, count):
    lane = iota((1, LANES), 1)
    return [
        jnp.broadcast_to(jnp.sum(jnp.where(lane == i, row, 0.0), axis=1, keepdims=True), (8, LANES))
        for i in range(count)
    ]


def read_dots(total, count):
    lane = iota((8, LANES), 1)
    out = []
    for at in (64, 96):
        column = jnp.sum(jnp.where(lane == at, total, 0.0), axis=1, keepdims=True)
        column = jnp.broadcast_to(column, (8, LANES))
        out += [jnp.broadcast_to(column[i : i + 1, :], (8, LANES)) for i in range(8)]
    return out[:count]


def pack_kernel(
    members,
    stamps_any,
    target_ref,
    counts_ref,
    cols_ref,
    send_ref,
    next_ref,
    own_ref,
    pos_ref,
    inner_ref,
    stamps_ref,
    arrival,
):
    copy = pltpu.make_async_copy(stamps_any, stamps_ref, arrival)
    copy.start()
    devices = stamps_ref.shape[0]
    local_rows = cols_ref.shape[1]
    far_slots = K - K // 2
    per_owner = far_slots * local_rows // devices
    me, first = my_place(members)
    nxt = jnp.where(me + 1 == devices, 0, me + 1)
    lane = iota((1, LANES), 1)

    ids, slots = iota((devices, LANES), 0), iota((devices, LANES), 1)
    counts = jnp.broadcast_to(counts_ref[...], (devices, devices))
    diagonal = iota((devices, devices), 0) == iota((devices, devices), 1)
    counts = jnp.sum(jnp.where(diagonal, counts, 0).astype(F32), axis=1, keepdims=True)
    target = jnp.where(slots.astype(F32) < counts, target_ref[...].astype(F32), -1.0)
    low = jnp.where((ids == me) | (ids == nxt) | (slots >= LOW), -1.0, target)

    owners = iota((devices, LANES), 0)
    before = (iota((LANES, LANES), 0) < iota((LANES, LANES), 1)).astype(BF16)
    running = jnp.zeros((devices, 1), F32)
    asked = jnp.zeros((devices, LANES), F32)
    tiled = iota((LANES, LANES), 0) - 64
    for k in range(far_slots):
        for h in range(halves_of(local_rows)):
            cols = cols_ref[K // 2 + k : K // 2 + k + 1, half(h)]
            owner = cols // local_rows
            row = cols - owner * local_rows
            hot = (owners == owner).astype(F32)
            ahead = jnp.dot(hot.astype(BF16), before, preferred_element_type=F32) + running
            running = running + jnp.sum(hot, axis=1, keepdims=True)
            rank = jnp.sum(hot * ahead, axis=0, keepdims=True).astype(I32)
            asked += lax.dot_general(
                (hot * row.astype(F32)).astype(BF16),
                (tiled == rank).astype(F32).astype(BF16),
                (((1,), (1,)), ((), ())),
                preferred_element_type=F32,
            )
            ahead_of = jnp.where(owner < first, owner - first + devices, owner - first)
            pos_ref[k : k + 1, half(h)] = ahead_of * per_owner + rank

    copy.wait()
    for ref, at in ((next_ref, nxt), (own_ref, me)):
        ref[0:64, :] = stamps_ref[at]
        row = jnp.sum(jnp.where(ids == at, target, 0.0), axis=0, keepdims=True)
        ref[64:72, :] = jnp.broadcast_to(row, (8, LANES))
    for d in range(devices):
        packed = jnp.zeros((16, LANES), F32)
        for g in range(4):
            piece = stamps_ref[d, 16 * g : 16 * g + 16, :]
            if g:
                piece = pltpu.roll(piece, LOW * g, 1)
            packed = jnp.where(lane // LOW == g, piece, packed)
        for i in range(8):
            send_ref[d, i] = packed[2 * i : 2 * i + 2, :]
        ints = jnp.where(lane < 64, low[d : d + 1, :], asked[d : d + 1, :])
        send_ref[d, 8] = jnp.broadcast_to(ints, (2, LANES))

    each = LANES // per_owner
    mine = jnp.where((ids >= first) & (ids < first + members), asked + ((ids - first) * local_rows).astype(F32), 0.0)
    sub = iota((8, LANES), 0)
    for q in range(members // each):
        row = jnp.zeros((1, LANES), F32)
        for j in range(each):
            part = jnp.sum(jnp.where(ids == first + q * each + j, mine, 0.0), axis=0, keepdims=True)
            row = jnp.where(lane // per_owner == j, pltpu.roll(part, (64 + j * per_owner) % LANES, 1), row)
        inner_ref[q] = jnp.broadcast_to(row, (8, LANES)).astype(I32)


def index_kernel(members, cols_ref, pos_ref, near_ref, far_ref):
    local_rows = cols_ref.shape[1]
    _, first = my_place(members)
    start, stop = first * local_rows, (first + members) * local_rows
    for k in range(K):
        cols = cols_ref[k : k + 1, :]
        near = jnp.where((cols >= start) & (cols < stop), cols - start, -1)
        near_ref[k] = jnp.broadcast_to(near, (8, local_rows))
    for k in range(K - K // 2):
        far_ref[k] = jnp.broadcast_to(pos_ref[k : k + 1, :], (8, local_rows))


def assemble_kernel(
    recv_ref, prev_ref, own_ref, cond_ref, resid_ref, whole_ref, jac_ref, inv_ref, served_ref, z_ref, left_ref, right_ref
):
    devices = recv_ref.shape[0]
    local_rows = cond_ref.shape[1]
    lane = iota((1, LANES), 1)
    blocks = devices // 4 + 2

    def stamp_rows(d):
        return jnp.concatenate([recv_ref[d, i] for i in range(8)], axis=0)

    def block(q):
        if q == 0:
            return own_ref[0:64, :], own_ref[64:65, :]
        if q == 1:
            return prev_ref[0:64, :], prev_ref[64:65, :]
        first = 4 * (q - 2)
        rows = []
        pieces = [stamp_rows(first + j) for j in range(4)]
        for g in range(4):
            out = jnp.zeros((16, LANES), F32)
            for j in range(4):
                piece = pieces[j]
                if j != g:
                    piece = pltpu.roll(piece, (LOW * (j - g)) % LANES, 1)
                out = jnp.where(lane // LOW == j, piece, out)
            rows.append(out)
        target = jnp.full((1, LANES), -1.0, F32)
        for j in range(4):
            piece = recv_ref[first + j, 8, 0:1, :]
            if j:
                piece = pltpu.roll(piece, LOW * j, 1)
            target = jnp.where(lane // LOW == j, piece, target)
        return jnp.concatenate(rows, axis=0), target

    most = 10
    for start in range(0, blocks, most):
        stop = min(start + most, blocks)
        width = 2 * (stop - start) * LANES
        values = []
        for q in range(start, stop):
            at = 2 * (q - start) * LANES
            stamp, target = block(q)
            target = target.astype(I32)
            slot, row = target >> (local_rows.bit_length() - 1), target & (local_rows - 1)
            hot = (iota((local_rows, LANES), 0) == row).astype(F32).astype(BF16)
            right_ref[:, at : at + LANES] = hot
            right_ref[:, at + LANES : at + 2 * LANES] = hot
            high = stamp.astype(BF16)
            low = (stamp - high.astype(F32)).astype(BF16)
            values.append((at, slot, high, low))

        for k in range(K):
            for at, slot, high, low in values:
                mask = (slot == k).astype(F32).astype(BF16)
                left_ref[64 * k : 64 * k + 64, at : at + LANES] = high * mask
                left_ref[64 * k : 64 * k + 64, at + LANES : at + 2 * LANES] = low * mask
        total = lax.dot_general(
            left_ref[:, 0:width],
            right_ref[:, 0:width],
            (((1,), (1,)), ((), ())),
            preferred_element_type=F32,
        ).reshape(K, 8, 8, local_rows)
        if start == 0:
            jac_ref[...] = total
        else:
            jac_ref[...] += total
    sub = iota((8, local_rows), 0)
    for a in range(8):
        jac_ref[0, a] = jac_ref[0, a] + jnp.where(sub == a, cond_ref[a : a + 1, :], 0.0)

    whole_ref[...] = jac_ref[...]

    work = [jac_ref[0, a] for a in range(8)]
    inverse = [jnp.where(sub == a, 1.0, 0.0).astype(F32) for a in range(8)]
    for p in range(8):
        scale = 1.0 / work[p][p : p + 1, :]
        top_work, top_inverse = work[p] * scale, inverse[p] * scale
        for a in range(8):
            if a != p:
                factor = work[a][p : p + 1, :]
                work[a] = work[a] - factor * top_work
                inverse[a] = inverse[a] - factor * top_inverse
        work[p], inverse[p] = top_work, top_inverse
    for a in range(8):
        inv_ref[a] = inverse[a]

    for d in range(devices):
        asked = pltpu.roll(recv_ref[d, 8, 0:1, :], 64, 1).astype(I32)
        served_ref[d] = jnp.broadcast_to(asked, (8, LANES))
    rhs = [-value for value in load(resid_ref)]
    spread(z_ref, apply_inverse(inv_ref, rhs) + [dots_block([(rhs, rhs)])])


def first_sweep_kernel(rhs, group_ref, vector_ref, jac_ref, inv_ref, near_ref, z_ref, dots_ref):
    vector = load(vector_ref)
    if rhs:
        vector = [-value for value in vector]
    members, count = group_ref.shape[0], len(vector)
    sources = block_sources(group_ref, 0, members, count)
    acc = couple(jac_ref, near_ref, 0, sources, 1, K, zero_acc(count))
    spread(z_ref, apply_inverse(inv_ref, [v - stack_rows(c) for v, c in zip(vector, acc)]))
    dots_ref[0] = combine([group_ref[d, :, half(count)] for d in range(members)])
    dots_ref[1] = group_ref[lax.axis_index("blk"), :, half(count)]


def second_sweep_kernel(
    rhs,
    group_ref,
    vector_ref,
    jac_ref,
    inv_ref,
    near_ref,
    served_ref,
    dots_ref,
    send_ref,
    coupled_ref,
):
    vector = load(vector_ref)
    if rhs:
        vector = [-value for value in vector]
    members, count = group_ref.shape[0], len(vector)
    sources = block_sources(group_ref, 0, members, count)
    acc = couple(jac_ref, near_ref, 0, sources, 1, K, zero_acc(count))
    coupled = [stack_rows(c) for c in acc]
    result = apply_inverse(inv_ref, [v - c for v, c in zip(vector, coupled)])
    store(coupled_ref, coupled)
    dots = dots_ref[1]
    lane = iota((8, LANES), 1)
    for d in range(send_ref.shape[0]):
        index = served_ref[d]
        lanes = index & (LANES - 1)
        picked = lane_gather(result[0], lanes)
        for h in range(1, count):
            picked = jnp.where(index >> 7 == h, lane_gather(result[h], lanes), picked)
        send_ref[d, :, half(0)] = jnp.where(lane < 64, picked, dots)
        for h in range(1, count):
            send_ref[d, :, half(h)] = result[h]
    _, first = my_place(members)
    for d in range(members):
        send_ref[first + d, :, half(0)] = result[0]


def combine(terms):
    return functools.reduce(lambda x, y: x + y, terms)


def orthogonalize(dots, step, gram):
    count = step + 1
    for i in range(count):
        gram[(i, step)] = gram[(step, i)] = dots[i]
    along = dots[count : 2 * count]
    hess = [gram[(i, step)] + along[i] for i in range(count)]
    coefs = [(1.0 - h if i == step else -h) for i, h in enumerate(hess)]
    square = dots[2 * count]
    for i in range(count):
        inner = combine([coefs[l] * gram[(i, l)] for l in range(count)])
        square = square + coefs[i] * (2.0 * along[i] + inner)
    length = jnp.sqrt(jnp.maximum(square, 0.0) + EPS)
    return hess, length, coefs


def read_scalars(refs):
    gram, hess, lengths = {}, {}, []
    beta = refs[0][0]
    for step, ref in enumerate(refs[1:]):
        count = step + 1
        for i in range(count):
            gram[(i, step)] = gram[(step, i)] = ref[i]
            hess[(i, step)] = ref[count + i]
        hess[(count, step)] = ref[2 * count]
    return beta, gram, hess


def operate_kernel(step, members, recv_ref, group_dots_ref, coupled_ref, vector_ref, *refs):
    jac_ref, inv_ref, near_ref, pos_ref, inner_ref = refs[:5]
    refs = refs[5:]
    states, scalar_refs = refs[:step], refs[step : 2 * step]
    state_ref, scalars_ref, vector_out_ref, z_ref = refs[2 * step :]
    devices = recv_ref.shape[0]
    rows = coupled_ref.shape[1]
    count = halves_of(rows)
    per_owner = (K - K // 2) * rows // devices
    each = LANES // per_owner
    lane = iota((8, LANES), 1)
    me, first = my_place(members)

    group = block_sources(recv_ref, first, members, count)
    far = []
    total = group_dots_ref[0]
    for q in range(devices // each):
        if q < members // each:
            out = pick(inner_ref[q], group)
        else:
            for j in range(each):
                d = first + q * each + j
                piece = recv_ref[jnp.where(d < devices, d, d - devices), :, half(0)]
                total = total + piece
                if j == 0:
                    out = piece
                else:
                    out = jnp.where(lane // per_owner == j, pltpu.roll(piece, j * per_owner, 1), out)
        far.append(out)

    acc = couple(jac_ref, near_ref, 0, group, 1, K // 2, zero_acc(count))
    acc = couple(jac_ref, pos_ref, K // 2, [(lambda v=v: v) for v in far], K // 2, K, acc)
    image = [stack_rows(c) - n for c, n in zip(acc, load(coupled_ref))]
    search = [recv_ref[me, :, half(h)] for h in range(count)]
    vector = load(vector_ref)

    if step == 0:
        vector = [-value for value in vector]
        length = jnp.sqrt(read_dots(total, 1)[0] + EPS)
        scalars_ref[0] = length
        coefs = []
    else:
        _, gram, _ = read_scalars(scalar_refs)
        dots = read_dots(total, 2 * step + 1)
        hess, length, coefs = orthogonalize(dots, step - 1, gram)
        for i in range(step):
            scalars_ref[i] = gram[(i, step - 1)]
            scalars_ref[step + i] = hess[i]
        scalars_ref[2 * step] = length
    scale = 1.0 / length

    def recombine(part, fresh):
        out = []
        for h, value in enumerate(fresh):
            for c, ref in zip(coefs, states):
                value = value + c * ref[part, :, half(h)]
            value = value * scale
            state_ref[part, :, half(h)] = value
            out.append(value)
        return out

    basis = [[ref[0, :, half(h)] for h in range(count)] for ref in states]
    basis.append(recombine(0, vector))
    recombine(1, search)
    image = recombine(2, image)
    store(vector_out_ref, image)
    pairs = [(b, basis[-1]) for b in basis] + [(b, image) for b in basis] + [(image, image)]
    block = dots_block(pairs)
    if step + 1 < KRYLOV:
        spread(z_ref, apply_inverse(inv_ref, image) + [block])
    else:
        row = dots_row(block)
        for d in range(devices):
            z_ref[d] = row


def finish_kernel(dots_ref, *refs):
    states, scalar_refs = refs[:KRYLOV], refs[KRYLOV : 2 * KRYLOV]
    update_ref, first_ref = refs[2 * KRYLOV :]
    total = combine([dots_ref[d] for d in range(dots_ref.shape[0])])
    beta, gram, hess = read_scalars(scalar_refs)
    last, length, _ = orthogonalize(read_row(total, 2 * KRYLOV + 1), KRYLOV - 1, gram)
    for i, value in enumerate(last):
        hess[(i, KRYLOV - 1)] = value
    hess[(KRYLOV, KRYLOV - 1)] = length

    work = [
        [combine([hess[(l, i)] * hess[(l, j)] for l in range(min(i, j) + 2)]) for j in range(KRYLOV)]
        for i in range(KRYLOV)
    ]
    vector = [beta * hess[(0, j)] for j in range(KRYLOV)]
    for p in range(KRYLOV):
        scale = 1.0 / work[p][p]
        top_work = [value * scale for value in work[p]]
        top = vector[p] * scale
        for i in range(KRYLOV):
            if i != p:
                factor = work[i][p]
                work[i] = [w - factor * t for w, t in zip(work[i], top_work)]
                vector[i] = vector[i] - factor * top
        work[p], vector[p] = top_work, top
    for h in range(halves_of(update_ref.shape[1])):
        update_ref[:, half(h)] = combine([c * ref[1, :, half(h)] for c, ref in zip(vector, states)])
        first_ref[:, half(h)] = beta * states[0][1, :, half(h)]


def shape(*dims, dtype=F32):
    return jax.ShapeDtypeStruct(dims, dtype)


def exchange(array, axes):
    return lax.all_to_all(array, axes, split_axis=0, concat_axis=0, tiled=True)


def local(stamps, stamp_target, pair_counts, conductance, block_cols, newton_residual):
    members = lax.axis_size("blk")
    devices = lax.axis_size("grp") * members
    rows = conductance.shape[1]

    send, to_next, own, pos, inner = pl.pallas_call(
        functools.partial(pack_kernel, members),
        out_shape=(
            shape(devices, 9, 2, LANES),
            shape(72, LANES),
            shape(72, LANES),
            shape(K - K // 2, rows, dtype=I32),
            shape(members * (K - K // 2) * rows // devices // LANES, 8, LANES, dtype=I32),
        ),
        in_specs=[pl.BlockSpec(memory_space=space) for space in (pl.ANY,) + 3 * (pltpu.VMEM,)],
        out_specs=tuple(pl.BlockSpec(memory_space=pltpu.VMEM) for _ in range(5)),
        scratch_shapes=[pltpu.VMEM(stamps.shape[1:], F32), pltpu.SemaphoreType.DMA],
        compiler_params=pltpu.CompilerParams(vmem_limit_bytes=60 * 2**20),
    )(stamps[0], stamp_target[0], pair_counts, block_cols)
    got = exchange(send, AXES)
    prev = lax.ppermute(to_next, AXES, [(i, (i + 1) % devices) for i in range(devices)])

    near, far = call(
        functools.partial(index_kernel, members),
        (shape(K, 8, rows, dtype=I32), shape(K - K // 2, 8, rows, dtype=I32)),
        block_cols,
        pos,
    )

    width = 2 * LANES * min(devices // 4 + 2, 10)
    jacobian, blocks, inverse, served, z = call(
        assemble_kernel,
        (
            shape(K, 8, 8, rows),
            shape(K, 8, 8, rows),
            shape(8, 8, rows),
            shape(devices, 8, LANES, dtype=I32),
            shape(members, 8, rows + LANES),
        ),
        got,
        prev,
        own,
        conductance,
        newton_residual,
        scratch=(pltpu.VMEM((64 * K, width), BF16), pltpu.VMEM((rows, width), BF16)),
    )

    states, scalars = [], []
    vector = newton_residual
    for step in range(KRYLOV):
        rhs = step == 0
        z, group_dots = call(
            functools.partial(first_sweep_kernel, rhs),
            (shape(members, 8, rows), shape(2, 8, LANES)),
            exchange(z, "blk"),
            vector,
            blocks,
            inverse,
            near,
        )
        send, coupled = call(
            functools.partial(second_sweep_kernel, rhs),
            (shape(devices, 8, rows), shape(8, rows)),
            exchange(z, "blk"),
            vector,
            blocks,
            inverse,
            near,
            served,
            group_dots,
        )
        last = step + 1 == KRYLOV
        state, scalar, vector, z = call(
            functools.partial(operate_kernel, step, members),
            (
                shape(3, 8, rows),
                shape(2 * step + 1, 8, LANES),
                shape(8, rows),
                shape(devices, 1, LANES) if last else shape(members, 8, rows + LANES),
            ),
            exchange(send, AXES),
            group_dots,
            coupled,
            vector,
            blocks,
            inverse,
            near,
            far,
            inner,
            *states,
            *scalars,
        )
        states.append(state)
        scalars.append(scalar)

    update, first = call(finish_kernel, (shape(8, rows), shape(8, rows)), exchange(z, AXES), *states, *scalars)
    return update, jacobian, first


def solution(mesh):
    placed = (
        P(AXES, None, None, None),
        P(AXES, None, None),
        P(AXES, None),
        P(None, AXES),
        P(None, AXES),
        P(None, AXES),
    )
    return jax.shard_map(
        local,
        mesh=mesh,
        in_specs=placed,
        out_specs=(P(None, AXES), P(None, None, None, AXES), P(None, AXES)),
        check_vma=False,
    )
```

```python
import functools

import jax
import jax.numpy as jnp
from jax import lax
from jax.experimental import pallas as pl
from jax.experimental.pallas import tpu as pltpu
from jax.sharding import PartitionSpec as P

K = 16
KRYLOV = 5
LOW = 32
EPS = 1e-06
LANES = 128
AXES = ("grp", "blk")

F32 = jnp.float32
BF16 = jnp.bfloat16
I32 = jnp.int32

LANE_GATHER = lax.GatherDimensionNumbers(
    offset_dims=(),
    collapsed_slice_dims=(1,),
    start_index_map=(1,),
    operand_batching_dims=(0,),
    start_indices_batching_dims=(0,),
)


def lane_gather(source, lanes):
    return lax.gather(
        source,
        lanes[..., None],
        LANE_GATHER,
        slice_sizes=(1, 1),
        mode=lax.GatherScatterMode.PROMISE_IN_BOUNDS,
    )


def my_place(members):
    first = lax.axis_index("grp") * members
    return first + lax.axis_index("blk"), first


def call(kernel, out_shape, *args, scratch=(), vmem=32 * 2**20, outside=0):
    flat, tree = jax.tree.flatten(out_shape)
    spaces = [pl.ANY] * outside + [pltpu.VMEM] * (len(flat) - outside)
    return pl.pallas_call(
        kernel,
        out_shape=out_shape,
        in_specs=[pl.BlockSpec(memory_space=pltpu.VMEM)] * len(args),
        out_specs=jax.tree.unflatten(tree, [pl.BlockSpec(memory_space=space) for space in spaces]),
        scratch_shapes=list(scratch),
        compiler_params=pltpu.CompilerParams(vmem_limit_bytes=vmem),
    )(*args)


def iota(shape, axis):
    return lax.broadcasted_iota(I32, shape, axis)


def halves_of(rows):
    return rows // LANES


def half(index):
    return slice(index * LANES, (index + 1) * LANES)


def stack_rows(rows):
    sub = iota((8, LANES), 0)
    out = jnp.zeros((8, LANES), F32)
    for a, value in enumerate(rows):
        out = jnp.where(sub == a, jnp.sum(value, axis=0, keepdims=True), out)
    return out


def apply_inverse(inv_ref, vector):
    out = []
    for h, value in enumerate(vector):
        out.append(stack_rows([inv_ref[a, :, half(h)] * value for a in range(8)]))
    return out


def pick(index, sources):
    at, lanes = index >> 7, index & (LANES - 1)
    picked = jnp.zeros((8, LANES), F32)
    for s, source in enumerate(sources):
        picked = jnp.where(at == s, lane_gather(source(), lanes), picked)
    return picked


def couple(jac_ref, index_ref, base, sources, first, last, acc):
    count = len(acc)
    for k in range(first, last):
        for h in range(count):
            picked = pick(index_ref[k - base, :, half(h)], sources)
            for a in range(8):
                acc[h][a] = acc[h][a] + jac_ref[k, a, :, half(h)] * picked
    return acc


def zero_acc(count):
    return [[jnp.zeros((8, LANES), F32) for _ in range(8)] for _ in range(count)]


def block_sources(ref, first, members, count):
    return [(lambda d=d, h=h: ref[first + d, :, half(h)]) for d in range(members) for h in range(count)]


def store(ref, vector):
    for h, value in enumerate(vector):
        ref[:, half(h)] = value


def spread(ref, vector):
    for d in range(ref.shape[0]):
        for h, value in enumerate(vector):
            ref[d, :, half(h)] = value


def load(ref):
    return [ref[:, half(h)] for h in range(halves_of(ref.shape[1]))]


def dots_block(pairs):
    sub, lane = iota((8, LANES), 0), iota((8, LANES), 1)
    blocks = []
    for start in (0, 8):
        rows = jnp.zeros((8, LANES), F32)
        for i, (left, right) in enumerate(pairs[start : start + 8]):
            total = sum(x * y for x, y in zip(left, right))
            rows = jnp.where(sub == i, jnp.sum(total, axis=0, keepdims=True), rows)
        blocks.append(jnp.sum(rows, axis=1, keepdims=True))
    return jnp.where(lane < 96, blocks[0], blocks[1])


def dots_row(block):
    sub, lane = iota((8, LANES), 0), iota((8, LANES), 1)
    late = pltpu.roll(block, 64, 1)
    row = jnp.where(lane == sub, late, 0.0) + jnp.where(lane == sub + 8, pltpu.roll(block, 32, 1), 0.0)
    return jnp.sum(row, axis=0, keepdims=True)


def read_row(row, count):
    lane = iota((1, LANES), 1)
    return [
        jnp.broadcast_to(jnp.sum(jnp.where(lane == i, row, 0.0), axis=1, keepdims=True), (8, LANES))
        for i in range(count)
    ]


def read_dots(total, count):
    lane = iota((8, LANES), 1)
    out = []
    for at in (64, 96):
        column = jnp.sum(jnp.where(lane == at, total, 0.0), axis=1, keepdims=True)
        column = jnp.broadcast_to(column, (8, LANES))
        out += [jnp.broadcast_to(column[i : i + 1, :], (8, LANES)) for i in range(8)]
    return out[:count]


def pack_kernel(
    members,
    stamps_any,
    target_ref,
    counts_ref,
    cols_ref,
    send_ref,
    next_ref,
    own_ref,
    pos_ref,
    inner_ref,
    stamps_ref,
    arrival,
):
    copy = pltpu.make_async_copy(stamps_any, stamps_ref, arrival)
    copy.start()
    devices = stamps_ref.shape[0]
    local_rows = cols_ref.shape[1]
    far_slots = K - K // 2
    per_owner = far_slots * local_rows // devices
    me, first = my_place(members)
    nxt = jnp.where(me + 1 == devices, 0, me + 1)
    lane = iota((1, LANES), 1)

    ids, slots = iota((devices, LANES), 0), iota((devices, LANES), 1)
    counts = jnp.broadcast_to(counts_ref[...], (devices, devices))
    diagonal = iota((devices, devices), 0) == iota((devices, devices), 1)
    counts = jnp.sum(jnp.where(diagonal, counts, 0).astype(F32), axis=1, keepdims=True)
    target = jnp.where(slots.astype(F32) < counts, target_ref[...].astype(F32), -1.0)
    low = jnp.where((ids == me) | (ids == nxt) | (slots >= LOW), -1.0, target)

    owners = iota((devices, LANES), 0)
    before = (iota((LANES, LANES), 0) < iota((LANES, LANES), 1)).astype(BF16)
    running = jnp.zeros((devices, 1), F32)
    asked = jnp.zeros((devices, LANES), F32)
    tiled = iota((LANES, LANES), 0) - 64
    for k in range(far_slots):
        for h in range(halves_of(local_rows)):
            cols = cols_ref[K // 2 + k : K // 2 + k + 1, half(h)]
            owner = cols // local_rows
            row = cols - owner * local_rows
            hot = (owners == owner).astype(F32)
            ahead = jnp.dot(hot.astype(BF16), before, preferred_element_type=F32) + running
            running = running + jnp.sum(hot, axis=1, keepdims=True)
            rank = jnp.sum(hot * ahead, axis=0, keepdims=True).astype(I32)
            asked += lax.dot_general(
                (hot * row.astype(F32)).astype(BF16),
                (tiled == rank).astype(F32).astype(BF16),
                (((1,), (1,)), ((), ())),
                preferred_element_type=F32,
            )
            ahead_of = jnp.where(owner < first, owner - first + devices, owner - first)
            pos_ref[k : k + 1, half(h)] = ahead_of * per_owner + rank

    copy.wait()
    for ref, at in ((next_ref, nxt), (own_ref, me)):
        ref[0:64, :] = stamps_ref[at]
        row = jnp.sum(jnp.where(ids == at, target, 0.0), axis=0, keepdims=True)
        ref[64:72, :] = jnp.broadcast_to(row, (8, LANES))
    for d in range(devices):
        packed = jnp.zeros((16, LANES), F32)
        for g in range(4):
            piece = stamps_ref[d, 16 * g : 16 * g + 16, :]
            if g:
                piece = pltpu.roll(piece, LOW * g, 1)
            packed = jnp.where(lane // LOW == g, piece, packed)
        for i in range(8):
            send_ref[d, i] = packed[2 * i : 2 * i + 2, :]
        ints = jnp.where(lane < 64, low[d : d + 1, :], asked[d : d + 1, :])
        send_ref[d, 8] = jnp.broadcast_to(ints, (2, LANES))

    each = LANES // per_owner
    mine = jnp.where((ids >= first) & (ids < first + members), asked + ((ids - first) * local_rows).astype(F32), 0.0)
    sub = iota((8, LANES), 0)
    for q in range(members // each):
        row = jnp.zeros((1, LANES), F32)
        for j in range(each):
            part = jnp.sum(jnp.where(ids == first + q * each + j, mine, 0.0), axis=0, keepdims=True)
            row = jnp.where(lane // per_owner == j, pltpu.roll(part, (64 + j * per_owner) % LANES, 1), row)
        inner_ref[q] = jnp.broadcast_to(row, (8, LANES)).astype(I32)


def index_kernel(members, cols_ref, pos_ref, near_ref, far_ref):
    local_rows = cols_ref.shape[1]
    _, first = my_place(members)
    start, stop = first * local_rows, (first + members) * local_rows
    for k in range(K):
        cols = cols_ref[k : k + 1, :]
        near = jnp.where((cols >= start) & (cols < stop), cols - start, -1)
        near_ref[k] = jnp.broadcast_to(near, (8, local_rows))
    for k in range(K - K // 2):
        far_ref[k] = jnp.broadcast_to(pos_ref[k : k + 1, :], (8, local_rows))


def assemble_kernel(
    near_ref, recv_ref, prev_ref, own_ref, cond_ref, resid_ref, whole_any, jac_ref, inv_ref, served_ref, z_ref, left_ref, right_ref, departure
):
    devices = recv_ref.shape[0]
    local_rows = cond_ref.shape[1]
    lane = iota((1, LANES), 1)
    blocks = devices // 4 + 2

    def stamp_rows(d):
        return jnp.concatenate([recv_ref[d, i] for i in range(8)], axis=0)

    def block(q):
        if q == 0:
            return own_ref[0:64, :], own_ref[64:65, :]
        if q == 1:
            return prev_ref[0:64, :], prev_ref[64:65, :]
        first = 4 * (q - 2)
        rows = []
        pieces = [stamp_rows(first + j) for j in range(4)]
        for g in range(4):
            out = jnp.zeros((16, LANES), F32)
            for j in range(4):
                piece = pieces[j]
                if j != g:
                    piece = pltpu.roll(piece, (LOW * (j - g)) % LANES, 1)
                out = jnp.where(lane // LOW == j, piece, out)
            rows.append(out)
        target = jnp.full((1, LANES), -1.0, F32)
        for j in range(4):
            piece = recv_ref[first + j, 8, 0:1, :]
            if j:
                piece = pltpu.roll(piece, LOW * j, 1)
            target = jnp.where(lane // LOW == j, piece, target)
        return jnp.concatenate(rows, axis=0), target

    most = 10
    for start in range(0, blocks, most):
        stop = min(start + most, blocks)
        width = 2 * (stop - start) * LANES
        values = []
        for q in range(start, stop):
            at = 2 * (q - start) * LANES
            stamp, target = block(q)
            target = target.astype(I32)
            slot, row = target >> (local_rows.bit_length() - 1), target & (local_rows - 1)
            hot = (iota((local_rows, LANES), 0) == row).astype(F32).astype(BF16)
            right_ref[:, at : at + LANES] = hot
            right_ref[:, at + LANES : at + 2 * LANES] = hot
            high = stamp.astype(BF16)
            low = (stamp - high.astype(F32)).astype(BF16)
            values.append((at, slot, high, low))

        for k in range(K):
            for at, slot, high, low in values:
                mask = (slot == k).astype(F32).astype(BF16)
                left_ref[64 * k : 64 * k + 64, at : at + LANES] = high * mask
                left_ref[64 * k : 64 * k + 64, at + LANES : at + 2 * LANES] = low * mask
        total = lax.dot_general(
            left_ref[:, 0:width],
            right_ref[:, 0:width],
            (((1,), (1,)), ((), ())),
            preferred_element_type=F32,
        ).reshape(K, 8, 8, local_rows)
        if start == 0:
            jac_ref[...] = total
        else:
            jac_ref[...] += total
    sub = iota((8, local_rows), 0)
    for a in range(8):
        jac_ref[0, a] = jac_ref[0, a] + jnp.where(sub == a, cond_ref[a : a + 1, :], 0.0)

    copy = pltpu.make_async_copy(jac_ref, whole_any, departure)
    copy.start()

    work = [jac_ref[0, a] for a in range(8)]
    inverse = [jnp.where(sub == a, 1.0, 0.0).astype(F32) for a in range(8)]
    for p in range(8):
        scale = 1.0 / work[p][p : p + 1, :]
        top_work, top_inverse = work[p] * scale, inverse[p] * scale
        for a in range(8):
            if a != p:
                factor = work[a][p : p + 1, :]
                work[a] = work[a] - factor * top_work
                inverse[a] = inverse[a] - factor * top_inverse
        work[p], inverse[p] = top_work, top_inverse
    for a in range(8):
        inv_ref[a] = inverse[a]

    for d in range(devices):
        asked = pltpu.roll(recv_ref[d, 8, 0:1, :], 64, 1).astype(I32)
        served_ref[d] = jnp.broadcast_to(asked, (8, LANES))
    rhs = [-value for value in load(resid_ref)]
    spread(z_ref, apply_inverse(inv_ref, rhs) + [dots_block([(rhs, rhs)])])
    copy.wait()


def first_sweep_kernel(rhs, group_ref, vector_ref, jac_ref, inv_ref, near_ref, z_ref, dots_ref):
    vector = load(vector_ref)
    if rhs:
        vector = [-value for value in vector]
    members, count = group_ref.shape[0], len(vector)
    sources = block_sources(group_ref, 0, members, count)
    acc = couple(jac_ref, near_ref, 0, sources, 1, K, zero_acc(count))
    spread(z_ref, apply_inverse(inv_ref, [v - stack_rows(c) for v, c in zip(vector, acc)]))
    dots_ref[0] = combine([group_ref[d, :, half(count)] for d in range(members)])
    dots_ref[1] = group_ref[lax.axis_index("blk"), :, half(count)]


def second_sweep_kernel(
    rhs,
    group_ref,
    vector_ref,
    jac_ref,
    inv_ref,
    near_ref,
    served_ref,
    dots_ref,
    send_ref,
    coupled_ref,
):
    vector = load(vector_ref)
    if rhs:
        vector = [-value for value in vector]
    members, count = group_ref.shape[0], len(vector)
    sources = block_sources(group_ref, 0, members, count)
    acc = couple(jac_ref, near_ref, 0, sources, 1, K, zero_acc(count))
    coupled = [stack_rows(c) for c in acc]
    result = apply_inverse(inv_ref, [v - c for v, c in zip(vector, coupled)])
    store(coupled_ref, coupled)
    dots = dots_ref[1]
    lane = iota((8, LANES), 1)
    for d in range(send_ref.shape[0]):
        index = served_ref[d]
        lanes = index & (LANES - 1)
        picked = lane_gather(result[0], lanes)
        for h in range(1, count):
            picked = jnp.where(index >> 7 == h, lane_gather(result[h], lanes), picked)
        send_ref[d, :, half(0)] = jnp.where(lane < 64, picked, dots)
        for h in range(1, count):
            send_ref[d, :, half(h)] = result[h]
    _, first = my_place(members)
    for d in range(members):
        send_ref[first + d, :, half(0)] = result[0]


def combine(terms):
    return functools.reduce(lambda x, y: x + y, terms)


def orthogonalize(dots, step, gram):
    count = step + 1
    for i in range(count):
        gram[(i, step)] = gram[(step, i)] = dots[i]
    along = dots[count : 2 * count]
    hess = [gram[(i, step)] + along[i] for i in range(count)]
    coefs = [(1.0 - h if i == step else -h) for i, h in enumerate(hess)]
    square = dots[2 * count]
    for i in range(count):
        inner = combine([coefs[l] * gram[(i, l)] for l in range(count)])
        square = square + coefs[i] * (2.0 * along[i] + inner)
    length = jnp.sqrt(jnp.maximum(square, 0.0) + EPS)
    return hess, length, coefs


def read_scalars(refs):
    gram, hess, lengths = {}, {}, []
    beta = refs[0][0]
    for step, ref in enumerate(refs[1:]):
        count = step + 1
        for i in range(count):
            gram[(i, step)] = gram[(step, i)] = ref[i]
            hess[(i, step)] = ref[count + i]
        hess[(count, step)] = ref[2 * count]
    return beta, gram, hess


def operate_kernel(step, members, recv_ref, group_dots_ref, coupled_ref, vector_ref, *refs):
    jac_ref, inv_ref, near_ref, pos_ref, inner_ref = refs[:5]
    refs = refs[5:]
    states, scalar_refs = refs[:step], refs[step : 2 * step]
    state_ref, scalars_ref, z_ref, *vector_out = refs[2 * step :]
    devices = recv_ref.shape[0]
    rows = coupled_ref.shape[1]
    count = halves_of(rows)
    per_owner = (K - K // 2) * rows // devices
    each = LANES // per_owner
    lane = iota((8, LANES), 1)
    me, first = my_place(members)

    group = block_sources(recv_ref, first, members, count)
    far = []
    total = group_dots_ref[0]
    for q in range(devices // each):
        if q < members // each:
            out = pick(inner_ref[q], group)
        else:
            for j in range(each):
                d = first + q * each + j
                piece = recv_ref[jnp.where(d < devices, d, d - devices), :, half(0)]
                total = total + piece
                if j == 0:
                    out = piece
                else:
                    out = jnp.where(lane // per_owner == j, pltpu.roll(piece, j * per_owner, 1), out)
        far.append(out)

    acc = couple(jac_ref, near_ref, 0, group, 1, K // 2, zero_acc(count))
    acc = couple(jac_ref, pos_ref, K // 2, [(lambda v=v: v) for v in far], K // 2, K, acc)
    image = [stack_rows(c) - n for c, n in zip(acc, load(coupled_ref))]
    search = [recv_ref[me, :, half(h)] for h in range(count)]
    vector = load(vector_ref)

    if step == 0:
        vector = [-value for value in vector]
        length = jnp.sqrt(read_dots(total, 1)[0] + EPS)
        scalars_ref[0] = length
        coefs = []
    else:
        _, gram, _ = read_scalars(scalar_refs)
        dots = read_dots(total, 2 * step + 1)
        hess, length, coefs = orthogonalize(dots, step - 1, gram)
        for i in range(step):
            scalars_ref[i] = gram[(i, step - 1)]
            scalars_ref[step + i] = hess[i]
        scalars_ref[2 * step] = length
    scale = 1.0 / length

    def recombine(part, fresh):
        out = []
        for h, value in enumerate(fresh):
            for c, ref in zip(coefs, states):
                value = value + c * ref[part, :, half(h)]
            value = value * scale
            state_ref[part, :, half(h)] = value
            out.append(value)
        return out

    basis = [[ref[0, :, half(h)] for h in range(count)] for ref in states]
    basis.append(recombine(0, vector))
    recombine(1, search)
    image = recombine(2, image)
    if vector_out:
        store(vector_out[0], image)
    pairs = [(b, basis[-1]) for b in basis] + [(b, image) for b in basis] + [(image, image)]
    block = dots_block(pairs)
    if step + 1 < KRYLOV:
        spread(z_ref, apply_inverse(inv_ref, image) + [block])
    else:
        row = dots_row(block)
        for d in range(devices):
            z_ref[d] = row


def finish_kernel(dots_ref, *refs):
    states, scalar_refs = refs[:KRYLOV], refs[KRYLOV : 2 * KRYLOV]
    update_ref, first_ref = refs[2 * KRYLOV :]
    total = combine([dots_ref[d] for d in range(dots_ref.shape[0])])
    beta, gram, hess = read_scalars(scalar_refs)
    last, length, _ = orthogonalize(read_row(total, 2 * KRYLOV + 1), KRYLOV - 1, gram)
    for i, value in enumerate(last):
        hess[(i, KRYLOV - 1)] = value
    hess[(KRYLOV, KRYLOV - 1)] = length

    work = [
        [combine([hess[(l, i)] * hess[(l, j)] for l in range(min(i, j) + 2)]) for j in range(KRYLOV)]
        for i in range(KRYLOV)
    ]
    vector = [beta * hess[(0, j)] for j in range(KRYLOV)]
    for p in range(KRYLOV):
        scale = 1.0 / work[p][p]
        top_work = [value * scale for value in work[p]]
        top = vector[p] * scale
        for i in range(KRYLOV):
            if i != p:
                factor = work[i][p]
                work[i] = [w - factor * t for w, t in zip(work[i], top_work)]
                vector[i] = vector[i] - factor * top
        work[p], vector[p] = top_work, top
    for h in range(halves_of(update_ref.shape[1])):
        update_ref[:, half(h)] = combine([c * ref[1, :, half(h)] for c, ref in zip(vector, states)])
        first_ref[:, half(h)] = beta * states[0][1, :, half(h)]


def shape(*dims, dtype=F32):
    return jax.ShapeDtypeStruct(dims, dtype)


def exchange(array, axes):
    return lax.all_to_all(array, axes, split_axis=0, concat_axis=0, tiled=True)


def local(stamps, stamp_target, pair_counts, conductance, block_cols, newton_residual):
    members = lax.axis_size("blk")
    devices = lax.axis_size("grp") * members
    rows = conductance.shape[1]

    send, to_next, own, pos, inner = pl.pallas_call(
        functools.partial(pack_kernel, members),
        out_shape=(
            shape(devices, 9, 2, LANES),
            shape(72, LANES),
            shape(72, LANES),
            shape(K - K // 2, rows, dtype=I32),
            shape(members * (K - K // 2) * rows // devices // LANES, 8, LANES, dtype=I32),
        ),
        in_specs=[pl.BlockSpec(memory_space=space) for space in (pl.ANY,) + 3 * (pltpu.VMEM,)],
        out_specs=tuple(pl.BlockSpec(memory_space=pltpu.VMEM) for _ in range(5)),
        scratch_shapes=[pltpu.VMEM(stamps.shape[1:], F32), pltpu.SemaphoreType.DMA],
        compiler_params=pltpu.CompilerParams(vmem_limit_bytes=60 * 2**20),
    )(stamps[0], stamp_target[0], pair_counts, block_cols)
    got = exchange(send, AXES)
    prev = lax.ppermute(to_next, AXES, [(i, (i + 1) % devices) for i in range(devices)])

    near, far = call(
        functools.partial(index_kernel, members),
        (shape(K, 8, rows, dtype=I32), shape(K - K // 2, 8, rows, dtype=I32)),
        block_cols,
        pos,
    )

    width = 2 * LANES * min(devices // 4 + 2, 10)
    jacobian, blocks, inverse, served, z = call(
        assemble_kernel,
        (
            shape(K, 8, 8, rows),
            shape(K, 8, 8, rows),
            shape(8, 8, rows),
            shape(devices, 8, LANES, dtype=I32),
            shape(members, 8, rows + LANES),
        ),
        near,
        got,
        prev,
        own,
        conductance,
        newton_residual,
        scratch=(pltpu.VMEM((64 * K, width), BF16), pltpu.VMEM((rows, width), BF16), pltpu.SemaphoreType.DMA),
        outside=1,
    )

    states, scalars = [], []
    vector = newton_residual
    for step in range(KRYLOV):
        rhs = step == 0
        z, group_dots = call(
            functools.partial(first_sweep_kernel, rhs),
            (shape(members, 8, rows), shape(2, 8, LANES)),
            exchange(z, "blk"),
            vector,
            blocks,
            inverse,
            near,
        )
        send, coupled = call(
            functools.partial(second_sweep_kernel, rhs),
            (shape(devices, 8, rows), shape(8, rows)),
            exchange(z, "blk"),
            vector,
            blocks,
            inverse,
            near,
            served,
            group_dots,
        )
        last = step + 1 == KRYLOV
        state, scalar, z, *rest = call(
            functools.partial(operate_kernel, step, members),
            [
                shape(3, 8, rows),
                shape(2 * step + 1, 8, LANES),
                shape(devices, 1, LANES) if last else shape(members, 8, rows + LANES),
            ]
            + ([] if last else [shape(8, rows)]),
            exchange(send, AXES),
            group_dots,
            coupled,
            vector,
            blocks,
            inverse,
            near,
            far,
            inner,
            *states,
            *scalars,
        )
        states.append(state)
        scalars.append(scalar)
        if not last:
            vector = rest[0]

    update, first = call(finish_kernel, (shape(8, rows), shape(8, rows)), exchange(z, AXES), *states, *scalars)
    return update, jacobian, first


def solution(mesh):
    placed = (
        P(AXES, None, None, None),
        P(AXES, None, None),
        P(AXES, None),
        P(None, AXES),
        P(None, AXES),
        P(None, AXES),
    )
    return jax.shard_map(
        local,
        mesh=mesh,
        in_specs=placed,
        out_specs=(P(None, AXES), P(None, None, None, AXES), P(None, AXES)),
        check_vma=False,
    )
```
